128 devices in a mesh: ctx: 8 (over x, core), vocab: 16 (over y, z).
Axes of the slice: x: 4, y: 4, z: 4, core: 2. Of those that a mesh axis runs over, the one named last changes fastest.
Arguments:
- hidden_state: bfloat16 [1024, 7168], P('ctx'), may hold values from -50 to 50
- embedded_next: bfloat16 [1024, 7168], P('ctx'), may hold values from -50 to 50
- gain_hidden: float32 [7168], replicated, may hold values from 0.1 to 1.9
- gain_embed: float32 [7168], replicated, may hold values from 0.1 to 1.9
- proj_hidden: bfloat16 [7168, 7168], P('ctx', 'vocab'), may hold values from -0.0625 to 0.0625
- proj_embed: bfloat16 [7168, 7168], P('ctx', 'vocab'), may hold values from -0.0625 to 0.0625
- final_gain: float32 [7168], P('vocab'), may hold values from 0.1 to 1.9
- head: bfloat16 [65536, 7168], P(('ctx', 'vocab')), may hold values from -0.875 to 0.875
- targets: int32 [1024], replicated, may hold values from 0 to 65535
- loss_mask: int32 [1024], replicated, may hold values 0 or 1
Outputs:
- mean_loss: float32 [], replicated
- grad_hidden: bfloat16 [1024, 7168], P('ctx', 'vocab')
- grad_embed: bfloat16 [1024, 7168], P('ctx', 'vocab')
- grad_gain_hidden: float32 [7168], P('vocab')
- grad_gain_embed: float32 [7168], P('vocab')
- grad_proj_hidden: bfloat16 [7168, 7168], P('ctx', 'vocab')
- grad_proj_embed: bfloat16 [7168, 7168], P('ctx', 'vocab')
- grad_final_gain: float32 [7168], P('vocab')
- grad_head: bfloat16 [65536, 7168], P(('ctx', 'vocab'))
The draws below stay inside these ranges and needn't reach their ends.
All inputs are finite; a program needn't handle non-finite values.
Results may differ from the reference program's by a relative error of at most 0.023.
Values may be sent and summed in bfloat16 or wider, within the bound.
A program may use at most 256 MiB of HBM per device.

```python
import math
import jax
import jax.numpy as jnp
from jax import lax

D = 7168
VOCAB = 65536
TOKENS = 1024


def spread_factors(key, row_total, col_total):
    row_key, col_key = jax.random.split(key)
    row_factor = jnp.exp(jax.random.uniform(row_key, (row_total, 1), jnp.float32) * math.log(10.0))
    col_factor = jnp.exp(jax.random.uniform(col_key, (1, col_total), jnp.float32) * math.log(10.0))
    return row_factor * col_factor


def draw_hidden_state(key, part):
    key = jax.random.fold_in(key, 11)
    base_key, scale_key = jax.random.split(key)
    base = jnp.clip(jax.random.normal(base_key, (TOKENS, D), jnp.float32), -5.0, 5.0)
    return (base * spread_factors(scale_key, TOKENS, D) * 0.1).astype(jnp.bfloat16)


def draw_embedded_next(key, part):
    key = jax.random.fold_in(key, 23)
    base_key, scale_key = jax.random.split(key)
    base = jnp.clip(jax.random.normal(base_key, (TOKENS, D), jnp.float32), -5.0, 5.0)
    return (base * spread_factors(scale_key, TOKENS, D) * 0.1).astype(jnp.bfloat16)


def set_ends(drawn, stream_key, least, largest):
    extent = drawn.shape
    place = [jax.random.randint(jax.random.fold_in(stream_key, axis), (), 0, extent[axis]) for axis in range(len(extent))]
    drawn = drawn.at[tuple(place)].set(least)
    longest = extent.index(max(extent))
    place[longest] = (place[longest] + 1) % extent[longest]
    return drawn.at[tuple(place)].set(largest)


def strengthened(array, own_key, source, target, parts, factor):
    owner, partner = [(jnp.arange(array.shape[position]) // (array.shape[position] // parts)).reshape([-1 if axis == position else 1 for axis in range(array.ndim)]) for position in (source, target)]
    chosen = jax.random.permutation(own_key, parts)[partner]
    strong = (owner == chosen) | (owner == (partner + parts // 2) % parts)
    return jnp.where(strong, factor * array, array)


def block_scale(key, shape, cuts, low, top_value):
    loudness = 1.0
    for axis_at, parts in cuts:
        steps = jax.random.uniform(jax.random.fold_in(jax.random.fold_in(key, 6), axis_at), (parts,), jnp.float32, low / len(cuts), top_value / len(cuts))
        loudness = loudness * jnp.repeat(jnp.exp(steps), shape[axis_at] // parts).reshape((-1,) + (1,) * (len(shape) - 1 - axis_at))
    return loudness


def bell_draw(stream_key, shape, spread, limit, cuts=(), held_as=jnp.bfloat16):
    entries = spread * jax.random.normal(stream_key, shape, jnp.float32)
    if cuts:
        entries = entries * block_scale(stream_key, shape, cuts, -0.22, 0.18)
    return jnp.clip(entries, -limit, limit).astype(held_as)


def noise_with(key, shape, deviation, limit, cuts, heavy, kind=jnp.bfloat16):
    array = deviation * jax.random.normal(key, shape, jnp.float32)
    if cuts:
        array = array * block_scale(key, shape, cuts, -0.22, 0.18)
    return jnp.clip(strengthened(array, jax.random.fold_in(key, 3), *heavy), -limit, limit).astype(kind)


def setup_inputs(seed: int = 0) -> dict:
    splits = jax.random.split(jax.random.key(seed), 11)
    return {
        "hidden_state": draw_hidden_state(jax.random.fold_in(splits[10], 71), 0),
        "embedded_next": draw_embedded_next(jax.random.fold_in(splits[10], 71), 0),
        "gain_hidden": jnp.clip(1.0 + 0.18 * jax.random.normal(splits[2], (D,), jnp.float32), 0.1, 1.9),
        "gain_embed": jnp.clip(1.0 + 0.18 * jax.random.normal(splits[3], (D,), jnp.float32), 0.1, 1.9),
        "proj_hidden": bell_draw(splits[4], (D, D), D ** -0.5, 0.0625, ((0, 8), (1, 16))),
        "proj_embed": bell_draw(splits[5], (D, D), D ** -0.5, 0.0625, ((0, 8), (1, 16))),
        "final_gain": jnp.clip(1.0 + 0.18 * jax.random.normal(splits[6], (D,), jnp.float32), 0.1, 1.9),
        "head": noise_with(splits[7], (VOCAB, D), (D // 9) ** -0.5, 0.875, ((0, 128),), (0, 1, 128, 5.5)),
        "targets": set_ends(jax.random.randint(splits[8], (TOKENS,), 0, VOCAB), jax.random.fold_in(splits[8], 1), 0, VOCAB - 1).astype(jnp.int32),
        "loss_mask": set_ends((jax.random.randint(splits[9], (TOKENS,), 0, 4) < 3).astype(jnp.int32), jax.random.fold_in(splits[9], 1), 0, 1),
    }


EPSILON = 1e-06

def scale_of(values):
    return lax.rsqrt(lax.optimization_barrier(jnp.mean(values * values, axis=-1, keepdims=True)) + EPSILON)

def reference(hidden_state, embedded_next, gain_hidden, gain_embed, proj_hidden, proj_embed, final_gain, head, targets, loss_mask):
    hidden_wide = hidden_state.astype(jnp.float32)
    embed_wide = embedded_next.astype(jnp.float32)
    hidden_scale = scale_of(hidden_wide)
    embed_scale = scale_of(embed_wide)
    normed_hidden = (hidden_wide * hidden_scale * gain_hidden).astype(jnp.bfloat16)
    normed_embed = (embed_wide * embed_scale * gain_embed).astype(jnp.bfloat16)
    projected = jnp.dot(normed_hidden, proj_hidden, preferred_element_type=jnp.float32) + jnp.dot(normed_embed, proj_embed, preferred_element_type=jnp.float32)
    row_scale = scale_of(projected)
    normed_rows = (projected * row_scale * final_gain).astype(jnp.bfloat16)
    logits = jnp.dot(normed_rows, head.T, preferred_element_type=jnp.float32)
    log_total = jnp.log(lax.optimization_barrier(jnp.sum(jnp.exp(logits), axis=-1)))
    is_target = targets[:, None] == jnp.arange(VOCAB, dtype=jnp.int32)[None, :]
    target_logit = lax.optimization_barrier(jnp.sum(jnp.where(is_target, logits, jnp.float32(0.0)), axis=-1))
    mask_weight = loss_mask.astype(jnp.float32)
    mean_loss = jnp.sum(mask_weight * (log_total - target_logit)) / TOKENS
    probs = jnp.exp(logits - log_total[:, None])
    logit_grad = (mask_weight[:, None] * (probs - is_target.astype(jnp.float32))).astype(jnp.bfloat16)
    block_size = math.gcd(VOCAB, 4096)
    block_count = VOCAB // block_size
    grad_blocks = logit_grad.reshape(TOKENS, block_count, block_size).transpose(1, 0, 2)
    head_blocks = head.reshape(block_count, block_size, D)

    def head_block(carry, pieces):
        grad_piece, weight_piece = pieces
        carry = carry + jnp.dot(grad_piece, weight_piece, preferred_element_type=jnp.float32)
        return (carry, jnp.dot(grad_piece.T, normed_rows, preferred_element_type=jnp.float32).astype(jnp.bfloat16))
    normed_grad, head_parts = lax.scan(head_block, jnp.zeros((TOKENS, D), jnp.float32), (grad_blocks, head_blocks))
    grad_head = head_parts.reshape(VOCAB, D)
    grad_final_gain = lax.optimization_barrier(jnp.sum(normed_grad * projected * row_scale, axis=0))
    scaled_grad = normed_grad * final_gain
    row_dot = lax.optimization_barrier(jnp.sum(scaled_grad * projected, axis=-1, keepdims=True))
    proj_grad = (row_scale * scaled_grad - projected * (row_scale * row_scale * row_scale) * (row_dot / D)).astype(jnp.bfloat16)
    grad_proj_hidden = jnp.dot(normed_hidden.T, proj_grad, preferred_element_type=jnp.float32).astype(jnp.bfloat16)
    grad_proj_embed = jnp.dot(normed_embed.T, proj_grad, preferred_element_type=jnp.float32).astype(jnp.bfloat16)
    hidden_back = jnp.dot(proj_grad, proj_hidden.T, preferred_element_type=jnp.float32)
    embed_back = jnp.dot(proj_grad, proj_embed.T, preferred_element_type=jnp.float32)
    grad_gain_hidden = lax.optimization_barrier(jnp.sum(hidden_back * hidden_wide * hidden_scale, axis=0))
    grad_gain_embed = lax.optimization_barrier(jnp.sum(embed_back * embed_wide * embed_scale, axis=0))
    hidden_dot = lax.optimization_barrier(jnp.sum(hidden_back * gain_hidden * hidden_wide, axis=-1, keepdims=True))
    embed_dot = lax.optimization_barrier(jnp.sum(embed_back * gain_embed * embed_wide, axis=-1, keepdims=True))
    grad_hidden = (hidden_scale * (hidden_back * gain_hidden) - hidden_wide * (hidden_scale * hidden_scale * hidden_scale) * (hidden_dot / D)).astype(jnp.bfloat16)
    grad_embed = (embed_scale * (embed_back * gain_embed) - embed_wide * (embed_scale * embed_scale * embed_scale) * (embed_dot / D)).astype(jnp.bfloat16)
    return (mean_loss, grad_hidden, grad_embed, grad_gain_hidden, grad_gain_embed, grad_proj_hidden, grad_proj_embed, grad_final_gain, grad_head)
```

```python
import functools

import jax
import jax.numpy as jnp
from jax import lax
from jax.experimental import pallas as pl
from jax.experimental.pallas import tpu as pltpu
from jax.sharding import PartitionSpec as P

EPSILON = 1e-06
MESH = pl.DeviceIdType.MESH
VMEM = pl.BlockSpec(memory_space=pltpu.VMEM)
ANY = pl.BlockSpec(memory_space=pl.ANY)
F32 = jnp.float32
BF16 = jnp.bfloat16
PARTS = ((0, 640, "xyz"), (640, 640, "yzx"), (1280, 512, "zxy"))


class Place:
    def __init__(self):
        self.ctx = lax.axis_index("ctx")
        self.v = lax.axis_index("vocab")
        self.c = {"x": self.ctx // 2, "y": self.v // 4, "z": self.v % 4}
        self.core = self.ctx % 2

    def at(self, ctx=None, v=None):
        return {"ctx": self.ctx if ctx is None else ctx, "vocab": self.v if v is None else v}

    def along(self, axis, step):
        i = lax.rem(self.c[axis] + step + 4, 4)
        if axis == "x":
            return self.at(ctx=i * 2 + self.core)
        if axis == "y":
            return self.at(v=i * 4 + self.c["z"])
        return self.at(v=self.c["y"] * 4 + i)

    def sibling(self):
        return self.at(ctx=self.c["x"] * 2 + 1 - self.core)

    def ctx_peer(self, o):
        return self.at(ctx=lax.rem(self.ctx + o, 8))

    def v_peer(self, o):
        return self.at(v=lax.rem(self.v + o, 16))


class Copies:
    def __init__(self, send, recv):
        self.send, self.recv, self.count, self.started = send, recv, 0, []

    def go(self, src, dst, device):
        copy = pltpu.make_async_remote_copy(
            src_ref=src,
            dst_ref=dst,
            send_sem=self.send.at[self.count],
            recv_sem=self.recv.at[self.count],
            device_id=device,
            device_id_type=MESH,
        )
        self.count += 1
        copy.start()
        self.started.append(copy)
        return copy

    def finish(self):
        for copy in self.started:
            copy.wait_send()
        self.started = []


def greet(devices):
    barrier = pltpu.get_barrier_semaphore()
    for device in devices:
        pl.semaphore_signal(barrier, inc=1, device_id=device, device_id_type=MESH)
    pl.semaphore_wait(barrier, len(devices))


def run(*rings):
    rings = list(rings)
    while rings:
        left = []
        for ring in rings:
            try:
                next(ring)
                left.append(ring)
            except StopIteration:
                pass
        rings = left


def chain(*makers):
    for maker in makers:
        yield from maker()


def gather_ring(copies, here, axis, slab):
    me = here.c[axis]
    right, left = here.along(axis, 1), here.along(axis, -1)
    before, after = lax.rem(me + 3, 4), lax.rem(me + 1, 4)
    from_left = copies.go(slab(me, None), slab(me, None), right)
    from_right = copies.go(slab(me, None), slab(me, None), left)
    yield
    from_left.wait_recv()
    far_a = copies.go(slab(before, 0), slab(before, 0), right)
    from_right.wait_recv()
    far_b = copies.go(slab(after, 1), slab(after, 1), left)
    yield
    far_a.wait_recv()
    far_b.wait_recv()


def reduce_ring(copies, here, axis, slab, half, one, two, held, add):
    me = here.c[axis]
    right, left = here.along(axis, 1), here.along(axis, -1)
    before, after, far = lax.rem(me + 3, 4), lax.rem(me + 1, 4), lax.rem(me + 2, 4)
    a1 = copies.go(slab(far, 0), one.at[0], right)
    b1 = copies.go(slab(far, 1), one.at[1], left)
    a2 = copies.go(slab(after, 1), half(two.at[0], 1), right)
    b2 = copies.go(slab(before, 0), half(two.at[1], 0), left)
    yield
    a1.wait_recv()
    add(held.at[0], (slab(after, 0), one.at[0]))
    a3 = copies.go(held.at[0], half(two.at[0], 0), right)
    b1.wait_recv()
    add(held.at[1], (slab(before, 1), one.at[1]))
    b3 = copies.go(held.at[1], half(two.at[1], 1), left)
    yield
    a2.wait_recv()
    b2.wait_recv()
    a3.wait_recv()
    b3.wait_recv()


def add_refs(out, terms):
    lead = out.shape[:-2]
    total = 1
    for n in lead:
        total *= n

    def block(index):
        acc = terms[0][index].astype(F32)
        for term in terms[1:]:
            acc = acc + term[index].astype(F32)
        out[index] = acc.astype(out.dtype)

    if total == 1:
        block(tuple(0 for _ in lead) + (slice(None), slice(None)))
        return

    @pl.loop(0, total)
    def _(i):
        index = []
        for n in reversed(lead):
            index.append(i % n)
            i = i // n
        block(tuple(reversed(index)) + (slice(None), slice(None)))


def columns_kernel(rows, head, cols, head_sib, send, recv, local_sem):
    here = Place()
    copies = Copies(send, recv)
    greet(
        [here.ctx_peer(o) for o in range(1, 8)]
        + [here.along("y", 1), here.along("y", -1), here.along("z", 1), here.along("z", -1)]
    )
    y, z = here.c["y"], here.c["z"]

    def block(c):
        return cols.at[y // 2, c, y % 2, z]

    arrivals = []
    for o in range(1, 8):
        peer = lax.rem(here.ctx + o, 8)
        arrivals.append(copies.go(rows.at[peer], block(here.ctx), here.ctx_peer(o)))
    own = pltpu.make_async_copy(rows.at[here.ctx], block(here.ctx), local_sem)
    own.start()
    swap = copies.go(head, head_sib, here.sibling())
    own.wait()
    for arrival in arrivals:
        arrival.wait_recv()

    def span(h):
        return slice(None) if h is None else pl.ds(h * 4, 4)

    def y_first(i, h):
        return cols.at[i // 2, span(h), i % 2, z]

    def z_last(i, h):
        return cols.at[:, span(h), :, i]

    def z_first(i, h):
        return cols.at[y // 2, span(h), y % 2, i]

    def y_last(i, h):
        return cols.at[i // 2, span(h), i % 2]

    def both(first, second):
        run(
            chain(
                lambda: gather_ring(copies, here, *first), lambda: gather_ring(copies, here, *second)
            )
        )

    mark, kept = copies.count, copies.started
    copies.started = []

    @pl.when(here.core == 0)
    def _():
        both(("y", y_first), ("z", z_last))
        copies.finish()

    copies.count = mark

    @pl.when(here.core == 1)
    def _():
        both(("z", z_first), ("y", y_last))
        copies.finish()

    copies.started = kept
    swap.wait_recv()
    copies.finish()


def rows_kernel(
    partial, gain, projected, scales, rows,
    sib, summed, one, two, held, squares, mine_sq, piece, pieces, block, send, recv, local_sem,
):
    here = Place()
    copies = Copies(send, recv)
    rings = [here.along(a, s) for a in "xyz" for s in (1, -1)]
    greet(
        rings
        + [here.sibling()]
        + [here.v_peer(o) for o in range(1, 16)]
        + [here.along(a, 2) for a in "x"]
    )
    width = 7168
    x, y, z = here.c["x"], here.c["y"], here.c["z"]
    swap = copies.go(partial.at[:, 1 - here.core], sib, here.sibling())
    swap.wait_recv()
    for i in range(4):
        summed[i] = partial[i, here.core] + sib[i]

    def half(ref, h):
        return ref.at[pl.ds(h * 64, 64)]

    run(
        reduce_ring(
            copies, here, "x",
            lambda i, h: half(summed.at[i], h), half, one, two, held,
            lambda out, terms: out.__setitem__(..., terms[0][...] + terms[1][...]),
        )
    )
    total = summed[x] + two[0] + two[1]
    projected[...] = total
    mine_sq[...] = lax.dot_general(
        jnp.ones((8, total.shape[1]), F32), total * total, (((1,), (1,)), ((), ())),
        precision=lax.Precision.HIGHEST, preferred_element_type=F32,
    )
    piece[...] = (total * gain[...]).astype(BF16).reshape(piece.shape)
    exchange = []
    for o in range(1, 4):
        to = lax.rem(z + o, 4)
        exchange.append(copies.go(piece.at[to], pieces.at[z], here.along("z", o)))
    sq_in = []
    for o in range(1, 16):
        sq_in.append(copies.go(mine_sq, squares.at[here.v], here.v_peer(o)))
    squares[here.v] = mine_sq[...]
    pieces[z] = piece[z]
    for copy in exchange:
        copy.wait_recv()
    for i in range(4):
        block[:, i * 448 : (i + 1) * 448] = pieces[i]
    own = pltpu.make_async_copy(block, rows.at[y, x, z], local_sem)
    own.start()
    own.wait()

    def stage(part, k):
        off, w, order = part

        def slab(i, h):
            index = []
            for a in "yxz":
                at = order.index(a)
                index.append(i if at == k else slice(None) if at < k else here.c[a])
            lines = slice(None) if h is None else pl.ds(h * 16, 16)
            return rows.at[(*index, lines, pl.ds(off, w))]

        return lambda: gather_ring(copies, here, order[k], slab)

    def scale():
        yield
        for copy in sq_in:
            copy.wait_recv()
        scales[x] = lax.rsqrt(jnp.sum(squares[...], axis=0) / width + EPSILON)
        out = [copies.go(scales.at[x], scales.at[x], here.along("x", o)) for o in range(1, 4)]
        yield
        yield
        for copy in out:
            copy.wait_recv()

    run(*[chain(*[stage(part, k) for k in range(3)]) for part in PARTS], scale())
    copies.finish()


def totals_kernel(tile, out, group, line, part, send, recv):
    here = Place()
    copies = Copies(send, recv)
    greet(
        [here.v_peer(o) for o in range(1, 16)]
        + [here.along("x", o) for o in (1, 2, 3)]
        + [here.sibling()]
    )
    group[here.v] = tile[...]
    ins = [copies.go(tile, group.at[here.v], here.v_peer(o)) for o in range(1, 16)]
    for copy in ins:
        copy.wait_recv()
    x = here.c["x"]
    line[x] = jnp.sum(group[...], axis=0)
    ins = [copies.go(line.at[x], line.at[x], here.along("x", o)) for o in (1, 2, 3)]
    for copy in ins:
        copy.wait_recv()
    out[here.core] = jnp.sum(line[...], axis=0)
    copies.go(out.at[here.core], out.at[here.core], here.sibling()).wait_recv()
    copies.finish()


def drop(shape, axes, axis):
    return tuple(n for n, a in zip(shape, axes) if a != axis)


def grad_kernel(
    terms, projected, gain, scale, rows, lgr,
    proj_grad, gain_grad, rows_sib, lgr_sib, *scratch,
):
    rings_scratch, (whole, piece, pieces, dots, mine_dot, gains, mine_gain, send, recv) = (
        scratch[:-9],
        scratch[-9:],
    )
    here = Place()
    copies = Copies(send, recv)
    greet(
        [here.along(a, s) for a in "xyz" for s in (1, -1)]
        + [here.along("z", 2)]
        + [here.v_peer(o) for o in range(1, 16)]
        + [here.ctx_peer(o) for o in range(1, 8)]
    )
    width = 7168
    z = here.c["z"]
    swaps = [
        copies.go(lgr.at[1], lgr_sib, here.sibling()),
        copies.go(rows, rows_sib, here.sibling()),
    ]

    def half(ref, h):
        index = (slice(None),) * (len(ref.shape) - 2) + (pl.ds(h * 16, 16),)
        return ref.at[index]

    def part_rings(n, part):
        off, w, order = part
        order = order[::-1]
        axes = "yxz"
        source = terms
        cols = pl.ds(off, w)
        for k in range(3):
            one, two, held, out = rings_scratch[(n * 3 + k) * 4 : (n * 3 + k) * 4 + 4]
            axis = order[k]

            def slab(i, h, source=source, axes=axes, cols=cols, axis=axis):
                index = tuple(i if a == axis else slice(None) for a in axes)
                lines = slice(None) if h is None else pl.ds(h * 16, 16)
                return source.at[(*index, lines, cols)]

            yield from reduce_ring(
                copies, here, axis, slab, half, one, two, held, add_refs
            )
            if k < 2:
                add_refs(out, (slab(here.c[axis], None), two.at[0], two.at[1]))
            else:
                own = slab(here.c[axis], None)[...].astype(F32)
                whole[:, off : off + w] = own + two[0].astype(F32) + two[1].astype(F32)
            source, cols = out, slice(None)
            axes = axes.replace(axis, "")
            yield

    run(*[part_rings(n, part) for n, part in enumerate(PARTS)])
    for i in range(4):
        piece[i] = whole[:, i * 448 : (i + 1) * 448]
    exchange = []
    for o in range(1, 4):
        to = lax.rem(z + o, 4)
        exchange.append(copies.go(piece.at[to], pieces.at[z], here.along("z", o)))
    pieces[z] = piece[z]
    for copy in exchange:
        copy.wait_recv()
    normed_grad = pieces[...].reshape(128, 448)
    wide = projected[...]
    row_scale = scale[...]
    scaled = normed_grad * gain[...]
    mine_dot[...] = lax.dot_general(
        jnp.ones((8, 448), F32), scaled * wide, (((1,), (1,)), ((), ())),
        precision=lax.Precision.HIGHEST, preferred_element_type=F32,
    )
    ins = [copies.go(mine_dot, dots.at[here.v], here.v_peer(o)) for o in range(1, 16)]
    dots[here.v] = mine_dot[...]
    mine_gain[...] = jnp.broadcast_to(
        jnp.sum(normed_grad * wide * row_scale, axis=0, keepdims=True), (8, 448)
    )
    gain_ins = [copies.go(mine_gain, gains.at[here.ctx], here.ctx_peer(o)) for o in range(1, 8)]
    gains[here.ctx] = mine_gain[...]
    for copy in ins:
        copy.wait_recv()
    row_dot = jnp.sum(dots[...], axis=0).T[:, :1]
    grad = row_scale * scaled - wide * (row_scale * row_scale * row_scale) * (row_dot / width)
    x, core = here.c["x"], here.core
    proj_grad[x, core] = grad.astype(BF16)

    def slab(i, h):
        lines = slice(None) if h is None else pl.ds(h * 64, 64)
        return proj_grad.at[i, core, lines]

    run(gather_ring(copies, here, "x", slab))
    copies.go(proj_grad.at[:, core], proj_grad.at[:, core], here.sibling()).wait_recv()
    for copy in gain_ins:
        copy.wait_recv()
    gain_grad[...] = jnp.sum(gains[...], axis=0)[:1]
    for copy in swaps:
        copy.wait_recv()
    copies.finish()


def back_kernel(
    terms, inputs, gains, scales, grads, gain_grads,
    one_a, two_a, held_a, out_a, one_b, two_b, held_b, out_b,
    one_c, two_c, held_c, one_d, two_d, held_d,
    summed, sent, got, mine_dot, dots, mine_gain, gain_all, send, recv, send_far, recv_far,
):
    here = Place()
    copies = Copies(send, recv)
    y, z, v, ctx = here.c["y"], here.c["z"], here.v, here.ctx
    width = 7168
    barrier = pltpu.get_barrier_semaphore()
    near = (
        [here.along(a, s) for a in "yz" for s in (1, -1)]
        + [here.v_peer(o) for o in range(1, 16)]
        + [here.ctx_peer(o) for o in range(1, 8)]
    )
    for device in near:
        pl.semaphore_signal(barrier, inc=1, device_id=device, device_id_type=MESH)
    for source in range(16):
        pl.semaphore_signal(
            barrier, inc=1, device_id=here.at(ctx=v // 2, v=source), device_id_type=MESH
        )
    pl.semaphore_wait(barrier, len(near) + 16)

    def span(h):
        return slice(None) if h is None else pl.ds(h * 4, 4)

    def back_y(i, h):
        return terms.at[i // 2, span(h), i % 2]

    def back_z(i, h):
        return terms.at[:, span(h), :, i]

    @pl.when(here.core == 0)
    def _():
        run(
            reduce_ring(
                copies, here, "y", back_y, lambda ref, h: ref.at[span(h)],
                one_a, two_a, held_a, add_refs,
            )
        )
        add_refs(out_a, (back_y(y, None), two_a.at[0], two_a.at[1]))
        run(
            reduce_ring(
                copies, here, "z", lambda i, h: out_a.at[span(h), i],
                lambda ref, h: ref.at[span(h)], one_c, two_c, held_c, add_refs,
            )
        )
        add_refs(summed, (out_a.at[:, z], two_c.at[0], two_c.at[1]))
        copies.finish()

    copies.count = 0

    @pl.when(here.core == 1)
    def _():
        run(
            reduce_ring(
                copies, here, "z", back_z, lambda ref, h: ref.at[:, span(h)],
                one_b, two_b, held_b, add_refs,
            )
        )
        add_refs(out_b, (back_z(z, None), two_b.at[0], two_b.at[1]))
        run(
            reduce_ring(
                copies, here, "y", lambda i, h: out_b.at[i // 2, span(h), i % 2],
                lambda ref, h: ref.at[span(h)], one_d, two_d, held_d, add_refs,
            )
        )
        add_refs(summed, (out_b.at[y // 2, :, y % 2], two_d.at[0], two_d.at[1]))
        copies.finish()

    @pl.loop(0, 8)
    def _(c):
        sent[0, c] = summed[c][:, :448].astype(BF16)
        sent[1, c] = summed[c][:, 448:].astype(BF16)

    def far_copy(o, s):
        to = lax.rem(ctx + o, 8)
        return pltpu.make_async_remote_copy(
            src_ref=sent.at[s, to],
            dst_ref=got.at[v // 8, pl.ds(lax.rem(v, 8) * 16, 16)],
            send_sem=send_far.at[o * 2 + s],
            recv_sem=recv_far.at[v],
            device_id=here.at(ctx=to, v=ctx * 2 + s),
            device_id_type=MESH,
        )

    for o in range(8):
        for s in range(2):
            if o:
                far_copy(o, s).start()
            else:

                @pl.when(v != ctx * 2 + s)
                def _(s=s):
                    far_copy(0, s).start()

                @pl.when(v == ctx * 2 + s)
                def _(s=s):
                    got[v // 8, pl.ds(lax.rem(v, 8) * 16, 16)] = sent[s, ctx]

    for source in range(16):

        @pl.when(jnp.logical_or(ctx != v // 2, v != source))
        def _(source=source):
            pltpu.make_async_remote_copy(
                src_ref=sent.at[0, 0],
                dst_ref=got.at[source // 8, pl.ds(source % 8 * 16, 16)],
                send_sem=send_far.at[0],
                recv_sem=recv_far.at[source],
                device_id=here.at(ctx=lax.rem(ctx + 1, 8)),
                device_id_type=MESH,
            ).wait_recv()

    for e in range(2):
        back = got[e].astype(F32)
        wide = inputs[e].astype(F32)
        mine_dot[e] = lax.dot_general(
            jnp.ones((8, 448), F32), back * gains[e] * wide, (((1,), (1,)), ((), ())),
            precision=lax.Precision.HIGHEST, preferred_element_type=F32,
        )
        mine_gain[e] = jnp.broadcast_to(
            jnp.sum(back * wide * scales[e], axis=0, keepdims=True), (8, 448)
        )
    ins = [copies.go(mine_dot, dots.at[v], here.v_peer(o)) for o in range(1, 16)]
    gain_ins = [copies.go(mine_gain, gain_all.at[ctx], here.ctx_peer(o)) for o in range(1, 8)]
    dots[v] = mine_dot[...]
    gain_all[ctx] = mine_gain[...]
    for copy in ins:
        copy.wait_recv()
    for e in range(2):
        back = got[e].astype(F32)
        wide = inputs[e].astype(F32)
        dot = jnp.sum(dots[:, e], axis=0).T[:, :1]
        scale = scales[e]
        grads[e] = (
            scale * (back * gains[e]) - wide * (scale * scale * scale) * (dot / width)
        ).astype(BF16)
    for copy in gain_ins:
        copy.wait_recv()
    gain_grads[...] = jnp.sum(gain_all[...], axis=0)
    for o in range(8):
        for s in range(2):
            if o:
                far_copy(o, s).wait_send()
            else:

                @pl.when(v != ctx * 2 + s)
                def _(s=s):
                    far_copy(0, s).wait_send()

    copies.finish()


def logits_kernel(rows, own, sib, out):
    @pl.when(pl.program_id(0) == 0)
    def _():
        out[...] = jnp.zeros_like(out)

    for h, head in enumerate((own, sib)):
        out[:, h * 512 : (h + 1) * 512] += lax.dot_general(
            rows[0], head[...], (((1,), (1,)), ((), ())), preferred_element_type=F32
        )


def normed_kernel(grad, own, sib, out):
    out[0] = (
        jnp.dot(grad[:, :512], own[...], preferred_element_type=F32)
        + jnp.dot(grad[:, 512:], sib[...], preferred_element_type=F32)
    ).astype(BF16)


def head_kernel(own_grad, sib_grad, own, sib, out):
    out[...] = (
        jnp.dot(own_grad[...], own[0], preferred_element_type=F32)
        + jnp.dot(sib_grad[...], sib[0], preferred_element_type=F32)
    ).astype(BF16)


def params(number, limit=56):
    return pltpu.CompilerParams(
        collective_id=number, has_side_effects=True, vmem_limit_bytes=limit * 2**20
    )


def plain():
    return pltpu.CompilerParams(vmem_limit_bytes=56 * 2**20)


def sems(n):
    return [pltpu.SemaphoreType.DMA((n,)), pltpu.SemaphoreType.DMA((n,))]


def shape(dims, kind):
    return jax.ShapeDtypeStruct(dims, kind)


def reduce_scratch():
    scratch = []
    for _, w, order in PARTS:
        dims = (4, 4)
        for k in range(3):
            scratch += [
                pltpu.VMEM((2, *dims, 16, w), BF16),
                pltpu.VMEM((2, *dims, 32, w), BF16),
                pltpu.VMEM((2, *dims, 16, w), BF16),
                pltpu.VMEM((*dims, 32, w), BF16),
            ]
            dims = dims[1:]
    return scratch


def scale_of(values):
    return lax.rsqrt(jnp.mean(values * values, axis=-1, keepdims=True) + EPSILON)


def contract_first(left, right):
    return lax.dot_general(
        left, right, (((0,), (0,)), ((), ())), preferred_element_type=F32
    )


def contract_last(left, right):
    return lax.dot_general(
        left, right, (((1,), (1,)), ((), ())), preferred_element_type=F32
    )


def local(
    hidden_state, embedded_next, gain_hidden, gain_embed, proj_hidden, proj_embed,
    final_gain, head, targets, loss_mask,
):
    width = hidden_state.shape[1]
    token_total = targets.shape[0]
    ctx, v = lax.axis_index("ctx"), lax.axis_index("vocab")
    x, core = ctx // 2, ctx % 2
    sliver = (v % 8) * 16
    first = v < 8
    raw = jnp.where(
        first,
        lax.dynamic_slice_in_dim(hidden_state, sliver, 16, 0),
        lax.dynamic_slice_in_dim(embedded_next, sliver, 16, 0),
    ).astype(F32)
    gain_in = jnp.where(first, gain_hidden, gain_embed)
    normed = (raw * scale_of(raw) * gain_in).astype(BF16)
    normed = normed.reshape(16, 8, 896).transpose(1, 0, 2)

    cols, head_sib = pl.pallas_call(
        columns_kernel,
        out_shape=[shape((2, 8, 2, 4, 16, 896), BF16), shape(head.shape, BF16)],
        in_specs=[VMEM, ANY],
        out_specs=[ANY, ANY],
        scratch_shapes=sems(16) + [pltpu.SemaphoreType.DMA],
        compiler_params=params(1),
        name="columns",
    )(normed, head)
    hidden_cols = cols[0].reshape(1024, 896)
    embed_cols = cols[1].reshape(1024, 896)
    partial = jnp.dot(hidden_cols, proj_hidden, preferred_element_type=F32) + jnp.dot(
        embed_cols, proj_embed, preferred_element_type=F32
    )

    projected, scales, rows = pl.pallas_call(
        rows_kernel,
        out_shape=[
            shape((128, 448), F32), shape((4, 8, 128), F32), shape((4, 4, 4, 32, 1792), BF16),
        ],
        in_specs=[VMEM, VMEM],
        out_specs=[VMEM, VMEM, ANY],
        scratch_shapes=[
            pltpu.VMEM((4, 128, 448), F32),
            pltpu.VMEM((4, 128, 448), F32),
            pltpu.VMEM((2, 64, 448), F32),
            pltpu.VMEM((2, 128, 448), F32),
            pltpu.VMEM((2, 64, 448), F32),
            pltpu.VMEM((16, 8, 128), F32),
            pltpu.VMEM((8, 128), F32),
            pltpu.VMEM((4, 32, 448), BF16),
            pltpu.VMEM((4, 32, 448), BF16),
            pltpu.VMEM((32, 1792), BF16),
        ]
        + sems(72)
        + [pltpu.SemaphoreType.DMA],
        compiler_params=params(2),
        name="rows",
    )(partial.reshape(4, 2, 128, 448), final_gain[None, :])

    gathered = rows.reshape(4, 512, 1792)
    row_scale = scales[:, 0].reshape(512, 1)
    block = pl.BlockSpec((1, 512, 1792), lambda i: (i, 0, 0))
    head_block = pl.BlockSpec((512, 1792), lambda i: (0, i))
    fixed = pl.BlockSpec((512, 1024), lambda i: (0, 0))
    raw_logits = pl.pallas_call(
        logits_kernel,
        grid=(4,),
        out_shape=shape((512, 1024), F32),
        in_specs=[block, head_block, head_block],
        out_specs=fixed,
        compiler_params=plain(),
        name="logits",
    )(gathered, head, head_sib)
    logits = raw_logits * row_scale
    own_ids = (ctx * 16 + v) * 512 + lax.iota(jnp.int32, 512)
    sib_ids = ((ctx + 1 - 2 * core) * 16 + v) * 512 + lax.iota(jnp.int32, 512)
    vocab_ids = jnp.concatenate([own_ids, sib_ids])

    def of_core(values, k):
        return lax.dynamic_index_in_dim(values.reshape(4, 2, 128), k, 1, keepdims=False)

    my_targets = of_core(targets, core).reshape(512)
    mask = of_core(loss_mask, core).reshape(512).astype(F32)
    is_target = my_targets[:, None] == vocab_ids[None, :]
    exp_part = jnp.sum(jnp.exp(logits), axis=-1)
    target_part = jnp.sum(jnp.where(is_target, logits, F32(0.0)), axis=-1)
    tile = jnp.concatenate([exp_part.reshape(4, 128), target_part.reshape(4, 128)])

    totals = pl.pallas_call(
        totals_kernel,
        out_shape=shape((2, 8, 128), F32),
        in_specs=[VMEM],
        out_specs=VMEM,
        scratch_shapes=[
            pltpu.VMEM((16, 8, 128), F32), pltpu.VMEM((4, 8, 128), F32), pltpu.VMEM((8, 128), F32),
        ]
        + sems(24),
        compiler_params=params(3),
        name="totals",
    )(tile)
    log_all = jnp.log(totals[:, :4])
    mask_all = loss_mask.reshape(4, 2, 128).transpose(1, 0, 2).astype(F32)
    mean_loss = jnp.sum(mask_all * (log_all - totals[:, 4:])) / token_total
    log_total = lax.dynamic_index_in_dim(log_all, core, 0, keepdims=False).reshape(512)
    wide_grad = mask[:, None] * (jnp.exp(logits - log_total[:, None]) - is_target.astype(F32))
    logit_grad = wide_grad.astype(BF16)
    scaled_grad = (wide_grad * row_scale).astype(BF16)
    scaled_grad = scaled_grad.reshape(512, 2, 512).transpose(1, 2, 0)

    normed_part = pl.pallas_call(
        normed_kernel,
        grid=(4,),
        out_shape=shape((4, 512, 1792), BF16),
        in_specs=[fixed, head_block, head_block],
        out_specs=block,
        compiler_params=plain(),
        name="normed",
    )(logit_grad, head, head_sib)

    own_scale = lax.dynamic_index_in_dim(scales, x, 0, keepdims=False)[0][:, None]
    proj_grad, gain_grad, rows_sib, grad_sib = pl.pallas_call(
        grad_kernel,
        out_shape=[
            shape((4, 2, 128, 448), BF16), shape((1, 448), F32),
            shape((4, 4, 4, 32, 1792), BF16), shape((512, 512), BF16),
        ],
        in_specs=[VMEM, VMEM, VMEM, VMEM, ANY, ANY],
        out_specs=[VMEM, VMEM, ANY, ANY],
        scratch_shapes=reduce_scratch()
        + [
            pltpu.VMEM((32, 1792), F32),
            pltpu.VMEM((4, 32, 448), F32),
            pltpu.VMEM((4, 32, 448), F32),
            pltpu.VMEM((16, 8, 128), F32),
            pltpu.VMEM((8, 128), F32),
            pltpu.VMEM((8, 8, 448), F32),
            pltpu.VMEM((8, 448), F32),
        ]
        + sems(96),
        compiler_params=params(4),
        name="grad",
    )(
        normed_part.reshape(4, 4, 4, 32, 1792), projected, final_gain[None, :], own_scale,
        rows, scaled_grad,
    )
    proj_grad = proj_grad.reshape(1024, 448)

    grad_head = pl.pallas_call(
        head_kernel,
        grid=(4,),
        out_shape=shape(head.shape, BF16),
        in_specs=[
            pl.BlockSpec((512, 512), lambda i: (0, 0)), pl.BlockSpec((512, 512), lambda i: (0, 0)),
            block, block,
        ],
        out_specs=head_block,
        compiler_params=plain(),
        name="head_grad",
    )(scaled_grad[0], grad_sib, gathered, rows_sib.reshape(4, 512, 1792))

    grad_proj_hidden = contract_first(hidden_cols, proj_grad).astype(BF16)
    grad_proj_embed = contract_first(embed_cols, proj_grad).astype(BF16)
    back = jnp.stack(
        [
            contract_last(proj_grad, proj_hidden).astype(BF16),
            contract_last(proj_grad, proj_embed).astype(BF16),
        ]
    )
    start = v * 448
    inputs = jnp.stack(
        [
            lax.dynamic_slice_in_dim(hidden_state, start, 448, 1),
            lax.dynamic_slice_in_dim(embedded_next, start, 448, 1),
        ]
    )
    gains = jnp.stack(
        [
            lax.dynamic_slice_in_dim(gain_hidden, start, 448, 0),
            lax.dynamic_slice_in_dim(gain_embed, start, 448, 0),
        ]
    )[:, None, :]
    in_scales = jnp.stack(
        [scale_of(hidden_state.astype(F32)), scale_of(embedded_next.astype(F32))]
    )

    def ring_scratch(halves, wholes, out=None):
        return [
            pltpu.VMEM((2, *halves), BF16), pltpu.VMEM((2, *wholes), BF16),
            pltpu.VMEM((2, *halves), BF16),
        ] + ([pltpu.VMEM(wholes, BF16)] if out else [])

    grads, gain_grads = pl.pallas_call(
        back_kernel,
        out_shape=[shape((2, 128, 448), BF16), shape((2, 8, 448), F32)],
        in_specs=[VMEM] * 4,
        out_specs=[VMEM] * 2,
        scratch_shapes=ring_scratch((4, 4, 16, 896), (8, 4, 16, 896), True)
        + ring_scratch((2, 4, 2, 16, 896), (2, 8, 2, 16, 896), True)
        + ring_scratch((4, 16, 896), (8, 16, 896))
        + ring_scratch((4, 16, 896), (8, 16, 896))
        + [
            pltpu.VMEM((8, 16, 896), F32),
            pltpu.VMEM((2, 8, 16, 448), BF16),
            pltpu.VMEM((2, 128, 448), BF16),
            pltpu.VMEM((2, 8, 128), F32),
            pltpu.VMEM((16, 2, 8, 128), F32),
            pltpu.VMEM((2, 8, 448), F32),
            pltpu.VMEM((8, 2, 8, 448), F32),
        ]
        + sems(48)
        + sems(16),
        compiler_params=params(5),
        name="back",
    )(back.reshape(2, 8, 2, 4, 16, 896), inputs, gains, in_scales)

    return (
        mean_loss, grads[0], grads[1], gain_grads[0, 0], gain_grads[1, 0],
        grad_proj_hidden, grad_proj_embed, gain_grad[0], grad_head,
    )


def solution(mesh):
    in_specs = (
        P("ctx", None), P("ctx", None), P(), P(), P("ctx", "vocab"), P("ctx", "vocab"),
        P("vocab"), P(("ctx", "vocab"), None), P(), P(),
    )
    out_specs = (
        P(), P("ctx", "vocab"), P("ctx", "vocab"), P("vocab"), P("vocab"),
        P("ctx", "vocab"), P("ctx", "vocab"), P("vocab"), P(("ctx", "vocab"), None),
    )
    return jax.shard_map(local, mesh=mesh, in_specs=in_specs, out_specs=out_specs, check_vma=False)
```

```python
import functools

import jax
import jax.numpy as jnp
from jax import lax
from jax.experimental import pallas as pl
from jax.experimental.pallas import tpu as pltpu
from jax.sharding import PartitionSpec as P

EPSILON = 1e-06
MESH = pl.DeviceIdType.MESH
VMEM = pl.BlockSpec(memory_space=pltpu.VMEM)
ANY = pl.BlockSpec(memory_space=pl.ANY)
F32 = jnp.float32
BF16 = jnp.bfloat16
PARTS = (
    (0, 384, "xyz"),
    (640, 384, "yzx"),
    (1280, 256, "zxy"),
    (384, 256, "xyz"),
    (1024, 256, "yzx"),
    (1536, 256, "zxy"),
)


class Place:
    def __init__(self):
        self.ctx = lax.axis_index("ctx")
        self.v = lax.axis_index("vocab")
        self.c = {"x": self.ctx // 2, "y": self.v // 4, "z": self.v % 4}
        self.core = self.ctx % 2

    def at(self, ctx=None, v=None):
        return {"ctx": self.ctx if ctx is None else ctx, "vocab": self.v if v is None else v}

    def along(self, axis, step):
        i = lax.rem(self.c[axis] + step + 4, 4)
        if axis == "x":
            return self.at(ctx=i * 2 + self.core)
        if axis == "y":
            return self.at(v=i * 4 + self.c["z"])
        return self.at(v=self.c["y"] * 4 + i)

    def sibling(self):
        return self.at(ctx=self.c["x"] * 2 + 1 - self.core)

    def ctx_peer(self, o):
        return self.at(ctx=lax.rem(self.ctx + o, 8))

    def v_peer(self, o):
        return self.at(v=lax.rem(self.v + o, 16))


class Copies:
    def __init__(self, send, recv):
        self.send, self.recv, self.count, self.started = send, recv, 0, []

    def go(self, src, dst, device):
        assert self.count < self.send.shape[0]
        copy = pltpu.make_async_remote_copy(
            src_ref=src,
            dst_ref=dst,
            send_sem=self.send.at[self.count],
            recv_sem=self.recv.at[self.count],
            device_id=device,
            device_id_type=MESH,
        )
        self.count += 1
        copy.start()
        self.started.append(copy)
        return copy

    def finish(self):
        for copy in self.started:
            copy.wait_send()
        self.started = []


def greet(devices):
    barrier = pltpu.get_barrier_semaphore()
    for device in devices:
        pl.semaphore_signal(barrier, inc=1, device_id=device, device_id_type=MESH)
    pl.semaphore_wait(barrier, len(devices))


def run(*rings):
    rings = list(rings)
    while rings:
        left = []
        for ring in rings:
            try:
                next(ring)
                left.append(ring)
            except StopIteration:
                pass
        rings = left


def chain(*makers):
    for maker in makers:
        yield from maker()


def gather_ring(copies, here, axis, slab):
    me = here.c[axis]
    right, left = here.along(axis, 1), here.along(axis, -1)
    before, after = lax.rem(me + 3, 4), lax.rem(me + 1, 4)
    from_left = copies.go(slab(me, None), slab(me, None), right)
    from_right = copies.go(slab(me, None), slab(me, None), left)
    yield
    from_left.wait_recv()
    far_a = copies.go(slab(before, 0), slab(before, 0), right)
    from_right.wait_recv()
    far_b = copies.go(slab(after, 1), slab(after, 1), left)
    yield
    far_a.wait_recv()
    far_b.wait_recv()


def reduce_ring(copies, here, axis, slab, half, one, two, held, add):
    me = here.c[axis]
    right, left = here.along(axis, 1), here.along(axis, -1)
    before, after, far = lax.rem(me + 3, 4), lax.rem(me + 1, 4), lax.rem(me + 2, 4)
    a1 = copies.go(slab(far, 0), one.at[0], right)
    b1 = copies.go(slab(far, 1), one.at[1], left)
    a2 = copies.go(slab(after, 1), half(two.at[0], 1), right)
    b2 = copies.go(slab(before, 0), half(two.at[1], 0), left)
    yield
    a1.wait_recv()
    add(held.at[0], (slab(after, 0), one.at[0]))
    a3 = copies.go(held.at[0], half(two.at[0], 0), right)
    b1.wait_recv()
    add(held.at[1], (slab(before, 1), one.at[1]))
    b3 = copies.go(held.at[1], half(two.at[1], 1), left)
    yield
    a2.wait_recv()
    b2.wait_recv()
    a3.wait_recv()
    b3.wait_recv()


def add_refs(out, terms):
    lead = out.shape[:-2]
    total = 1
    for n in lead:
        total *= n

    def block(index):
        acc = terms[0][index].astype(F32)
        for term in terms[1:]:
            acc = acc + term[index].astype(F32)
        out[index] = acc.astype(out.dtype)

    if total == 1:
        block(tuple(0 for _ in lead) + (slice(None), slice(None)))
        return

    @pl.loop(0, total)
    def _(i):
        index = []
        for n in reversed(lead):
            index.append(i % n)
            i = i // n
        block(tuple(reversed(index)) + (slice(None), slice(None)))


def columns_kernel(rows, head, cols, head_sib, send, recv, local_sem):
    here = Place()
    copies = Copies(send, recv)
    greet(
        [here.ctx_peer(o) for o in range(1, 8)]
        + [here.along("y", 1), here.along("y", -1), here.along("z", 1), here.along("z", -1)]
    )
    y, z = here.c["y"], here.c["z"]

    def block(c):
        return cols.at[y // 2, c, y % 2, z]

    arrivals = []
    for o in range(1, 8):
        peer = lax.rem(here.ctx + o, 8)
        arrivals.append(copies.go(rows.at[peer], block(here.ctx), here.ctx_peer(o)))
    own = pltpu.make_async_copy(rows.at[here.ctx], block(here.ctx), local_sem)
    own.start()
    swap = copies.go(head, head_sib, here.sibling())
    own.wait()
    for arrival in arrivals:
        arrival.wait_recv()

    def span(h):
        return slice(None) if h is None else pl.ds(h * 4, 4)

    def y_first(i, h):
        return cols.at[i // 2, span(h), i % 2, z]

    def z_last(i, h):
        return cols.at[:, span(h), :, i]

    def z_first(i, h):
        return cols.at[y // 2, span(h), y % 2, i]

    def y_last(i, h):
        return cols.at[i // 2, span(h), i % 2]

    def both(first, second):
        run(
            chain(
                lambda: gather_ring(copies, here, *first), lambda: gather_ring(copies, here, *second)
            )
        )

    mark, kept = copies.count, copies.started
    copies.started = []

    @pl.when(here.core == 0)
    def _():
        both(("y", y_first), ("z", z_last))
        copies.finish()

    copies.count = mark

    @pl.when(here.core == 1)
    def _():
        both(("z", z_first), ("y", y_last))
        copies.finish()

    copies.started = kept
    swap.wait_recv()
    copies.finish()


def all_sum(copies, here, tile, group, line, out):
    group[here.v] = tile[...]
    ins = [copies.go(tile, group.at[here.v], here.v_peer(o)) for o in range(1, 16)]
    yield
    for copy in ins:
        copy.wait_recv()
    x = here.c["x"]
    line[x] = jnp.sum(group[...], axis=0)
    ins = [copies.go(line.at[x], line.at[x], here.along("x", o)) for o in (1, 2, 3)]
    yield
    for copy in ins:
        copy.wait_recv()
    out[...] = jnp.sum(line[...], axis=0)


def spread(row):
    return jnp.broadcast_to(row, (128, 128)).T


def lanes(values):
    total = jnp.sum(values.T, axis=0, keepdims=True)
    return [total[:, i * 128 : (i + 1) * 128] for i in range(4)]


def reduce_name(n, k, what):
    return f"{what}{n}{k}"


def middle_kernel(
    partial, gain, head_own, head_sib, position, mask, mask_row,
    proj_grad, gain_grad, loss, rows_own, rows_sib, lgr_own, lgr_sib, r, send, recv, local_sem,
):
    here = Place()
    copies = Copies(send, recv)
    greet(
        [here.along(a, s) for a in "xyz" for s in (1, -1)]
        + [here.along("x", 2)]
        + [here.v_peer(o) for o in range(1, 16)]
        + [here.ctx_peer(o) for o in range(1, 8)]
    )
    width = 7168
    x, y, z, core = here.c["x"], here.c["y"], here.c["z"], here.core
    head, rows = r["head"], r["rows"]
    loads = [
        pltpu.make_async_copy(head_own, head.at[pl.ds(0, 512)], local_sem.at[0]),
        pltpu.make_async_copy(head_sib, head.at[pl.ds(512, 512)], local_sem.at[1]),
    ]
    swap = copies.go(partial.at[:, 1 - core], r["sib"], here.sibling())
    for load in loads:
        load.start()
    swap.wait_recv()
    summed, two = r["summed"], r["two"]
    for i in range(4):
        summed[i] = partial[i, core] + r["sib"][i]

    def half(ref, h):
        return ref.at[pl.ds(h * 64, 64)]

    run(
        reduce_ring(
            copies, here, "x",
            lambda i, h: half(summed.at[i], h), half, r["one"], two, r["held"],
            lambda out, terms: out.__setitem__(..., terms[0][...] + terms[1][...]),
        )
    )
    total = summed[x] + two[0] + two[1]
    r["projected"][...] = total
    piece, pieces = r["piece"], r["pieces"]
    piece[...] = (total * gain[...]).astype(BF16).reshape(piece.shape)
    exchange = []
    for o in range(1, 4):
        to = lax.rem(z + o, 4)
        exchange.append(copies.go(piece.at[to], pieces.at[z], here.along("z", o)))
    pieces[z] = piece[z]
    r["square"][...] = lax.dot_general(
        jnp.ones((8, total.shape[1]), F32), total * total, (((1,), (1,)), ((), ())),
        precision=lax.Precision.HIGHEST, preferred_element_type=F32,
    )
    squares, scales = r["squares"], r["scales"]
    squares[here.v] = r["square"][...]
    for copy in exchange:
        copy.wait_recv()
    for i in range(4):
        rows[y, x, z, :, i * 448 : (i + 1) * 448] = pieces[i]

    def stage(part, k):
        off, w, order = part

        def slab(i, h):
            index = []
            for a in "yxz":
                at = order.index(a)
                index.append(i if at == k else slice(None) if at < k else here.c[a])
            lines = slice(None) if h is None else pl.ds(h * 16, 16)
            return rows.at[(*index, lines, pl.ds(off, w))]

        return lambda: gather_ring(copies, here, order[k], slab)

    def scale():
        ins = [copies.go(r["square"], squares.at[here.v], here.v_peer(o)) for o in range(1, 16)]
        yield
        yield
        for copy in ins:
            copy.wait_recv()
        scales[x] = lax.rsqrt(jnp.sum(squares[...], axis=0) / width + EPSILON)
        ins = [copies.go(scales.at[x], scales.at[x], here.along("x", o)) for o in range(1, 4)]
        yield
        yield
        for copy in ins:
            copy.wait_recv()

    run(*[chain(*[stage(part, k) for k in range(3)]) for part in PARTS], scale())

    for load in loads:
        load.wait()
    keep = pltpu.make_async_copy(rows, rows_own, local_sem.at[2])
    keep.start()
    swap_rows = copies.go(rows, rows_sib, here.sibling())
    raw = r["raw"]
    raw[...] = jnp.zeros_like(raw)

    @pl.loop(0, 4)
    def _(j):
        raw[...] += lax.dot_general(
            rows[j].reshape(512, 1792), head[:, pl.ds(pl.multiple_of(j * 1792, 128), 1792)],
            (((1,), (1,)), ((), ())), preferred_element_type=F32,
        )

    scale_wide, log_wide = r["scale_wide"], r["log_wide"]
    for i in range(4):
        scale_wide[i * 128 : (i + 1) * 128] = spread(scales[i, :1])
    column = lax.broadcasted_iota(jnp.int32, (512, 128), 1)
    exps = jnp.zeros((512, 128), F32)
    hits = jnp.zeros((512, 128), F32)
    for j in range(8):
        logit = raw[:, j * 128 : (j + 1) * 128] * scale_wide[...]
        exps = exps + jnp.exp(logit)
        hits = hits + jnp.where(position[...] == column + j * 128, logit, 0.0)
    tile, sums = r["tile"], r["sums"]
    for i, row in enumerate(lanes(exps) + lanes(hits)):
        tile[i : i + 1] = row
    run(all_sum(copies, here, tile, r["group"], r["line"], sums))
    logs = jnp.log(sums[:4])
    for i in range(4):
        log_wide[i * 128 : (i + 1) * 128] = spread(logs[i : i + 1])
    lost = jnp.sum(mask_row[...] * (logs - sums[4:]), axis=(0, 1), keepdims=True)
    loss[core] = jnp.broadcast_to(lost, (8, 128))
    swap_loss = copies.go(loss.at[core], loss.at[core], here.sibling())
    grad, grad_t = r["grad"], r["grad_t"]
    dots = jnp.zeros((512, 128), F32)
    for j in range(8):
        term = raw[:, j * 128 : (j + 1) * 128]
        prob = jnp.exp(term * scale_wide[...] - log_wide[...])
        hit = (position[...] == column + j * 128).astype(F32)
        wide = mask[...] * (prob - hit)
        rounded = wide.astype(BF16)
        grad[:, j * 128 : (j + 1) * 128] = rounded
        dots = dots + rounded.astype(F32) * term
        grad_t[j * 128 : (j + 1) * 128] = (wide * scale_wide[...]).T.astype(BF16)
    dot_tile = r["dot_tile"]
    for i, row in enumerate(lanes(dots)):
        dot_tile[i : i + 1] = row
        dot_tile[i + 4 : i + 5] = row
    swap_grad = copies.go(grad_t.at[pl.ds(512, 512)], lgr_sib, here.sibling())
    keep_grad = pltpu.make_async_copy(grad_t.at[pl.ds(0, 512)], lgr_own, local_sem.at[3])
    keep_grad.start()

    terms, whole = r["terms"], r["whole"]

    def half_lines(ref, h):
        index = (slice(None),) * (len(ref.shape) - 2) + (pl.ds(h * 16, 16),)
        return ref.at[index]

    def part_rings(n, part):
        off, w, order = part
        order = order[::-1]
        axes = "yxz"
        source = terms
        cols = pl.ds(off, w)
        for k in range(3):
            one, two, held = (r[reduce_name(n, k, what)] for what in ("one", "two", "held"))
            axis = order[k]

            def slab(i, h, source=source, axes=axes, cols=cols, axis=axis):
                index = tuple(i if a == axis else slice(None) for a in axes)
                lines = slice(None) if h is None else pl.ds(h * 16, 16)
                return source.at[(*index, lines, cols)]

            yield from reduce_ring(
                copies, here, axis, slab, half_lines, one, two, held, add_refs
            )
            if k < 2:
                out = r[reduce_name(n, k, "out")]
                add_refs(out, (slab(here.c[axis], None), two.at[0], two.at[1]))
                source, cols = out, slice(None)
            else:
                own = slab(here.c[axis], None)[...].astype(F32)
                whole[:, off : off + w] = own + two[0].astype(F32) + two[1].astype(F32)
            axes = axes.replace(axis, "")

    def product(part):
        off, w, _ = part

        @pl.loop(0, 4)
        def _(j):
            terms[j, :, :, :, off : off + w] = (
                jnp.dot(
                    grad[...], head[:, pl.ds(pl.multiple_of(j * 1792 + off, 128), w)],
                    preferred_element_type=F32,
                )
                .astype(BF16)
                .reshape(4, 4, 32, w)
            )

    rings = []
    for n, part in enumerate(PARTS):
        product(part)
        ring = part_rings(n, part)
        next(ring)
        rings.append(ring)
    row_dots = all_sum(copies, here, dot_tile, r["group2"], r["line2"], r["sums2"])
    run(*rings, row_dots)

    back, backs = r["back"], r["backs"]
    for i in range(4):
        back[i] = whole[:, i * 448 : (i + 1) * 448]
    exchange = []
    for o in range(1, 4):
        to = lax.rem(z + o, 4)
        exchange.append(copies.go(back.at[to], backs.at[z], here.along("z", o)))
    backs[z] = back[z]
    row_scale = scale_wide[pl.ds(pl.multiple_of(x * 128, 128), 128)][:, :1]
    row_dot = spread(r["sums2"][pl.ds(x, 1)])[:, :1]
    wide = r["projected"][...]
    for copy in exchange:
        copy.wait_recv()
    normed_grad = backs[...].reshape(128, 448)
    grad_out = row_scale * (normed_grad * gain[...]) - wide * (
        row_scale * row_scale * row_scale
    ) * (row_dot / width)
    proj_grad[x, core] = grad_out.astype(BF16)

    def row_slab(i, h):
        lines = slice(None) if h is None else pl.ds(h * 64, 64)
        return proj_grad.at[i, core, lines]

    def gain_sum():
        mine, every = r["gain_mine"], r["gain_all"]
        mine[...] = jnp.broadcast_to(
            jnp.sum(normed_grad * wide * row_scale, axis=0, keepdims=True), (8, 448)
        )
        every[here.ctx] = mine[...]
        ins = [copies.go(mine, every.at[here.ctx], here.ctx_peer(o)) for o in range(1, 8)]
        yield
        yield
        for copy in ins:
            copy.wait_recv()
        gain_grad[...] = jnp.sum(every[...], axis=0)[:1]

    run(gather_ring(copies, here, "x", row_slab), gain_sum())
    copies.go(proj_grad.at[:, core], proj_grad.at[:, core], here.sibling()).wait_recv()
    for copy in (swap_rows, swap_loss, swap_grad):
        copy.wait_recv()
    keep.wait()
    keep_grad.wait()
    copies.finish()


def back_kernel(
    terms, inputs, gains, scales, grads, gain_grads,
    one_a, two_a, held_a, out_a, one_b, two_b, held_b, out_b,
    one_c, two_c, held_c, one_d, two_d, held_d,
    summed, sent, got, mine_dot, dots, mine_gain, gain_all, send, recv, send_far, recv_far,
):
    here = Place()
    copies = Copies(send, recv)
    y, z, v, ctx = here.c["y"], here.c["z"], here.v, here.ctx
    width = 7168
    barrier = pltpu.get_barrier_semaphore()
    near = (
        [here.along(a, s) for a in "yz" for s in (1, -1)]
        + [here.v_peer(o) for o in range(1, 16)]
        + [here.ctx_peer(o) for o in range(1, 8)]
    )
    for device in near:
        pl.semaphore_signal(barrier, inc=1, device_id=device, device_id_type=MESH)
    for source in range(16):
        pl.semaphore_signal(
            barrier, inc=1, device_id=here.at(ctx=v // 2, v=source), device_id_type=MESH
        )
    pl.semaphore_wait(barrier, len(near) + 16)

    def span(h):
        return slice(None) if h is None else pl.ds(h * 4, 4)

    def back_y(i, h):
        return terms.at[i // 2, span(h), i % 2]

    def back_z(i, h):
        return terms.at[:, span(h), :, i]

    @pl.when(here.core == 0)
    def _():
        run(
            reduce_ring(
                copies, here, "y", back_y, lambda ref, h: ref.at[span(h)],
                one_a, two_a, held_a, add_refs,
            )
        )
        add_refs(out_a, (back_y(y, None), two_a.at[0], two_a.at[1]))
        run(
            reduce_ring(
                copies, here, "z", lambda i, h: out_a.at[span(h), i],
                lambda ref, h: ref.at[span(h)], one_c, two_c, held_c, add_refs,
            )
        )
        add_refs(summed, (out_a.at[:, z], two_c.at[0], two_c.at[1]))
        copies.finish()

    copies.count = 0

    @pl.when(here.core == 1)
    def _():
        run(
            reduce_ring(
                copies, here, "z", back_z, lambda ref, h: ref.at[:, span(h)],
                one_b, two_b, held_b, add_refs,
            )
        )
        add_refs(out_b, (back_z(z, None), two_b.at[0], two_b.at[1]))
        run(
            reduce_ring(
                copies, here, "y", lambda i, h: out_b.at[i // 2, span(h), i % 2],
                lambda ref, h: ref.at[span(h)], one_d, two_d, held_d, add_refs,
            )
        )
        add_refs(summed, (out_b.at[y // 2, :, y % 2], two_d.at[0], two_d.at[1]))
        copies.finish()

    @pl.loop(0, 8)
    def _(c):
        sent[0, c] = summed[c][:, :448].astype(BF16)
        sent[1, c] = summed[c][:, 448:].astype(BF16)

    def far_copy(o, s):
        to = lax.rem(ctx + o, 8)
        return pltpu.make_async_remote_copy(
            src_ref=sent.at[s, to],
            dst_ref=got.at[v // 8, pl.ds(lax.rem(v, 8) * 16, 16)],
            send_sem=send_far.at[o * 2 + s],
            recv_sem=recv_far.at[v],
            device_id=here.at(ctx=to, v=ctx * 2 + s),
            device_id_type=MESH,
        )

    for o in range(8):
        for s in range(2):
            if o:
                far_copy(o, s).start()
            else:

                @pl.when(v != ctx * 2 + s)
                def _(s=s):
                    far_copy(0, s).start()

                @pl.when(v == ctx * 2 + s)
                def _(s=s):
                    got[v // 8, pl.ds(lax.rem(v, 8) * 16, 16)] = sent[s, ctx]

    for source in range(16):

        @pl.when(jnp.logical_or(ctx != v // 2, v != source))
        def _(source=source):
            pltpu.make_async_remote_copy(
                src_ref=sent.at[0, 0],
                dst_ref=got.at[source // 8, pl.ds(source % 8 * 16, 16)],
                send_sem=send_far.at[0],
                recv_sem=recv_far.at[source],
                device_id=here.at(ctx=lax.rem(ctx + 1, 8)),
                device_id_type=MESH,
            ).wait_recv()

    for e in range(2):
        back = got[e].astype(F32)
        wide = inputs[e].astype(F32)
        mine_dot[e] = lax.dot_general(
            jnp.ones((8, 448), F32), back * gains[e] * wide, (((1,), (1,)), ((), ())),
            precision=lax.Precision.HIGHEST, preferred_element_type=F32,
        )
        mine_gain[e] = jnp.broadcast_to(
            jnp.sum(back * wide * scales[e], axis=0, keepdims=True), (8, 448)
        )
    ins = [copies.go(mine_dot, dots.at[v], here.v_peer(o)) for o in range(1, 16)]
    gain_ins = [copies.go(mine_gain, gain_all.at[ctx], here.ctx_peer(o)) for o in range(1, 8)]
    dots[v] = mine_dot[...]
    gain_all[ctx] = mine_gain[...]
    for copy in ins:
        copy.wait_recv()
    for e in range(2):
        back = got[e].astype(F32)
        wide = inputs[e].astype(F32)
        dot = jnp.sum(dots[:, e], axis=0).T[:, :1]
        scale = scales[e]
        grads[e] = (
            scale * (back * gains[e]) - wide * (scale * scale * scale) * (dot / width)
        ).astype(BF16)
    for copy in gain_ins:
        copy.wait_recv()
    gain_grads[...] = jnp.sum(gain_all[...], axis=0)
    for o in range(8):
        for s in range(2):
            if o:
                far_copy(o, s).wait_send()
            else:

                @pl.when(v != ctx * 2 + s)
                def _(s=s):
                    far_copy(0, s).wait_send()

    copies.finish()


def head_kernel(own_grad, sib_grad, own, sib, out):
    out[...] = (
        jnp.dot(own_grad[...], own[0], preferred_element_type=F32)
        + jnp.dot(sib_grad[...], sib[0], preferred_element_type=F32)
    ).astype(BF16)


def params(number, limit=56):
    return pltpu.CompilerParams(
        collective_id=number, has_side_effects=True, vmem_limit_bytes=limit * 2**20
    )


def plain():
    return pltpu.CompilerParams(vmem_limit_bytes=56 * 2**20)


def sems(n):
    return [pltpu.SemaphoreType.DMA((n,)), pltpu.SemaphoreType.DMA((n,))]


def shape(dims, kind):
    return jax.ShapeDtypeStruct(dims, kind)


def middle_scratch():
    scratch = {
        "head": pltpu.VMEM((1024, 7168), BF16),
        "rows": pltpu.VMEM((4, 4, 4, 32, 1792), BF16),
        "terms": pltpu.VMEM((4, 4, 4, 32, 1792), BF16),
        "raw": pltpu.VMEM((512, 1024), F32),
        "grad": pltpu.VMEM((512, 1024), BF16),
        "grad_t": pltpu.VMEM((1024, 512), BF16),
        "scale_wide": pltpu.VMEM((512, 128), F32),
        "log_wide": pltpu.VMEM((512, 128), F32),
        "sib": pltpu.VMEM((4, 128, 448), F32),
        "summed": pltpu.VMEM((4, 128, 448), F32),
        "one": pltpu.VMEM((2, 64, 448), F32),
        "two": pltpu.VMEM((2, 128, 448), F32),
        "held": pltpu.VMEM((2, 64, 448), F32),
        "projected": pltpu.VMEM((128, 448), F32),
        "square": pltpu.VMEM((8, 128), F32),
        "squares": pltpu.VMEM((16, 8, 128), F32),
        "scales": pltpu.VMEM((4, 8, 128), F32),
        "piece": pltpu.VMEM((4, 32, 448), BF16),
        "pieces": pltpu.VMEM((4, 32, 448), BF16),
        "back": pltpu.VMEM((4, 32, 448), F32),
        "backs": pltpu.VMEM((4, 32, 448), F32),
        "whole": pltpu.VMEM((32, 1792), F32),
        "gain_mine": pltpu.VMEM((8, 448), F32),
        "gain_all": pltpu.VMEM((8, 8, 448), F32),
    }
    for name in ("tile", "sums", "dot_tile", "sums2"):
        scratch[name] = pltpu.VMEM((8, 128), F32)
    for name in ("group", "group2"):
        scratch[name] = pltpu.VMEM((16, 8, 128), F32)
    for name in ("line", "line2"):
        scratch[name] = pltpu.VMEM((4, 8, 128), F32)
    for n, (_, w, _) in enumerate(PARTS):
        dims = (4, 4)
        for k in range(3):
            scratch[reduce_name(n, k, "one")] = pltpu.VMEM((2, *dims, 16, w), BF16)
            scratch[reduce_name(n, k, "held")] = pltpu.VMEM((2, *dims, 16, w), BF16)
            scratch[reduce_name(n, k, "two")] = pltpu.VMEM((2, *dims, 32, w), BF16)
            if k < 2:
                scratch[reduce_name(n, k, "out")] = pltpu.VMEM((*dims, 32, w), BF16)
            dims = dims[1:]
    return scratch


def scale_of(values):
    return lax.rsqrt(jnp.mean(values * values, axis=-1, keepdims=True) + EPSILON)


def contract_first(left, right):
    return lax.dot_general(
        left, right, (((0,), (0,)), ((), ())), preferred_element_type=F32
    )


def contract_last(left, right):
    return lax.dot_general(
        left, right, (((1,), (1,)), ((), ())), preferred_element_type=F32
    )


def local(
    hidden_state, embedded_next, gain_hidden, gain_embed, proj_hidden, proj_embed,
    final_gain, head, targets, loss_mask,
):
    width = hidden_state.shape[1]
    token_total = targets.shape[0]
    ctx, v = lax.axis_index("ctx"), lax.axis_index("vocab")
    x, core = ctx // 2, ctx % 2
    sliver = (v % 8) * 16
    first = v < 8
    raw = jnp.where(
        first,
        lax.dynamic_slice_in_dim(hidden_state, sliver, 16, 0),
        lax.dynamic_slice_in_dim(embedded_next, sliver, 16, 0),
    ).astype(F32)
    gain_in = jnp.where(first, gain_hidden, gain_embed)
    normed = (raw * scale_of(raw) * gain_in).astype(BF16)
    normed = normed.reshape(16, 8, 896).transpose(1, 0, 2)

    cols, head_sib = pl.pallas_call(
        columns_kernel,
        out_shape=[shape((2, 8, 2, 4, 16, 896), BF16), shape(head.shape, BF16)],
        in_specs=[VMEM, ANY],
        out_specs=[ANY, ANY],
        scratch_shapes=sems(16) + [pltpu.SemaphoreType.DMA],
        compiler_params=params(1),
        name="columns",
    )(normed, head)
    hidden_cols = cols[0].reshape(1024, 896)
    embed_cols = cols[1].reshape(1024, 896)
    partial = jnp.dot(hidden_cols, proj_hidden, preferred_element_type=F32) + jnp.dot(
        embed_cols, proj_embed, preferred_element_type=F32
    )

    def of_core(values, k):
        return lax.dynamic_index_in_dim(values.reshape(4, 2, 128), k, 1, keepdims=False)

    my_targets = of_core(targets, core)
    mask_row = of_core(loss_mask, core).astype(F32)
    own_at = my_targets - (ctx * 16 + v) * 512
    sib_at = my_targets - ((ctx + 1 - 2 * core) * 16 + v) * 512
    position = jnp.where(
        (own_at >= 0) & (own_at < 512),
        own_at,
        jnp.where((sib_at >= 0) & (sib_at < 512), sib_at + 512, -1),
    )
    block = pl.BlockSpec((1, 512, 1792), lambda i: (i, 0, 0))
    head_block = pl.BlockSpec((512, 1792), lambda i: (0, i))
    proj_grad, gain_grad, loss, rows_own, rows_sib, lgr_own, lgr_sib = pl.pallas_call(
        middle_kernel,
        out_shape=[
            shape((4, 2, 128, 448), BF16), shape((1, 448), F32), shape((2, 8, 128), F32),
            shape((4, 4, 4, 32, 1792), BF16), shape((4, 4, 4, 32, 1792), BF16),
            shape((512, 512), BF16), shape((512, 512), BF16),
        ],
        in_specs=[VMEM, VMEM, ANY, ANY, VMEM, VMEM, VMEM],
        out_specs=[VMEM, VMEM, VMEM, ANY, ANY, ANY, ANY],
        scratch_shapes=[middle_scratch()] + sems(264) + [pltpu.SemaphoreType.DMA((4,))],
        compiler_params=params(2, 60),
        name="middle",
    )(
        partial.reshape(4, 2, 128, 448), final_gain[None, :], head, head_sib,
        position.reshape(512, 1), mask_row.reshape(512, 1), mask_row,
    )
    mean_loss = (loss[0, 0, 0] + loss[1, 0, 0]) / token_total
    proj_grad = proj_grad.reshape(1024, 448)

    grad_head = pl.pallas_call(
        head_kernel,
        grid=(4,),
        out_shape=shape(head.shape, BF16),
        in_specs=[
            pl.BlockSpec((512, 512), lambda i: (0, 0)), pl.BlockSpec((512, 512), lambda i: (0, 0)),
            block, block,
        ],
        out_specs=head_block,
        compiler_params=plain(),
        name="head_grad",
    )(lgr_own, lgr_sib, rows_own.reshape(4, 512, 1792), rows_sib.reshape(4, 512, 1792))

    grad_proj_hidden = contract_first(hidden_cols, proj_grad).astype(BF16)
    grad_proj_embed = contract_first(embed_cols, proj_grad).astype(BF16)
    back = jnp.stack(
        [
            contract_last(proj_grad, proj_hidden).astype(BF16),
            contract_last(proj_grad, proj_embed).astype(BF16),
        ]
    )
    start = v * 448
    inputs = jnp.stack(
        [
            lax.dynamic_slice_in_dim(hidden_state, start, 448, 1),
            lax.dynamic_slice_in_dim(embedded_next, start, 448, 1),
        ]
    )
    gains = jnp.stack(
        [
            lax.dynamic_slice_in_dim(gain_hidden, start, 448, 0),
            lax.dynamic_slice_in_dim(gain_embed, start, 448, 0),
        ]
    )[:, None, :]
    in_scales = jnp.stack(
        [scale_of(hidden_state.astype(F32)), scale_of(embedded_next.astype(F32))]
    )

    def ring_scratch(halves, wholes, out=None):
        return [
            pltpu.VMEM((2, *halves), BF16), pltpu.VMEM((2, *wholes), BF16),
            pltpu.VMEM((2, *halves), BF16),
        ] + ([pltpu.VMEM(wholes, BF16)] if out else [])

    grads, gain_grads = pl.pallas_call(
        back_kernel,
        out_shape=[shape((2, 128, 448), BF16), shape((2, 8, 448), F32)],
        in_specs=[VMEM] * 4,
        out_specs=[VMEM] * 2,
        scratch_shapes=ring_scratch((4, 4, 16, 896), (8, 4, 16, 896), True)
        + ring_scratch((2, 4, 2, 16, 896), (2, 8, 2, 16, 896), True)
        + ring_scratch((4, 16, 896), (8, 16, 896))
        + ring_scratch((4, 16, 896), (8, 16, 896))
        + [
            pltpu.VMEM((8, 16, 896), F32),
            pltpu.VMEM((2, 8, 16, 448), BF16),
            pltpu.VMEM((2, 128, 448), BF16),
            pltpu.VMEM((2, 8, 128), F32),
            pltpu.VMEM((16, 2, 8, 128), F32),
            pltpu.VMEM((2, 8, 448), F32),
            pltpu.VMEM((8, 2, 8, 448), F32),
        ]
        + sems(48)
        + sems(16),
        compiler_params=params(5),
        name="back",
    )(back.reshape(2, 8, 2, 4, 16, 896), inputs, gains, in_scales)

    return (
        mean_loss, grads[0], grads[1], gain_grads[0, 0], gain_grads[1, 0],
        grad_proj_hidden, grad_proj_embed, gain_grad[0], grad_head,
    )


def solution(mesh):
    in_specs = (
        P("ctx", None), P("ctx", None), P(), P(), P("ctx", "vocab"), P("ctx", "vocab"),
        P("vocab"), P(("ctx", "vocab"), None), P(), P(),
    )
    out_specs = (
        P(), P("ctx", "vocab"), P("ctx", "vocab"), P("vocab"), P("vocab"),
        P("ctx", "vocab"), P("ctx", "vocab"), P("vocab"), P(("ctx", "vocab"), None),
    )
    return jax.shard_map(local, mesh=mesh, in_specs=in_specs, out_specs=out_specs, check_vma=False)
```

```python
import jax
import jax.numpy as jnp
from jax import lax
from jax.experimental import pallas as pl
from jax.experimental.pallas import tpu as pltpu
from jax.sharding import PartitionSpec as P

EPSILON = 1e-06
MESH = pl.DeviceIdType.MESH
VMEM = pl.BlockSpec(memory_space=pltpu.VMEM)
ANY = pl.BlockSpec(memory_space=pl.ANY)
F32 = jnp.float32
BF16 = jnp.bfloat16
PARTS = (
    (0, 384, "xyz"),
    (384, 384, "yzx"),
    (768, 256, "zxy"),
    (1024, 256, "xyz"),
    (1280, 256, "yzx"),
    (1536, 256, "zxy"),
)
BATCHES = ((0, 1024), (1024, 768))


class Place:
    def __init__(self):
        self.ctx = lax.axis_index("ctx")
        self.v = lax.axis_index("vocab")
        self.c = {"x": self.ctx // 2, "y": self.v // 4, "z": self.v % 4}
        self.core = self.ctx % 2

    def at(self, ctx=None, v=None):
        return {"ctx": self.ctx if ctx is None else ctx, "vocab": self.v if v is None else v}

    def along(self, axis, step):
        i = lax.rem(self.c[axis] + step + 4, 4)
        if axis == "x":
            return self.at(ctx=i * 2 + self.core)
        if axis == "y":
            return self.at(v=i * 4 + self.c["z"])
        return self.at(v=self.c["y"] * 4 + i)

    def sibling(self):
        return self.at(ctx=self.c["x"] * 2 + 1 - self.core)

    def ctx_peer(self, o):
        return self.at(ctx=lax.rem(self.ctx + o, 8))

    def v_peer(self, o):
        return self.at(v=lax.rem(self.v + o, 16))


class Copies:
    def __init__(self, send, recv):
        self.send, self.recv, self.count, self.started = send, recv, 0, []

    def go(self, src, dst, device):
        assert self.count < self.send.shape[0]
        copy = pltpu.make_async_remote_copy(
            src_ref=src,
            dst_ref=dst,
            send_sem=self.send.at[self.count],
            recv_sem=self.recv.at[self.count],
            device_id=device,
            device_id_type=MESH,
        )
        self.count += 1
        copy.start()
        self.started.append(copy)
        return copy

    def finish(self):
        for copy in self.started:
            copy.wait_send()
        self.started = []


def greet(devices):
    barrier = pltpu.get_barrier_semaphore()
    for device in devices:
        pl.semaphore_signal(barrier, inc=1, device_id=device, device_id_type=MESH)


def met(devices):
    pl.semaphore_wait(pltpu.get_barrier_semaphore(), len(devices))


def run(*rings):
    rings = list(rings)
    while rings:
        left = []
        for ring in rings:
            try:
                next(ring)
                left.append(ring)
            except StopIteration:
                pass
        rings = left


def chain(*makers):
    for maker in makers:
        yield from maker()


def gather_ring(copies, here, axis, slab):
    me = here.c[axis]
    right, left = here.along(axis, 1), here.along(axis, -1)
    before, after = lax.rem(me + 3, 4), lax.rem(me + 1, 4)

    def send(i, h, device):
        return copies.go(slab(i, h), slab(i, h), device)

    right_0, left_1 = send(me, 0, right), send(me, 1, left)
    right_1, left_0 = send(me, 1, right), send(me, 0, left)
    yield
    right_0.wait_recv()
    far_a = send(before, 0, right)
    left_1.wait_recv()
    far_b = send(after, 1, left)
    yield
    for copy in (right_1, left_0, far_a, far_b):
        copy.wait_recv()


def gather_near(copies, here, axis, slab):
    me = here.c[axis]
    ins = [copies.go(slab(me, None), slab(me, None), here.along(axis, o)) for o in (1, 2, 3)]
    yield
    for copy in ins:
        copy.wait_recv()


def reduce_ring(copies, here, axis, slab, half, one, two, held, add):
    if isinstance(axis, str):
        me, right, left = here.c[axis], here.along(axis, 1), here.along(axis, -1)
    else:
        me, right, left = axis
    before, after, far = lax.rem(me + 3, 4), lax.rem(me + 1, 4), lax.rem(me + 2, 4)
    a1 = copies.go(slab(far, 0), one.at[0], right)
    b1 = copies.go(slab(far, 1), one.at[1], left)
    a2 = copies.go(slab(after, 1), half(two.at[0], 1), right)
    b2 = copies.go(slab(before, 0), half(two.at[1], 0), left)
    yield
    a1.wait_recv()
    add(held.at[0], (slab(after, 0), one.at[0]))
    a3 = copies.go(held.at[0], half(two.at[0], 0), right)
    b1.wait_recv()
    add(held.at[1], (slab(before, 1), one.at[1]))
    b3 = copies.go(held.at[1], half(two.at[1], 1), left)
    yield
    a2.wait_recv()
    b2.wait_recv()
    a3.wait_recv()
    b3.wait_recv()


def reduce_near(copies, here, axis, slab, recv, finish):
    if isinstance(axis, str):
        me, to = here.c[axis], [here.along(axis, o) for o in (1, 2, 3)]
    else:
        me, to = axis
    ins = [
        copies.go(slab(lax.rem(me + o, 4)), recv.at[o - 1], to[o - 1]) for o in (1, 2, 3)
    ]
    yield
    for copy in ins:
        copy.wait_recv()
    finish(slab(me), [recv.at[o] for o in range(3)])


def add_refs(out, terms):
    lead = out.shape[:-2]
    total = 1
    for n in lead:
        total *= n

    def block(index):
        acc = terms[0][index].astype(F32)
        for term in terms[1:]:
            acc = acc + term[index].astype(F32)
        out[index] = acc.astype(out.dtype)

    if total == 1:
        block(tuple(0 for _ in lead) + (slice(None), slice(None)))
        return

    @pl.loop(0, total)
    def _(i):
        index = []
        for n in reversed(lead):
            index.append(i % n)
            i = i // n
        block(tuple(reversed(index)) + (slice(None), slice(None)))


def all_sum(copies, here, tile, group, line, out):
    group[here.v] = tile[...]
    ins = [copies.go(tile, group.at[here.v], here.v_peer(o)) for o in range(1, 16)]
    yield
    for copy in ins:
        copy.wait_recv()
    x = here.c["x"]
    line[x] = jnp.sum(group[...], axis=0)
    ins = [copies.go(line.at[x], line.at[x], here.along("x", o)) for o in (1, 2, 3)]
    yield
    for copy in ins:
        copy.wait_recv()
    out[...] = jnp.sum(line[...], axis=0)


def spread(row):
    return jnp.broadcast_to(row, (128, 128)).T


def lanes(values):
    total = jnp.sum(values.T, axis=0, keepdims=True)
    return [total[:, i * 128 : (i + 1) * 128] for i in range(4)]


class Bag:
    def __init__(self, refs):
        self.__dict__.update(refs)


def trickle(pieces):
    for start in pieces:
        start()
        yield


def middle_kernel(
    hidden, embed, gain_h, gain_e, proj_h, proj_e, gain, head_own, targets, loss_mask,
    proj_grad, gain_grad, loss, cols_out, half_out, rows_sib, lgr_sib,
    r, send, recv, local_sem,
):
    r = Bag(r)
    here = Place()
    copies = Copies(send, recv)
    friends = [here.ctx_peer(o) for o in range(1, 8)] + [here.v_peer(o) for o in range(1, 16)]
    greet(friends)
    width = 7168
    x, y, z, core = here.c["x"], here.c["y"], here.c["z"], here.core
    head, rows, cols = r.head, r.rows, r.cols
    locals_ = []

    def bring(src, dst):
        copy = pltpu.make_async_copy(src, dst, local_sem.at[len(locals_)])
        copy.start()
        locals_.append(copy)
        return copy

    sliver = pl.ds(pl.multiple_of(lax.rem(here.v, 8) * 16, 16), 16)
    raw_in = [bring(hidden.at[sliver], r.raw_in.at[0]), bring(embed.at[sliver], r.raw_in.at[1])]
    weights = [bring(proj_h, r.weights.at[0]), bring(proj_e, r.weights.at[1])]
    load = bring(head_own, head.at[pl.ds(0, 512)])
    for copy in raw_in:
        copy.wait()
    first = here.v < 8
    normed = r.normed

    def norm(e, gains):
        wide = r.raw_in[e].astype(F32)
        scale = lax.rsqrt(jnp.mean(wide * wide, axis=-1, keepdims=True) + EPSILON)
        for c in range(8):
            part = slice(c * 896, (c + 1) * 896)
            normed[c] = (wide[:, part] * scale * gains[:, part]).astype(BF16)

    @pl.when(first)
    def _():
        norm(0, gain_h)

    @pl.when(jnp.logical_not(first))
    def _():
        norm(1, gain_e)

    met(friends)

    def sliver_at(c):
        return cols.at[y // 2, c // 2, c % 2, y % 2, z]

    arrivals = []
    for o in range(1, 8):
        peer = lax.rem(here.ctx + o, 8)
        arrivals.append(copies.go(normed.at[peer], sliver_at(here.ctx), here.ctx_peer(o)))
    cols[y // 2, x, core, y % 2, z] = normed[here.ctx]
    for arrival in arrivals:
        arrival.wait_recv()

    def col_slabs(part):
        lanes_ = pl.ds(*part)

        def span(h):
            return slice(None) if h is None else pl.ds(h * 2, 2)

        return {
            "y_first": lambda i, h: cols.at[i // 2, span(h), :, i % 2, z, :, lanes_],
            "z_last": lambda i, h: cols.at[:, span(h), :, :, i, :, lanes_],
            "z_first": lambda i, h: cols.at[y // 2, span(h), :, y % 2, i, :, lanes_],
            "y_last": lambda i, h: cols.at[i // 2, span(h), :, i % 2, :, :, lanes_],
        }

    def col_ring(part, names):
        slabs = col_slabs(part)
        return chain(
            lambda: gather_near(copies, here, names[0][0], slabs[names[0]]),
            lambda: gather_ring(copies, here, names[1][0], slabs[names[1]]),
        )

    head_pieces = []

    def head_piece(i):
        piece_rows = pl.ds(i * 128, 128)
        head_pieces.append(
            copies.go(
                head_own.at[piece_rows], head.at[pl.ds(512 + i * 128, 128)], here.sibling()
            )
        )

    for i in range(4):
        head_piece(i)
    mark, kept = copies.count, copies.started
    copies.started = []

    @pl.when(core == 0)
    def _():
        run(*[col_ring(part, ("y_first", "z_last")) for part in ((0, 512), (512, 384))])
        copies.finish()

    copies.count = mark

    @pl.when(core == 1)
    def _():
        run(*[col_ring(part, ("z_first", "y_last")) for part in ((0, 512), (512, 384))])
        copies.finish()

    copies.started = kept
    for copy in weights:
        copy.wait()

    def project(k):
        return contract_last(cols[0, :, k].reshape(512, 896), r.weights[0]) + contract_last(
            cols[1, :, k].reshape(512, 896), r.weights[1]
        )

    r.away[...] = project(1 - core).reshape(4, 128, 448)
    swap = copies.go(r.away, r.sib, here.sibling())
    summed = r.summed
    summed[...] = project(core).reshape(4, 128, 448)
    bring(cols, cols_out)
    tgt_wide, mask_wide = r.tgt_wide, r.mask_wide
    mask_rows = []
    for i in range(4):
        at = pl.ds(i * 2 + core, 1)
        tgt_wide[i * 128 : (i + 1) * 128] = spread(targets[at].astype(F32))
        mask_row = loss_mask[at].astype(F32)
        mask_rows.append(mask_row)
        mask_wide[i * 128 : (i + 1) * 128] = spread(mask_row)
    swap.wait_recv()
    for i in range(4):
        summed[i] += r.sib[i]
        r.summed_out[i] = summed[i].astype(BF16)

    def add_x(own, others):
        del own
        total = summed[x]
        for other in others:
            total = total + other[...].astype(F32)
        r.projected[...] = total

    run(reduce_near(copies, here, "x", lambda i: r.summed_out.at[i], r.three, add_x))
    total = r.projected[...]
    piece, pieces = r.piece, r.pieces
    piece[...] = (total * gain[...]).astype(BF16).reshape(piece.shape)
    exchange = []
    for o in range(1, 4):
        to = lax.rem(z + o, 4)
        exchange.append(copies.go(piece.at[to], pieces.at[z], here.along("z", o)))
    pieces[z] = piece[z]
    r.square[...] = lax.dot_general(
        jnp.ones((8, total.shape[1]), F32), total * total, (((1,), (1,)), ((), ())),
        precision=lax.Precision.HIGHEST, preferred_element_type=F32,
    )
    squares, scales = r.squares, r.scales
    squares[here.v] = r.square[...]
    for copy in exchange:
        copy.wait_recv()
    for i in range(4):
        rows[y, x, z, :, i * 448 : (i + 1) * 448] = pieces[i]

    def stage(part, k):
        off, w, order = part

        def slab(i, h):
            index = []
            for a in "yxz":
                at = order.index(a)
                index.append(i if at == k else slice(None) if at < k else here.c[a])
            lines = slice(None) if h is None else pl.ds(h * 16, 16)
            return rows.at[(*index, lines, pl.ds(off, w))]

        ring = gather_near if k < 2 else gather_ring
        return lambda: ring(copies, here, order[k], slab)

    def scale():
        ins = [copies.go(r.square, squares.at[here.v], here.v_peer(o)) for o in range(1, 16)]
        yield
        yield
        for copy in ins:
            copy.wait_recv()
        scales[x] = lax.rsqrt(jnp.sum(squares[...], axis=0) / width + EPSILON)
        ins = [copies.go(scales.at[x], scales.at[x], here.along("x", o)) for o in range(1, 4)]
        yield
        yield
        for copy in ins:
            copy.wait_recv()

    raw = r.raw

    def logits_of(batch):
        off, w = BATCHES[batch]

        @pl.loop(0, 4)
        def _(j):
            term = lax.dot_general(
                rows[j, :, :, :, off : off + w].reshape(512, w),
                head[:, pl.ds(pl.multiple_of(j * 1792 + off, 128), w)],
                (((1,), (1,)), ((), ())), preferred_element_type=F32,
            )
            if batch:
                raw[...] += term
            else:

                @pl.when(j == 0)
                def _():
                    raw[...] = term

                @pl.when(j > 0)
                def _():
                    raw[...] += term

    gathers = [chain(*[stage(part, k) for k in range(3)]) for part in PARTS]
    leading, trailing, scaling = gathers[:3], gathers[3:], scale()

    def advance(group):
        alive = False
        for ring in group:
            try:
                next(ring)
                alive = True
            except StopIteration:
                pass
        return alive

    advance(leading)
    advance([scaling])
    alive = True
    while alive:
        alive = advance(leading)
        advance(trailing)
        advance([scaling])
    while advance([scaling]):
        pass
    load.wait()
    for copy in head_pieces:
        copy.wait_recv()
    logits_of(0)
    advance(trailing)
    logits_of(1)

    scale_wide, log_wide = r.scale_wide, r.log_wide
    for i in range(4):
        scale_wide[i * 128 : (i + 1) * 128] = spread(scales[i, :1])
    column = lax.broadcasted_iota(jnp.int32, (512, 128), 1)
    starts = [(here.ctx * 16 + here.v) * 512, ((here.ctx + 1 - 2 * core) * 16 + here.v) * 512]

    def is_hit(j):
        return tgt_wide[...] == (column + (starts[j // 4] + j % 4 * 128)).astype(F32)

    exps = jnp.zeros((512, 128), F32)
    hits = jnp.zeros((512, 128), F32)
    for j in range(8):
        logit = raw[:, j * 128 : (j + 1) * 128] * scale_wide[...]
        exps = exps + jnp.exp(logit)
        hits = hits + jnp.where(is_hit(j), logit, 0.0)
    tile, sums = r.tile, r.sums
    for i, row in enumerate(lanes(exps) + lanes(hits)):
        tile[i : i + 1] = row
    run(all_sum(copies, here, tile, r.group, r.line, sums))
    logs = jnp.log(sums[:4])
    for i in range(4):
        log_wide[i * 128 : (i + 1) * 128] = spread(logs[i : i + 1])
    grad, grad_t = r.grad, r.grad_t

    def wide_of(j):
        term = raw[:, j * 128 : (j + 1) * 128]
        prob = jnp.exp(term * scale_wide[...] - log_wide[...])
        return mask_wide[...] * (prob - is_hit(j).astype(F32)), term

    for j in range(8):
        grad[:, j * 128 : (j + 1) * 128] = wide_of(j)[0].astype(BF16)
    late = []

    def beside():
        each = logs - sums[4:]
        lost = sum(
            jnp.sum(mask_rows[i] * each[i : i + 1], axis=1, keepdims=True) for i in range(4)
        )
        loss_part = r.loss
        loss_part[core] = jnp.broadcast_to(lost, (8, 128))
        late.append(copies.go(loss_part.at[core], loss_part.at[core], here.sibling()))
        dots = jnp.zeros((512, 128), F32)
        for j in range(8):
            wide, term = wide_of(j)
            dots = dots + wide.astype(BF16).astype(F32) * term
            grad_t[j * 128 : (j + 1) * 128] = (wide * scale_wide[...]).T.astype(BF16)
        dot_tile = r.dot_tile
        for i, row in enumerate(lanes(dots)):
            dot_tile[i : i + 1] = row
            dot_tile[i + 4 : i + 5] = row
        late.append(copies.go(grad_t.at[pl.ds(512, 512)], lgr_sib, here.sibling()))

    terms, whole = r.terms, r.whole

    def half_lines(ref, h):
        index = (slice(None),) * (len(ref.shape) - 2) + (pl.ds(h * 16, 16),)
        return ref.at[index]

    def part_rings(n, part):
        off, w, order = part
        order = order[::-1]
        axes = "yxz"
        cols = pl.ds(off, w)
        one, two, held = r.ones[n], r.twos[n], r.helds[n]
        out = r.outs[n * 2]

        def slab(i, h):
            index = tuple(i if a == order[0] else slice(None) for a in "yxz")
            lines = slice(None) if h is None else pl.ds(h * 16, 16)
            return terms.at[(*index, lines, cols)]

        yield from reduce_ring(copies, here, order[0], slab, half_lines, one, two, held, add_refs)
        add_refs(out, (slab(here.c[order[0]], None), two.at[0], two.at[1]))
        axes = axes.replace(order[0], "")
        last = r.outs[n * 2 + 1]

        def second(i):
            return out.at[tuple(i if a == order[1] else slice(None) for a in axes)]

        yield from reduce_near(
            copies, here, order[1], second, r.threes[n * 2],
            lambda own, others: add_refs(last, (own, *others)),
        )

        def third(own, others):
            total = own[...].astype(F32)
            for other in others:
                total = total + other[...].astype(F32)
            whole[:, off : off + w] = total

        yield from reduce_near(
            copies, here, order[2], lambda i: last.at[i], r.threes[n * 2 + 1], third
        )

    def product(off, w):

        @pl.loop(0, 4)
        def _(j):
            terms[j, :, :, :, off : off + w] = (
                jnp.dot(
                    grad[...], head[:, pl.ds(pl.multiple_of(j * 1792 + off, 128), w)],
                    preferred_element_type=F32,
                )
                .astype(BF16)
                .reshape(4, 4, 32, w)
            )

    swap_rows = []

    def row_piece(j):
        swap_rows.append(copies.go(rows.at[j], rows_sib.at[j], here.sibling()))

    rings = [part_rings(n, part) for n, part in enumerate(PARTS)]
    for n in range(3):
        product(*PARTS[n][:2])
        advance(rings[n : n + 1])
    product(*BATCHES[1])
    advance(rings[3:])
    beside()
    row_dots = all_sum(copies, here, r.dot_tile, r.group2, r.line2, r.sums2)

    def half_head(j):
        lanes_ = pl.ds(j * 1792, 1792)
        head[:512, lanes_] = jnp.dot(
            grad_t[:512], rows[j].reshape(512, 1792), preferred_element_type=F32
        ).astype(BF16)
        bring(head.at[pl.ds(0, 512), lanes_], half_out.at[:, lanes_])

    run(
        *rings,
        row_dots,
        trickle([lambda j=j: row_piece(j) for j in range(4)]),
        trickle([lambda j=j: half_head(j) for j in range(4)]),
    )

    back, backs = r.back, r.backs
    for i in range(4):
        back[i] = whole[:, i * 448 : (i + 1) * 448]
    exchange = []
    for o in range(1, 4):
        to = lax.rem(z + o, 4)
        exchange.append(copies.go(back.at[to], backs.at[z], here.along("z", o)))
    backs[z] = back[z]
    row_scale = scale_wide[pl.ds(pl.multiple_of(x * 128, 128), 128)][:, :1]
    row_dot = spread(r.sums2[pl.ds(x, 1)])[:, :1]
    wide = r.projected[...]
    for copy in exchange:
        copy.wait_recv()
    normed_grad = backs[...].reshape(128, 448)
    grad_out = row_scale * (normed_grad * gain[...]) - wide * (
        row_scale * row_scale * row_scale
    ) * (row_dot / width)
    proj_grad[x, core] = grad_out.astype(BF16)

    def share():
        def at(i):
            return proj_grad.at[i, core]

        def pass_on(i):
            return copies.go(at(i), at(i), here.sibling())

        ins = [copies.go(at(x), at(x), here.along("x", o)) for o in (1, 2, 3)]
        passed = [pass_on(x)]
        yield
        for o in (1, 3, 2):
            ins[o - 1].wait_recv()
            passed.append(pass_on(lax.rem(x + 4 - o, 4)))
        for copy in passed:
            copy.wait_recv()

    def gain_sum():
        mine, every = r.gain_mine, r.gain_all
        mine[...] = jnp.broadcast_to(
            jnp.sum(normed_grad * wide * row_scale, axis=0, keepdims=True), (8, 448)
        )
        every[here.ctx] = mine[...]
        ins = [copies.go(mine, every.at[here.ctx], here.ctx_peer(o)) for o in range(1, 8)]
        yield
        yield
        for copy in ins:
            copy.wait_recv()
        gain_grad[...] = jnp.sum(every[...], axis=0)[:1]

    run(share(), gain_sum())
    for copy in (*swap_rows, *late):
        copy.wait_recv()
    loss[...] = (r.loss[0, :1, :1] + r.loss[1, :1, :1]) / 1024.0
    for copy in locals_[5:]:
        copy.wait()
    copies.finish()


BACK_BATCHES = ((0, 512), (512, 384))


def back_kernel(
    proj_grad, proj_h, proj_e, cols, hidden, embed, gain_h, gain_e, head_half, rows_sib, lgr_sib,
    grad_h, grad_e, gain_grad_h, gain_grad_e, grad_proj_h, grad_proj_e, grad_head,
    r, send, recv, send_far, recv_far, local_sem, out_sem,
):
    r = Bag(r)
    here = Place()
    copies = Copies(send, recv)
    y, z, v, ctx, core = here.c["y"], here.c["z"], here.v, here.ctx, here.core
    width = 7168
    friends = (
        [here.v_peer(o) for o in range(1, 16)]
        + [here.ctx_peer(o) for o in range(1, 8)]
        + [here.at(ctx=v // 2, v=source) for source in range(16)]
    )
    greet(friends)
    locals_ = []

    def bring(src, dst):
        copy = pltpu.make_async_copy(src, dst, local_sem.at[len(locals_)])
        copy.start()
        locals_.append(copy)
        return copy

    weights = [bring(proj_h, r.weights.at[0]), bring(proj_e, r.weights.at[1])]
    cols_in = bring(cols, r.cols)
    inputs = [bring(hidden, r.inputs.at[0]), bring(embed, r.inputs.at[1])]
    lgr_in = bring(lgr_sib, r.lgr)
    rows_in = []
    for j in range(4):
        rows_in.append(
            [
                bring(head_half.at[:, pl.ds(j * 1792, 1792)], r.halves.at[j]),
                bring(rows_sib.at[j], r.rows.at[j]),
            ]
        )
    for copy in weights:
        copy.wait()

    first_at, second_at = jnp.where(core == 0, y, z), jnp.where(core == 0, z, y)

    def near(second, step):
        along_y, along_z = here.along("y", step)["vocab"], here.along("z", step)["vocab"]
        pick = (core == 0) if not second else (core == 1)
        return here.at(v=jnp.where(pick, along_y, along_z))

    ring_first = (first_at, near(False, 1), near(False, -1))
    ring_second = (second_at, [near(True, o) for o in (1, 2, 3)])
    terms, summed, flat = r.terms, r.summed, r.flat

    def fill(batch):
        off, w = BACK_BATCHES[batch]
        for e in range(2):
            back = jnp.dot(
                proj_grad[...], r.weights[e, :, off : off + w], preferred_element_type=F32
            ).astype(BF16)
            flat[e, :, off : off + w] = back
            back = back.reshape(8, 8, 16, w)
            for j in range(8):
                at_y, at_z = e * 2 + j // 4, j % 4
                p = jnp.where(core == 0, at_y, at_z)
                q = jnp.where(core == 0, at_z, at_y)
                terms[p, q, :, :, off : off + w] = back[:, j]

    def back_ring(batch):
        off, w = BACK_BATCHES[batch]
        lanes_ = pl.ds(off, w)

        def span(h):
            return slice(None) if h is None else pl.ds(h * 4, 4)

        one, two, held, out, three = r.rings[batch]

        def big(i, h):
            return terms.at[i, :, span(h), :, lanes_]

        yield from reduce_ring(
            copies, here, ring_first, big, lambda ref, h: ref.at[:, span(h)], one, two, held, add_refs
        )
        add_refs(out, (big(first_at, None), two.at[0], two.at[1]))

        def end(own, others):
            for c in range(8):
                total = own[c].astype(F32)
                for other in others:
                    total = total + other[c].astype(F32)
                summed[c, :, off : off + w] = total

        yield from reduce_near(copies, here, ring_second, lambda i: out.at[i], three, end)

    outs = []

    def head_part(j):
        for copy in rows_in[j]:
            copy.wait()
        slot = j % 2
        if j >= 2:
            outs[j - 2].wait()
        r.stage[slot] = (
            jnp.dot(r.lgr[...], r.rows[j].reshape(512, 1792), preferred_element_type=F32)
            + r.halves[j].astype(F32)
        ).astype(BF16)
        copy = pltpu.make_async_copy(
            r.stage.at[slot], grad_head.at[:, pl.ds(j * 1792, 1792)], out_sem.at[j]
        )
        copy.start()
        outs.append(copy)

    def proj_part(e):
        out = (grad_proj_h, grad_proj_e)[e]
        out[...] = jnp.dot(
            r.turned[...], r.cols[e].reshape(1024, 896), preferred_element_type=F32
        ).astype(BF16)

    mine_dot, dots, dot_rows, dot_in = r.mine_dot, r.dots, r.dot_rows, r.dot_in

    def inner():
        for e in range(2):
            acc = jnp.zeros((1024, 128), F32)
            for c in range(7):
                part = slice(c * 128, (c + 1) * 128)
                cols_part = r.cols[e, :, :, :, :, :, part].reshape(1024, 128).astype(F32)
                acc = acc + flat[e, :, part].astype(F32) * cols_part
            for c in range(8):
                row = jnp.sum(acc[c * 128 : (c + 1) * 128].T, axis=0, keepdims=True)
                mine_dot[e, c : c + 1] = row
        ins = [copies.go(mine_dot, dots.at[v], here.v_peer(o)) for o in range(1, 16)]
        dots[v] = mine_dot[...]
        yield
        for copy in ins:
            copy.wait_recv()
        total = jnp.sum(dots[...], axis=0)
        for c in range(8):
            for e in range(2):
                dot_rows[c, e : e + 1] = total[e, c : c + 1]
        ins = [
            copies.go(dot_rows.at[lax.rem(ctx + o, 8)], dot_in.at[ctx], here.ctx_peer(o))
            for o in range(1, 8)
        ]
        dot_in[ctx] = dot_rows[ctx]
        yield
        for copy in ins:
            copy.wait_recv()

    rings = [back_ring(0), back_ring(1)]
    dotting = inner()
    fill(0)
    met(friends)
    next(rings[0])
    fill(1)
    next(rings[1])
    dot_rows[...] = jnp.zeros_like(dot_rows)
    cols_in.wait()
    next(dotting)
    next(rings[0])
    r.turned[...] = proj_grad[...].astype(F32).T.astype(BF16)
    proj_part(0)
    next(rings[1])
    lgr_in.wait()
    head_part(0)
    head_part(1)
    next(rings[0])
    next(dotting)
    next(rings[1])
    proj_part(1)
    next(rings[0], None)
    next(rings[1], None)
    next(dotting, None)

    sent_gain, got_gain = r.sent_gain, r.got_gain
    gain_acc = jnp.zeros((1, 896), F32)
    for c in range(8):
        gain_acc = gain_acc + jnp.sum(
            summed[c] * r.cols[y // 2, c // 2, c % 2, y % 2, z].astype(F32), axis=0, keepdims=True
        )
    sent_gain[0] = gain_acc[:, :448]
    sent_gain[1] = gain_acc[:, 448:]

    @pl.loop(0, 8)
    def _(c):
        r.sent[0, c] = summed[c][:, :448].astype(BF16)
        r.sent[1, c] = summed[c][:, 448:].astype(BF16)

    sent, got = r.sent, r.got

    def far_copy(o, s):
        to = lax.rem(ctx + o, 8)
        return pltpu.make_async_remote_copy(
            src_ref=sent.at[s, to],
            dst_ref=got.at[v // 8, pl.ds(pl.multiple_of(lax.rem(v, 8) * 16, 16), 16)],
            send_sem=send_far.at[o * 2 + s],
            recv_sem=recv_far.at[v],
            device_id=here.at(ctx=to, v=ctx * 2 + s),
            device_id_type=MESH,
        )

    def far_gain(o, s):
        return pltpu.make_async_remote_copy(
            src_ref=sent_gain.at[s],
            dst_ref=got_gain.at[v],
            send_sem=send_far.at[16 + o * 2 + s],
            recv_sem=recv_far.at[16 + v],
            device_id=here.at(ctx=lax.rem(ctx + o, 8), v=ctx * 2 + s),
            device_id_type=MESH,
        )

    for o in range(8):
        for s in range(2):
            if o:
                far_copy(o, s).start()
                far_gain(o, s).start()
            else:

                @pl.when(v != ctx * 2 + s)
                def _(s=s):
                    far_copy(0, s).start()
                    far_gain(0, s).start()

                @pl.when(v == ctx * 2 + s)
                def _(s=s):
                    got_gain[v] = sent_gain[s]
                    got[v // 8, pl.ds(pl.multiple_of(lax.rem(v, 8) * 16, 16), 16)] = sent[s, ctx]

    for copy in inputs:
        copy.wait()
    odd = lax.rem(v, 2)
    window = pl.ds(pl.multiple_of(v // 2 * 896 + odd * 384, 128), 512)
    mine, gains, scales = r.mine, r.gains, r.scales
    for e, gain in enumerate((gain_h, gain_e)):
        squares = jnp.zeros((128, 128), F32)
        for c in range(56):
            part = r.inputs[e, :, c * 128 : (c + 1) * 128].astype(F32)
            squares = squares + part * part
        scales[e] = jnp.broadcast_to(
            lax.rsqrt(jnp.sum(squares, axis=1, keepdims=True) / width + EPSILON), (128, 128)
        )

        @pl.when(odd == 0)
        def _(e=e, gain=gain):
            mine[e] = r.inputs[e, :, window][:, :448].astype(F32)
            gains[e] = gain[:, window][:, :448]

        @pl.when(odd == 1)
        def _(e=e, gain=gain):
            mine[e] = r.inputs[e, :, window].astype(F32)[:, 64:]
            gains[e] = gain[:, window][:, 64:]

    head_part(2)
    head_part(3)
    for source in range(16):

        @pl.when(jnp.logical_or(ctx != v // 2, v != source))
        def _(source=source):
            pltpu.make_async_remote_copy(
                src_ref=sent.at[0, 0],
                dst_ref=got.at[source // 8, pl.ds(source % 8 * 16, 16)],
                send_sem=send_far.at[0],
                recv_sem=recv_far.at[source],
                device_id=here.at(ctx=lax.rem(ctx + 1, 8)),
                device_id_type=MESH,
            ).wait_recv()
            pltpu.make_async_remote_copy(
                src_ref=sent_gain.at[0],
                dst_ref=got_gain.at[source],
                send_sem=send_far.at[0],
                recv_sem=recv_far.at[16 + source],
                device_id=here.at(ctx=lax.rem(ctx + 1, 8)),
                device_id_type=MESH,
            ).wait_recv()

    dot_sum = jnp.sum(dot_in[...], axis=0).T
    for e, (out, gain_out) in enumerate(((grad_h, gain_grad_h), (grad_e, gain_grad_e))):
        back = got[e].astype(F32)
        scale = scales[e][:, :1]
        dot = dot_sum[:, e : e + 1]
        grad = scale * (back * gains[e]) - mine[e] * (scale * scale) * (dot / width)
        out[...] = grad.T.astype(BF16)
        gain_out[...] = jnp.sum(got_gain[e * 8 : e * 8 + 8], axis=0) / gains[e]
    for o in range(8):
        for s in range(2):
            if o:
                far_copy(o, s).wait_send()
                far_gain(o, s).wait_send()
            else:

                @pl.when(v != ctx * 2 + s)
                def _(s=s):
                    far_copy(0, s).wait_send()
                    far_gain(0, s).wait_send()

    for copy in outs[2:]:
        copy.wait()
    copies.finish()


def place_kernel(*refs):
    ins, outs, buffers, sem_in, sem_out = refs[:9], refs[9:18], refs[18:23], refs[23], refs[24]
    moves = [(ins[4 + i], buffers[i], outs[4 + i]) for i in range(4)]
    for i in range(8):
        lines = pl.ds(i * 64, 64)
        moves.append((ins[8].at[lines], buffers[4].at[lines], outs[8].at[lines]))
    loads = [pltpu.make_async_copy(a, b, sem_in.at[n]) for n, (a, b, _) in enumerate(moves)]
    stores = [pltpu.make_async_copy(b, c, sem_out.at[n]) for n, (_, b, c) in enumerate(moves)]
    for load in loads:
        load.start()
    for value, out in zip(ins[:4], outs[:4]):
        out[...] = value[...]
    for load, store in zip(loads, stores):
        load.wait()
        store.start()
    for store in stores:
        store.wait()


def back_scratch():
    scratch = dict(
        weights=pltpu.VMEM((2, 448, 896), BF16),
        cols=pltpu.VMEM((2, 4, 2, 2, 4, 16, 896), BF16),
        inputs=pltpu.VMEM((2, 128, 7168), BF16),
        lgr=pltpu.VMEM((512, 512), BF16),
        rows=pltpu.VMEM((4, 4, 4, 32, 1792), BF16),
        halves=pltpu.VMEM((4, 512, 1792), BF16),
        terms=pltpu.VMEM((4, 4, 8, 16, 896), BF16),
        summed=pltpu.VMEM((8, 16, 896), F32),
        stage=pltpu.VMEM((2, 512, 1792), BF16),
        turned=pltpu.VMEM((448, 1024), BF16),
        sent=pltpu.VMEM((2, 8, 16, 448), BF16),
        got=pltpu.VMEM((2, 128, 448), BF16),
        mine=pltpu.VMEM((2, 128, 448), F32),
        gains=pltpu.VMEM((2, 1, 448), F32),
        scales=pltpu.VMEM((2, 128, 128), F32),
        mine_dot=pltpu.VMEM((2, 8, 128), F32),
        dots=pltpu.VMEM((16, 2, 8, 128), F32),
        dot_rows=pltpu.VMEM((8, 8, 128), F32),
        dot_in=pltpu.VMEM((8, 8, 128), F32),
        sent_gain=pltpu.VMEM((2, 1, 448), F32),
        got_gain=pltpu.VMEM((16, 1, 448), F32),
        flat=pltpu.VMEM((2, 1024, 896), BF16),
        rings=[],
    )
    for n, (_, w) in enumerate(BACK_BATCHES):
        scratch["rings"].append(
            [
                pltpu.VMEM((2, 4, 4, 16, w), BF16),
                pltpu.VMEM((2, 4, 8, 16, w), BF16),
                pltpu.VMEM((2, 4, 4, 16, w), BF16),
                pltpu.VMEM((4, 8, 16, w), BF16),
                pltpu.VMEM((3, 8, 16, w), BF16),
            ]
        )
    return scratch


def params(number, limit=56):
    return pltpu.CompilerParams(
        collective_id=number, has_side_effects=True, vmem_limit_bytes=limit * 2**20
    )


def sems(n):
    return [pltpu.SemaphoreType.DMA((n,)), pltpu.SemaphoreType.DMA((n,))]


def shape(dims, kind):
    return jax.ShapeDtypeStruct(dims, kind)


def middle_scratch():
    scratch = dict(
        head=pltpu.VMEM((1024, 7168), BF16),
        rows=pltpu.VMEM((4, 4, 4, 32, 1792), BF16),
        terms=pltpu.VMEM((4, 4, 4, 32, 1792), BF16),
        raw=pltpu.VMEM((512, 1024), F32),
        grad=pltpu.VMEM((512, 1024), BF16),
        grad_t=pltpu.VMEM((1024, 512), BF16),
        scale_wide=pltpu.VMEM((512, 128), F32),
        log_wide=pltpu.VMEM((512, 128), F32),
        cols=pltpu.VMEM((2, 4, 2, 2, 4, 16, 896), BF16),
        raw_in=pltpu.VMEM((2, 16, 7168), BF16),
        normed=pltpu.VMEM((8, 16, 896), BF16),
        weights=pltpu.VMEM((2, 448, 896), BF16),
        loss=pltpu.VMEM((2, 8, 128), F32),
        tgt_wide=pltpu.VMEM((512, 128), F32),
        mask_wide=pltpu.VMEM((512, 128), F32),
        away=pltpu.VMEM((4, 128, 448), F32),
        sib=pltpu.VMEM((4, 128, 448), F32),
        summed=pltpu.VMEM((4, 128, 448), F32),
        summed_out=pltpu.VMEM((4, 128, 448), BF16),
        three=pltpu.VMEM((3, 128, 448), BF16),
        projected=pltpu.VMEM((128, 448), F32),
        square=pltpu.VMEM((8, 128), F32),
        squares=pltpu.VMEM((16, 8, 128), F32),
        scales=pltpu.VMEM((4, 8, 128), F32),
        piece=pltpu.VMEM((4, 32, 448), BF16),
        pieces=pltpu.VMEM((4, 32, 448), BF16),
        back=pltpu.VMEM((4, 32, 448), F32),
        backs=pltpu.VMEM((4, 32, 448), F32),
        whole=pltpu.VMEM((32, 1792), F32),
        gain_mine=pltpu.VMEM((8, 448), F32),
        gain_all=pltpu.VMEM((8, 8, 448), F32),
        tile=pltpu.VMEM((8, 128), F32),
        sums=pltpu.VMEM((8, 128), F32),
        dot_tile=pltpu.VMEM((8, 128), F32),
        sums2=pltpu.VMEM((8, 128), F32),
        group=pltpu.VMEM((16, 8, 128), F32),
        group2=pltpu.VMEM((16, 8, 128), F32),
        line=pltpu.VMEM((4, 8, 128), F32),
        line2=pltpu.VMEM((4, 8, 128), F32),
        ones=[],
        threes=[],
        twos=[],
        helds=[],
        outs=[],
    )
    for _, w, _ in PARTS:
        scratch["ones"].append(pltpu.VMEM((2, 4, 4, 16, w), BF16))
        scratch["helds"].append(pltpu.VMEM((2, 4, 4, 16, w), BF16))
        scratch["twos"].append(pltpu.VMEM((2, 4, 4, 32, w), BF16))
        scratch["outs"] += [pltpu.VMEM((4, 4, 32, w), BF16), pltpu.VMEM((4, 32, w), BF16)]
        scratch["threes"] += [pltpu.VMEM((3, 4, 32, w), BF16), pltpu.VMEM((3, 32, w), BF16)]
    return scratch


def contract_last(left, right):
    return lax.dot_general(
        left, right, (((1,), (1,)), ((), ())), preferred_element_type=F32
    )


def local(
    hidden_state, embedded_next, gain_hidden, gain_embed, proj_hidden, proj_embed,
    final_gain, head, targets, loss_mask,
):
    proj_grad, gain_grad, loss, cols, head_half, rows_sib, lgr_sib = pl.pallas_call(
        middle_kernel,
        out_shape=[
            shape((4, 2, 128, 448), BF16), shape((1, 448), F32), shape((1, 1), F32),
            shape((2, 4, 2, 2, 4, 16, 896), BF16),
            shape(head.shape, BF16), shape((4, 4, 4, 32, 1792), BF16), shape((512, 512), BF16),
        ],
        in_specs=[ANY, ANY, VMEM, VMEM, ANY, ANY, VMEM, ANY, VMEM, VMEM],
        out_specs=[VMEM, VMEM, VMEM, ANY, ANY, ANY, ANY],
        scratch_shapes=[middle_scratch()] + sems(360) + [pltpu.SemaphoreType.DMA((10,))],
        compiler_params=params(2, 61),
        name="middle",
    )(
        hidden_state, embedded_next, gain_hidden[None, :], gain_embed[None, :],
        proj_hidden.T, proj_embed.T, final_gain[None, :], head,
        targets.reshape(8, 128), loss_mask.reshape(8, 128),
    )
    grad_h, grad_e, gain_grad_h, gain_grad_e, grad_proj_h, grad_proj_e, grad_head = pl.pallas_call(
        back_kernel,
        out_shape=[
            shape((448, 128), BF16), shape((448, 128), BF16), shape((1, 448), F32), shape((1, 448), F32),
            shape((448, 896), BF16), shape((448, 896), BF16), shape(head.shape, BF16),
        ],
        in_specs=[VMEM, ANY, ANY, ANY, ANY, ANY, VMEM, VMEM, ANY, ANY, ANY],
        out_specs=[VMEM] * 6 + [ANY],
        scratch_shapes=[back_scratch()]
        + sems(46)
        + sems(32)
        + [pltpu.SemaphoreType.DMA((15,)), pltpu.SemaphoreType.DMA((4,))],
        compiler_params=params(5, 58),
        name="back",
    )(
        proj_grad.reshape(1024, 448), proj_hidden.T, proj_embed.T, cols, hidden_state, embedded_next,
        gain_hidden[None, :], gain_embed[None, :], head_half, rows_sib, lgr_sib,
    )
    values = [
        loss, gain_grad_h, gain_grad_e, gain_grad, grad_h, grad_e, grad_proj_h, grad_proj_e, grad_head,
    ]
    specs = [VMEM] * 4 + [ANY] * 5
    loss, gain_grad_h, gain_grad_e, gain_grad, grad_h, grad_e, grad_proj_h, grad_proj_e, grad_head = (
        pl.pallas_call(
            place_kernel,
            out_shape=[shape(value.shape, value.dtype) for value in values],
            in_specs=specs,
            out_specs=specs,
            scratch_shapes=[pltpu.VMEM(value.shape, value.dtype) for value in values[4:]]
            + [pltpu.SemaphoreType.DMA((12,)), pltpu.SemaphoreType.DMA((12,))],
            compiler_params=pltpu.CompilerParams(vmem_limit_bytes=60 * 2**20),
            name="place",
        )(*values)
    )
    return (
        loss[0, 0], grad_h.T, grad_e.T, gain_grad_h[0], gain_grad_e[0],
        grad_proj_h.T, grad_proj_e.T, gain_grad[0], grad_head,
    )


def solution(mesh):
    in_specs = (
        P("ctx", None), P("ctx", None), P(), P(), P("ctx", "vocab"), P("ctx", "vocab"),
        P("vocab"), P(("ctx", "vocab"), None), P(), P(),
    )
    out_specs = (
        P(), P("ctx", "vocab"), P("ctx", "vocab"), P("vocab"), P("vocab"),
        P("ctx", "vocab"), P("ctx", "vocab"), P("vocab"), P(("ctx", "vocab"), None),
    )
    return jax.shard_map(local, mesh=mesh, in_specs=in_specs, out_specs=out_specs, check_vma=False)
```

```python
import jax
import jax.numpy as jnp
from jax import lax
from jax.experimental import pallas as pl
from jax.experimental.pallas import tpu as pltpu
from jax.sharding import PartitionSpec as P

EPSILON = 1e-06
MESH = pl.DeviceIdType.MESH
VMEM = pl.BlockSpec(memory_space=pltpu.VMEM)
ANY = pl.BlockSpec(memory_space=pl.ANY)
F32 = jnp.float32
BF16 = jnp.bfloat16
PARTS = (
    (0, 384, "xyz"),
    (384, 384, "yzx"),
    (768, 256, "zxy"),
    (1024, 256, "xyz"),
    (1280, 256, "yzx"),
    (1536, 256, "zxy"),
)
BATCHES = ((0, 1024), (1024, 768))
SHARED = 640


class Place:
    def __init__(self):
        self.ctx = lax.axis_index("ctx")
        self.v = lax.axis_index("vocab")
        self.c = {"x": self.ctx // 2, "y": self.v // 4, "z": self.v % 4}
        self.core = self.ctx % 2

    def at(self, ctx=None, v=None):
        return {"ctx": self.ctx if ctx is None else ctx, "vocab": self.v if v is None else v}

    def along(self, axis, step):
        i = lax.rem(self.c[axis] + step + 4, 4)
        if axis == "x":
            return self.at(ctx=i * 2 + self.core)
        if axis == "y":
            return self.at(v=i * 4 + self.c["z"])
        return self.at(v=self.c["y"] * 4 + i)

    def sibling(self):
        return self.at(ctx=self.c["x"] * 2 + 1 - self.core)

    def ctx_peer(self, o):
        return self.at(ctx=lax.rem(self.ctx + o, 8))

    def v_peer(self, o):
        return self.at(v=lax.rem(self.v + o, 16))


class Copies:
    def __init__(self, send, recv):
        self.send, self.recv, self.count, self.started = send, recv, 0, []

    def go(self, src, dst, device):
        assert self.count < self.send.shape[0]
        copy = pltpu.make_async_remote_copy(
            src_ref=src,
            dst_ref=dst,
            send_sem=self.send.at[self.count],
            recv_sem=self.recv.at[self.count],
            device_id=device,
            device_id_type=MESH,
        )
        self.count += 1
        copy.start()
        self.started.append(copy)
        return copy

    def finish(self):
        for copy in self.started:
            copy.wait_send()
        self.started = []


def greet(devices):
    barrier = pltpu.get_barrier_semaphore()
    for device in devices:
        pl.semaphore_signal(barrier, inc=1, device_id=device, device_id_type=MESH)


def met(devices):
    pl.semaphore_wait(pltpu.get_barrier_semaphore(), len(devices))


def run(*rings):
    rings = list(rings)
    while rings:
        left = []
        for ring in rings:
            try:
                next(ring)
                left.append(ring)
            except StopIteration:
                pass
        rings = left


def chain(*makers):
    for maker in makers:
        yield from maker()


def gather_ring(copies, here, axis, slab):
    me = here.c[axis]
    right, left = here.along(axis, 1), here.along(axis, -1)
    before, after = lax.rem(me + 3, 4), lax.rem(me + 1, 4)

    def send(i, h, device):
        return copies.go(slab(i, h), slab(i, h), device)

    right_0, left_1 = send(me, 0, right), send(me, 1, left)
    right_1, left_0 = send(me, 1, right), send(me, 0, left)
    yield
    right_0.wait_recv()
    far_a = send(before, 0, right)
    left_1.wait_recv()
    far_b = send(after, 1, left)
    yield
    for copy in (right_1, left_0, far_a, far_b):
        copy.wait_recv()


def gather_near(copies, here, axis, slab):
    me = here.c[axis]
    ins = [copies.go(slab(me, None), slab(me, None), here.along(axis, o)) for o in (1, 2, 3)]
    yield
    for copy in ins:
        copy.wait_recv()


def reduce_ring(copies, here, axis, slab, half, one, two, held, add):
    if isinstance(axis, str):
        me, right, left = here.c[axis], here.along(axis, 1), here.along(axis, -1)
    else:
        me, right, left = axis
    before, after, far = lax.rem(me + 3, 4), lax.rem(me + 1, 4), lax.rem(me + 2, 4)
    a1 = copies.go(slab(far, 0), one.at[0], right)
    b1 = copies.go(slab(far, 1), one.at[1], left)
    a2 = copies.go(slab(after, 1), half(two.at[0], 1), right)
    b2 = copies.go(slab(before, 0), half(two.at[1], 0), left)
    yield
    a1.wait_recv()
    add(held.at[0], (slab(after, 0), one.at[0]))
    a3 = copies.go(held.at[0], half(two.at[0], 0), right)
    b1.wait_recv()
    add(held.at[1], (slab(before, 1), one.at[1]))
    b3 = copies.go(held.at[1], half(two.at[1], 1), left)
    yield
    a2.wait_recv()
    b2.wait_recv()
    a3.wait_recv()
    b3.wait_recv()


def reduce_near(copies, here, axis, slab, recv, finish):
    if isinstance(axis, str):
        me, to = here.c[axis], [here.along(axis, o) for o in (1, 2, 3)]
    else:
        me, to = axis
    ins = [
        copies.go(slab(lax.rem(me + o, 4)), recv.at[o - 1], to[o - 1]) for o in (1, 2, 3)
    ]
    yield
    for copy in ins:
        copy.wait_recv()
    finish(slab(me), [recv.at[o] for o in range(3)])


def add_refs(out, terms):
    lead = out.shape[:-2]
    total = 1
    for n in lead:
        total *= n

    def block(index):
        acc = terms[0][index].astype(F32)
        for term in terms[1:]:
            acc = acc + term[index].astype(F32)
        out[index] = acc.astype(out.dtype)

    if total == 1:
        block(tuple(0 for _ in lead) + (slice(None), slice(None)))
        return

    @pl.loop(0, total)
    def _(i):
        index = []
        for n in reversed(lead):
            index.append(i % n)
            i = i // n
        block(tuple(reversed(index)) + (slice(None), slice(None)))


def all_sum(copies, here, tile, group, line, out):
    group[here.v] = tile[...]
    ins = [copies.go(tile, group.at[here.v], here.v_peer(o)) for o in range(1, 16)]
    yield
    for copy in ins:
        copy.wait_recv()
    x = here.c["x"]
    line[x] = jnp.sum(group[...], axis=0)
    ins = [copies.go(line.at[x], line.at[x], here.along("x", o)) for o in (1, 2, 3)]
    yield
    for copy in ins:
        copy.wait_recv()
    out[...] = jnp.sum(line[...], axis=0)


def spread(row):
    return jnp.broadcast_to(row, (128, 128)).T


def lanes(values):
    total = jnp.sum(values.T, axis=0, keepdims=True)
    return [total[:, i * 128 : (i + 1) * 128] for i in range(4)]


class Bag:
    def __init__(self, refs):
        self.__dict__.update(refs)


def trickle(pieces):
    for start in pieces:
        start()
        yield


def middle_kernel(
    hidden, embed, gain_h, gain_e, proj_h, proj_e, gain, head_own, targets, loss_mask,
    proj_grad, gain_grad, loss, cols_out, half_out, rows_sib, lgr_sib,
    r, send, recv, local_sem,
):
    r = Bag(r)
    here = Place()
    copies = Copies(send, recv)
    friends = [here.ctx_peer(o) for o in range(1, 8)] + [here.v_peer(o) for o in range(1, 16)]
    greet(friends)
    width = 7168
    x, y, z, core = here.c["x"], here.c["y"], here.c["z"], here.core
    head, rows, cols = r.head, r.rows, r.cols
    locals_ = []

    def bring(src, dst):
        copy = pltpu.make_async_copy(src, dst, local_sem.at[len(locals_)])
        copy.start()
        locals_.append(copy)
        return copy

    sliver = pl.ds(pl.multiple_of(lax.rem(here.v, 8) * 16, 16), 16)
    raw_in = [bring(hidden.at[sliver], r.raw_in.at[0]), bring(embed.at[sliver], r.raw_in.at[1])]
    wide_in = [bring(hidden, head.at[pl.ds(0, 128)]), bring(embed, head.at[pl.ds(128, 128)])]
    weights = [bring(proj_h, r.weights.at[0]), bring(proj_e, r.weights.at[1])]
    for copy in raw_in:
        copy.wait()
    first = here.v < 8
    normed = r.normed

    def norm(e, gains):
        wide = r.raw_in[e].astype(F32)
        scale = lax.rsqrt(jnp.mean(wide * wide, axis=-1, keepdims=True) + EPSILON)
        for c in range(8):
            part = slice(c * 896, c * 896 + SHARED)
            normed[c] = (wide[:, part] * scale * gains[:, part]).astype(BF16)

    @pl.when(first)
    def _():
        norm(0, gain_h)

    @pl.when(jnp.logical_not(first))
    def _():
        norm(1, gain_e)

    met(friends)

    def sliver_at(c):
        return cols.at[y // 2, c // 2, c % 2, y % 2, z, :, pl.ds(0, SHARED)]

    arrivals = []
    for o in range(1, 8):
        peer = lax.rem(here.ctx + o, 8)
        arrivals.append(copies.go(normed.at[peer], sliver_at(here.ctx), here.ctx_peer(o)))
    cols[y // 2, x, core, y % 2, z, :, :SHARED] = normed[here.ctx]

    for arrival in arrivals:
        arrival.wait_recv()

    def col_slabs(part):
        lanes_ = pl.ds(*part)

        def span(h):
            return slice(None) if h is None else pl.ds(h * 2, 2)

        return {
            "y_first": lambda i, h: cols.at[i // 2, span(h), :, i % 2, z, :, lanes_],
            "z_last": lambda i, h: cols.at[:, span(h), :, :, i, :, lanes_],
            "z_first": lambda i, h: cols.at[y // 2, span(h), :, y % 2, i, :, lanes_],
            "y_last": lambda i, h: cols.at[i // 2, span(h), :, i % 2, :, :, lanes_],
        }

    def col_ring(part, names):
        slabs = col_slabs(part)
        return chain(
            lambda: gather_near(copies, here, names[0][0], slabs[names[0]]),
            lambda: gather_ring(copies, here, names[1][0], slabs[names[1]]),
        )

    def straight_part():
        direct = r.direct
        for copy in wide_in:
            copy.wait()
        for e, gains in enumerate((gain_h, gain_e)):
            lines = slice(e * 128, (e + 1) * 128)
            squares = jnp.zeros((128, 128), F32)
            for c in range(56):
                part = head[lines, c * 128 : (c + 1) * 128].astype(F32)
                squares = squares + part * part
            scale = lax.rsqrt(jnp.sum(squares, axis=1, keepdims=True) / width + EPSILON)
            for c in range(8):
                part = slice(c * 896 + SHARED, (c + 1) * 896)
                direct[c, e] = (
                    (head[lines, part].astype(F32) * scale * gains[:, part])
                    .astype(BF16)
                    .reshape(2, 4, 16, 896 - SHARED)
                )

        straight = []
        for o in range(1, 8):
            peer = lax.rem(here.ctx + o, 8)
            straight.append(
                copies.go(
                    direct.at[peer],
                    cols.at[:, x, core, :, :, :, pl.ds(SHARED, 896 - SHARED)],
                    here.ctx_peer(o),
                )
            )
        cols[:, x, core, :, :, :, SHARED:] = direct[here.ctx]
        yield
        yield
        for copy in straight:
            copy.wait_recv()

    head_pieces = []

    def head_piece(i):
        piece_rows = pl.ds(i * 128, 128)
        head_pieces.append(
            copies.go(
                head_own.at[piece_rows], head.at[pl.ds(512 + i * 128, 128)], here.sibling()
            )
        )

    for i in range(4):
        head_piece(i)
    mark, kept = copies.count, copies.started
    copies.started = []

    @pl.when(core == 0)
    def _():
        run(*[col_ring(part, ("y_first", "z_last")) for part in ((0, 384), (384, 256))], straight_part())
        copies.finish()

    copies.count = mark

    @pl.when(core == 1)
    def _():
        run(*[col_ring(part, ("z_first", "y_last")) for part in ((0, 384), (384, 256))], straight_part())
        copies.finish()

    copies.started = kept
    loads = [bring(head_own.at[pl.ds(i * 128, 128)], head.at[pl.ds(i * 128, 128)]) for i in range(4)]
    for copy in weights:
        copy.wait()

    def project(k):
        return contract_last(cols[0, :, k].reshape(512, 896), r.weights[0]) + contract_last(
            cols[1, :, k].reshape(512, 896), r.weights[1]
        )

    r.away[...] = project(1 - core).reshape(4, 128, 448)
    swap = copies.go(r.away, r.sib, here.sibling())
    summed = r.summed
    summed[...] = project(core).reshape(4, 128, 448)
    bring(cols, cols_out)
    tgt_wide, mask_wide = r.tgt_wide, r.mask_wide
    mask_rows = []
    for i in range(4):
        at = pl.ds(i * 2 + core, 1)
        tgt_wide[i * 128 : (i + 1) * 128] = spread(targets[at].astype(F32))
        mask_row = loss_mask[at].astype(F32)
        mask_rows.append(mask_row)
        mask_wide[i * 128 : (i + 1) * 128] = spread(mask_row)
    swap.wait_recv()
    for i in range(4):
        summed[i] += r.sib[i]
        r.summed_out[i] = summed[i].astype(BF16)

    def add_x(own, others):
        del own
        total = summed[x]
        for other in others:
            total = total + other[...].astype(F32)
        r.projected[...] = total

    run(reduce_near(copies, here, "x", lambda i: r.summed_out.at[i], r.three, add_x))
    total = r.projected[...]
    piece, pieces = r.piece, r.pieces
    piece[...] = (total * gain[...]).astype(BF16).reshape(piece.shape)
    exchange = []
    for o in range(1, 4):
        to = lax.rem(z + o, 4)
        exchange.append(copies.go(piece.at[to], pieces.at[z], here.along("z", o)))
    pieces[z] = piece[z]
    r.square[...] = lax.dot_general(
        jnp.ones((8, total.shape[1]), F32), total * total, (((1,), (1,)), ((), ())),
        precision=lax.Precision.HIGHEST, preferred_element_type=F32,
    )
    squares, scales = r.squares, r.scales
    squares[here.v] = r.square[...]
    for copy in exchange:
        copy.wait_recv()
    for i in range(4):
        rows[y, x, z, :, i * 448 : (i + 1) * 448] = pieces[i]

    def stage(part, k):
        off, w, order = part

        def slab(i, h):
            index = []
            for a in "yxz":
                at = order.index(a)
                index.append(i if at == k else slice(None) if at < k else here.c[a])
            lines = slice(None) if h is None else pl.ds(h * 16, 16)
            return rows.at[(*index, lines, pl.ds(off, w))]

        ring = gather_near if k < 2 else gather_ring
        return lambda: ring(copies, here, order[k], slab)

    def scale():
        ins = [copies.go(r.square, squares.at[here.v], here.v_peer(o)) for o in range(1, 16)]
        yield
        yield
        for copy in ins:
            copy.wait_recv()
        scales[x] = lax.rsqrt(jnp.sum(squares[...], axis=0) / width + EPSILON)
        ins = [copies.go(scales.at[x], scales.at[x], here.along("x", o)) for o in range(1, 4)]
        yield
        yield
        for copy in ins:
            copy.wait_recv()

    raw = r.raw

    def logits_of(batch):
        off, w = BATCHES[batch]

        @pl.loop(0, 4)
        def _(j):
            term = lax.dot_general(
                rows[j, :, :, :, off : off + w].reshape(512, w),
                head[:, pl.ds(pl.multiple_of(j * 1792 + off, 128), w)],
                (((1,), (1,)), ((), ())), preferred_element_type=F32,
            )
            if batch:
                raw[...] += term
            else:

                @pl.when(j == 0)
                def _():
                    raw[...] = term

                @pl.when(j > 0)
                def _():
                    raw[...] += term

    gathers = [chain(*[stage(part, k) for k in range(3)]) for part in PARTS]
    leading, trailing, scaling = gathers[:3], gathers[3:], scale()

    def advance(group):
        alive = False
        for ring in group:
            try:
                next(ring)
                alive = True
            except StopIteration:
                pass
        return alive

    advance(leading)
    advance([scaling])
    alive = True
    while alive:
        alive = advance(leading)
        advance(trailing)
        advance([scaling])
    while advance([scaling]):
        pass
    for copy in loads:
        copy.wait()
    for copy in head_pieces:
        copy.wait_recv()
    logits_of(0)
    advance(trailing)
    logits_of(1)

    scale_wide, log_wide = r.scale_wide, r.log_wide
    for i in range(4):
        scale_wide[i * 128 : (i + 1) * 128] = spread(scales[i, :1])
    column = lax.broadcasted_iota(jnp.int32, (512, 128), 1)
    starts = [(here.ctx * 16 + here.v) * 512, ((here.ctx + 1 - 2 * core) * 16 + here.v) * 512]

    def is_hit(j):
        return tgt_wide[...] == (column + (starts[j // 4] + j % 4 * 128)).astype(F32)

    exps = jnp.zeros((512, 128), F32)
    hits = jnp.zeros((512, 128), F32)
    for j in range(8):
        logit = raw[:, j * 128 : (j + 1) * 128] * scale_wide[...]
        exps = exps + jnp.exp(logit)
        hits = hits + jnp.where(is_hit(j), logit, 0.0)
    tile, sums = r.tile, r.sums
    for i, row in enumerate(lanes(exps) + lanes(hits)):
        tile[i : i + 1] = row
    run(all_sum(copies, here, tile, r.group, r.line, sums))
    logs = jnp.log(sums[:4])
    for i in range(4):
        log_wide[i * 128 : (i + 1) * 128] = spread(logs[i : i + 1])
    grad, grad_t = r.grad, r.grad_t

    def wide_of(j):
        term = raw[:, j * 128 : (j + 1) * 128]
        prob = jnp.exp(term * scale_wide[...] - log_wide[...])
        return mask_wide[...] * (prob - is_hit(j).astype(F32)), term

    for j in range(8):
        grad[:, j * 128 : (j + 1) * 128] = wide_of(j)[0].astype(BF16)
    late = []

    def beside():
        each = logs - sums[4:]
        lost = sum(
            jnp.sum(mask_rows[i] * each[i : i + 1], axis=1, keepdims=True) for i in range(4)
        )
        loss_part = r.loss
        loss_part[core] = jnp.broadcast_to(lost, (8, 128))
        late.append(copies.go(loss_part.at[core], loss_part.at[core], here.sibling()))
        dots = jnp.zeros((512, 128), F32)
        for j in range(8):
            wide, term = wide_of(j)
            dots = dots + wide.astype(BF16).astype(F32) * term
            grad_t[j * 128 : (j + 1) * 128] = (wide * scale_wide[...]).T.astype(BF16)
        dot_tile = r.dot_tile
        for i, row in enumerate(lanes(dots)):
            dot_tile[i : i + 1] = row
            dot_tile[i + 4 : i + 5] = row
        late.append(copies.go(grad_t.at[pl.ds(512, 512)], lgr_sib, here.sibling()))

    terms, whole = r.terms, r.whole

    def half_lines(ref, h):
        index = (slice(None),) * (len(ref.shape) - 2) + (pl.ds(h * 16, 16),)
        return ref.at[index]

    def part_rings(n, part):
        off, w, order = part
        order = order[::-1]
        axes = "yxz"
        cols = pl.ds(off, w)
        one, two, held = r.ones[n], r.twos[n], r.helds[n]
        out = r.outs[n * 2]

        def slab(i, h):
            index = tuple(i if a == order[0] else slice(None) for a in "yxz")
            lines = slice(None) if h is None else pl.ds(h * 16, 16)
            return terms.at[(*index, lines, cols)]

        yield from reduce_ring(copies, here, order[0], slab, half_lines, one, two, held, add_refs)
        add_refs(out, (slab(here.c[order[0]], None), two.at[0], two.at[1]))
        axes = axes.replace(order[0], "")
        last = r.outs[n * 2 + 1]

        def second(i):
            return out.at[tuple(i if a == order[1] else slice(None) for a in axes)]

        yield from reduce_near(
            copies, here, order[1], second, r.threes[n * 2],
            lambda own, others: add_refs(last, (own, *others)),
        )

        def third(own, others):
            total = own[...].astype(F32)
            for other in others:
                total = total + other[...].astype(F32)
            whole[:, off : off + w] = total

        yield from reduce_near(
            copies, here, order[2], lambda i: last.at[i], r.threes[n * 2 + 1], third
        )

    def product(off, w):

        @pl.loop(0, 4)
        def _(j):
            terms[j, :, :, :, off : off + w] = (
                jnp.dot(
                    grad[...], head[:, pl.ds(pl.multiple_of(j * 1792 + off, 128), w)],
                    preferred_element_type=F32,
                )
                .astype(BF16)
                .reshape(4, 4, 32, w)
            )

    swap_rows = []

    def row_piece(j):
        swap_rows.append(copies.go(rows.at[j], rows_sib.at[j], here.sibling()))

    rings = [part_rings(n, part) for n, part in enumerate(PARTS)]
    for n in range(3):
        product(*PARTS[n][:2])
        advance(rings[n : n + 1])
    product(*BATCHES[1])
    advance(rings[3:])
    beside()
    row_dots = all_sum(copies, here, r.dot_tile, r.group2, r.line2, r.sums2)

    def half_head(j):
        lanes_ = pl.ds(j * 1792, 1792)
        head[:512, lanes_] = jnp.dot(
            grad_t[:512], rows[j].reshape(512, 1792), preferred_element_type=F32
        ).astype(BF16)
        bring(head.at[pl.ds(0, 512), lanes_], half_out.at[:, lanes_])

    run(
        *rings,
        row_dots,
        trickle([lambda j=j: row_piece(j) for j in range(4)]),
        trickle([lambda j=j: half_head(j) for j in range(4)]),
    )

    back, backs = r.back, r.backs
    for i in range(4):
        back[i] = whole[:, i * 448 : (i + 1) * 448]
    exchange = []
    for o in range(1, 4):
        to = lax.rem(z + o, 4)
        exchange.append(copies.go(back.at[to], backs.at[z], here.along("z", o)))
    backs[z] = back[z]
    row_scale = scale_wide[pl.ds(pl.multiple_of(x * 128, 128), 128)][:, :1]
    row_dot = spread(r.sums2[pl.ds(x, 1)])[:, :1]
    wide = r.projected[...]
    for copy in exchange:
        copy.wait_recv()
    normed_grad = backs[...].reshape(128, 448)
    grad_out = row_scale * (normed_grad * gain[...]) - wide * (
        row_scale * row_scale * row_scale
    ) * (row_dot / width)
    proj_grad[x, core] = grad_out.astype(BF16)

    def share():
        def at(i):
            return proj_grad.at[i, core]

        def pass_on(i):
            return copies.go(at(i), at(i), here.sibling())

        ins = [copies.go(at(x), at(x), here.along("x", o)) for o in (1, 2, 3)]
        passed = [pass_on(x)]
        yield
        for o in (1, 3, 2):
            ins[o - 1].wait_recv()
            passed.append(pass_on(lax.rem(x + 4 - o, 4)))
        for copy in passed:
            copy.wait_recv()

    def gain_sum():
        mine, every = r.gain_mine, r.gain_all
        mine[...] = jnp.broadcast_to(
            jnp.sum(normed_grad * wide * row_scale, axis=0, keepdims=True), (8, 448)
        )
        every[here.ctx] = mine[...]
        ins = [copies.go(mine, every.at[here.ctx], here.ctx_peer(o)) for o in range(1, 8)]
        yield
        yield
        for copy in ins:
            copy.wait_recv()
        gain_grad[...] = jnp.sum(every[...], axis=0)[:1]

    run(share(), gain_sum())
    for copy in (*swap_rows, *late):
        copy.wait_recv()
    loss[...] = (r.loss[0, :1, :1] + r.loss[1, :1, :1]) / 1024.0
    for copy in [copy for copy in locals_[6:] if not any(copy is one for one in loads)]:
        copy.wait()
    copies.finish()


BACK_BATCHES = ((0, 512), (512, 384))


def back_kernel(
    proj_grad, proj_h, proj_e, cols, hidden, embed, gain_h, gain_e, head_half, rows_sib, lgr_sib,
    grad_h, grad_e, gain_grad_h, gain_grad_e, grad_proj_h, grad_proj_e, grad_head,
    r, send, recv, send_far, recv_far, local_sem, out_sem,
):
    r = Bag(r)
    here = Place()
    copies = Copies(send, recv)
    y, z, v, ctx, core = here.c["y"], here.c["z"], here.v, here.ctx, here.core
    width = 7168
    friends = (
        [here.v_peer(o) for o in range(1, 16)]
        + [here.ctx_peer(o) for o in range(1, 8)]
        + [here.at(ctx=v // 2, v=source) for source in range(16)]
    )
    greet(friends)
    locals_ = []

    def bring(src, dst):
        copy = pltpu.make_async_copy(src, dst, local_sem.at[len(locals_)])
        copy.start()
        locals_.append(copy)
        return copy

    weights = [bring(proj_h, r.weights.at[0]), bring(proj_e, r.weights.at[1])]
    cols_in = bring(cols, r.cols)
    inputs = [bring(hidden, r.inputs.at[0]), bring(embed, r.inputs.at[1])]
    lgr_in = bring(lgr_sib, r.lgr)
    rows_in = []
    for j in range(4):
        rows_in.append(
            [
                bring(head_half.at[:, pl.ds(j * 1792, 1792)], r.halves.at[j]),
                bring(rows_sib.at[j], r.rows.at[j]),
            ]
        )
    for copy in weights:
        copy.wait()

    first_at, second_at = jnp.where(core == 0, y, z), jnp.where(core == 0, z, y)

    def near(second, step):
        along_y, along_z = here.along("y", step)["vocab"], here.along("z", step)["vocab"]
        pick = (core == 0) if not second else (core == 1)
        return here.at(v=jnp.where(pick, along_y, along_z))

    ring_first = (first_at, near(False, 1), near(False, -1))
    ring_second = (second_at, [near(True, o) for o in (1, 2, 3)])
    terms, summed, flat = r.terms, r.summed, r.flat

    def fill(batch):
        off, w = BACK_BATCHES[batch]
        for e in range(2):
            back = jnp.dot(
                proj_grad[...], r.weights[e, :, off : off + w], preferred_element_type=F32
            ).astype(BF16)
            flat[e, :, off : off + w] = back
            back = back.reshape(8, 8, 16, w)
            for j in range(8):
                at_y, at_z = e * 2 + j // 4, j % 4
                p = jnp.where(core == 0, at_y, at_z)
                q = jnp.where(core == 0, at_z, at_y)
                terms[p, q, :, :, off : off + w] = back[:, j]

    def back_ring(batch):
        off, w = BACK_BATCHES[batch]
        lanes_ = pl.ds(off, w)

        def span(h):
            return slice(None) if h is None else pl.ds(h * 4, 4)

        one, two, held, out, three = r.rings[batch]

        def big(i, h):
            return terms.at[i, :, span(h), :, lanes_]

        yield from reduce_ring(
            copies, here, ring_first, big, lambda ref, h: ref.at[:, span(h)], one, two, held, add_refs
        )
        add_refs(out, (big(first_at, None), two.at[0], two.at[1]))

        def end(own, others):
            for c in range(8):
                total = own[c].astype(F32)
                for other in others:
                    total = total + other[c].astype(F32)
                summed[c, :, off : off + w] = total

        yield from reduce_near(copies, here, ring_second, lambda i: out.at[i], three, end)

    outs = []

    def head_part(j):
        for copy in rows_in[j]:
            copy.wait()
        slot = j % 2
        if j >= 2:
            outs[j - 2].wait()
        r.stage[slot] = (
            jnp.dot(r.lgr[...], r.rows[j].reshape(512, 1792), preferred_element_type=F32)
            + r.halves[j].astype(F32)
        ).astype(BF16)
        copy = pltpu.make_async_copy(
            r.stage.at[slot], grad_head.at[:, pl.ds(j * 1792, 1792)], out_sem.at[j]
        )
        copy.start()
        outs.append(copy)

    def proj_part(e):
        out = (grad_proj_h, grad_proj_e)[e]
        out[...] = jnp.dot(
            r.turned[...], r.cols[e].reshape(1024, 896), preferred_element_type=F32
        ).astype(BF16)

    mine_dot, dots, dot_rows, dot_in = r.mine_dot, r.dots, r.dot_rows, r.dot_in

    def inner():
        for e in range(2):
            acc = jnp.zeros((1024, 128), F32)
            for c in range(7):
                part = slice(c * 128, (c + 1) * 128)
                cols_part = r.cols[e, :, :, :, :, :, part].reshape(1024, 128).astype(F32)
                acc = acc + flat[e, :, part].astype(F32) * cols_part
            for c in range(8):
                row = jnp.sum(acc[c * 128 : (c + 1) * 128].T, axis=0, keepdims=True)
                mine_dot[e, c : c + 1] = row
        ins = [copies.go(mine_dot, dots.at[v], here.v_peer(o)) for o in range(1, 16)]
        dots[v] = mine_dot[...]
        yield
        for copy in ins:
            copy.wait_recv()
        total = jnp.sum(dots[...], axis=0)
        for c in range(8):
            for e in range(2):
                dot_rows[c, e : e + 1] = total[e, c : c + 1]
        ins = [
            copies.go(dot_rows.at[lax.rem(ctx + o, 8)], dot_in.at[ctx], here.ctx_peer(o))
            for o in range(1, 8)
        ]
        dot_in[ctx] = dot_rows[ctx]
        yield
        for copy in ins:
            copy.wait_recv()

    rings = [back_ring(0), back_ring(1)]
    dotting = inner()
    fill(0)
    met(friends)
    next(rings[0])
    fill(1)
    next(rings[1])
    dot_rows[...] = jnp.zeros_like(dot_rows)
    cols_in.wait()
    next(dotting)
    next(rings[0])
    r.turned[...] = proj_grad[...].astype(F32).T.astype(BF16)
    proj_part(0)
    next(rings[1])
    lgr_in.wait()
    head_part(0)
    head_part(1)
    next(rings[0])
    next(dotting)
    next(rings[1])
    proj_part(1)
    next(rings[0], None)
    next(rings[1], None)
    next(dotting, None)

    sent_gain, got_gain = r.sent_gain, r.got_gain
    gain_acc = jnp.zeros((1, 896), F32)
    for c in range(8):
        gain_acc = gain_acc + jnp.sum(
            summed[c] * r.cols[y // 2, c // 2, c % 2, y % 2, z].astype(F32), axis=0, keepdims=True
        )
    sent_gain[0] = gain_acc[:, :448]
    sent_gain[1] = gain_acc[:, 448:]

    @pl.loop(0, 8)
    def _(c):
        r.sent[0, c] = summed[c][:, :448].astype(BF16)
        r.sent[1, c] = summed[c][:, 448:].astype(BF16)

    sent, got = r.sent, r.got

    def far_copy(o, s):
        to = lax.rem(ctx + o, 8)
        return pltpu.make_async_remote_copy(
            src_ref=sent.at[s, to],
            dst_ref=got.at[v // 8, pl.ds(pl.multiple_of(lax.rem(v, 8) * 16, 16), 16)],
            send_sem=send_far.at[o * 2 + s],
            recv_sem=recv_far.at[v],
            device_id=here.at(ctx=to, v=ctx * 2 + s),
            device_id_type=MESH,
        )

    def far_gain(o, s):
        return pltpu.make_async_remote_copy(
            src_ref=sent_gain.at[s],
            dst_ref=got_gain.at[v],
            send_sem=send_far.at[16 + o * 2 + s],
            recv_sem=recv_far.at[16 + v],
            device_id=here.at(ctx=lax.rem(ctx + o, 8), v=ctx * 2 + s),
            device_id_type=MESH,
        )

    for o in range(8):
        for s in range(2):
            if o:
                far_copy(o, s).start()
                far_gain(o, s).start()
            else:

                @pl.when(v != ctx * 2 + s)
                def _(s=s):
                    far_copy(0, s).start()
                    far_gain(0, s).start()

                @pl.when(v == ctx * 2 + s)
                def _(s=s):
                    got_gain[v] = sent_gain[s]
                    got[v // 8, pl.ds(pl.multiple_of(lax.rem(v, 8) * 16, 16), 16)] = sent[s, ctx]

    for copy in inputs:
        copy.wait()
    odd = lax.rem(v, 2)
    window = pl.ds(pl.multiple_of(v // 2 * 896 + odd * 384, 128), 512)
    mine, gains, scales = r.mine, r.gains, r.scales
    for e, gain in enumerate((gain_h, gain_e)):
        squares = jnp.zeros((128, 128), F32)
        for c in range(56):
            part = r.inputs[e, :, c * 128 : (c + 1) * 128].astype(F32)
            squares = squares + part * part
        scales[e] = jnp.broadcast_to(
            lax.rsqrt(jnp.sum(squares, axis=1, keepdims=True) / width + EPSILON), (128, 128)
        )

        @pl.when(odd == 0)
        def _(e=e, gain=gain):
            mine[e] = r.inputs[e, :, window][:, :448].astype(F32)
            gains[e] = gain[:, window][:, :448]

        @pl.when(odd == 1)
        def _(e=e, gain=gain):
            mine[e] = r.inputs[e, :, window].astype(F32)[:, 64:]
            gains[e] = gain[:, window][:, 64:]

    head_part(2)
    head_part(3)
    for source in range(16):

        @pl.when(jnp.logical_or(ctx != v // 2, v != source))
        def _(source=source):
            pltpu.make_async_remote_copy(
                src_ref=sent.at[0, 0],
                dst_ref=got.at[source // 8, pl.ds(source % 8 * 16, 16)],
                send_sem=send_far.at[0],
                recv_sem=recv_far.at[source],
                device_id=here.at(ctx=lax.rem(ctx + 1, 8)),
                device_id_type=MESH,
            ).wait_recv()
            pltpu.make_async_remote_copy(
                src_ref=sent_gain.at[0],
                dst_ref=got_gain.at[source],
                send_sem=send_far.at[0],
                recv_sem=recv_far.at[16 + source],
                device_id=here.at(ctx=lax.rem(ctx + 1, 8)),
                device_id_type=MESH,
            ).wait_recv()

    dot_sum = jnp.sum(dot_in[...], axis=0).T
    for e, (out, gain_out) in enumerate(((grad_h, gain_grad_h), (grad_e, gain_grad_e))):
        back = got[e].astype(F32)
        scale = scales[e][:, :1]
        dot = dot_sum[:, e : e + 1]
        grad = scale * (back * gains[e]) - mine[e] * (scale * scale) * (dot / width)
        out[...] = grad.T.astype(BF16)
        gain_out[...] = jnp.sum(got_gain[e * 8 : e * 8 + 8], axis=0) / gains[e]
    for o in range(8):
        for s in range(2):
            if o:
                far_copy(o, s).wait_send()
                far_gain(o, s).wait_send()
            else:

                @pl.when(v != ctx * 2 + s)
                def _(s=s):
                    far_copy(0, s).wait_send()
                    far_gain(0, s).wait_send()

    for copy in outs[2:]:
        copy.wait()
    copies.finish()


def place_kernel(*refs):
    ins, outs, buffers, sem_in, sem_out = refs[:9], refs[9:18], refs[18:23], refs[23], refs[24]
    moves = [(ins[4 + i], buffers[i], outs[4 + i]) for i in range(4)]
    for i in range(8):
        lines = pl.ds(i * 64, 64)
        moves.append((ins[8].at[lines], buffers[4].at[lines], outs[8].at[lines]))
    loads = [pltpu.make_async_copy(a, b, sem_in.at[n]) for n, (a, b, _) in enumerate(moves)]
    stores = [pltpu.make_async_copy(b, c, sem_out.at[n]) for n, (_, b, c) in enumerate(moves)]
    for load in loads:
        load.start()
    for value, out in zip(ins[:4], outs[:4]):
        out[...] = value[...]
    for load, store in zip(loads, stores):
        load.wait()
        store.start()
    for store in stores:
        store.wait()


def back_scratch():
    scratch = dict(
        weights=pltpu.VMEM((2, 448, 896), BF16),
        cols=pltpu.VMEM((2, 4, 2, 2, 4, 16, 896), BF16),
        inputs=pltpu.VMEM((2, 128, 7168), BF16),
        lgr=pltpu.VMEM((512, 512), BF16),
        rows=pltpu.VMEM((4, 4, 4, 32, 1792), BF16),
        halves=pltpu.VMEM((4, 512, 1792), BF16),
        terms=pltpu.VMEM((4, 4, 8, 16, 896), BF16),
        summed=pltpu.VMEM((8, 16, 896), F32),
        stage=pltpu.VMEM((2, 512, 1792), BF16),
        turned=pltpu.VMEM((448, 1024), BF16),
        sent=pltpu.VMEM((2, 8, 16, 448), BF16),
        got=pltpu.VMEM((2, 128, 448), BF16),
        mine=pltpu.VMEM((2, 128, 448), F32),
        gains=pltpu.VMEM((2, 1, 448), F32),
        scales=pltpu.VMEM((2, 128, 128), F32),
        mine_dot=pltpu.VMEM((2, 8, 128), F32),
        dots=pltpu.VMEM((16, 2, 8, 128), F32),
        dot_rows=pltpu.VMEM((8, 8, 128), F32),
        dot_in=pltpu.VMEM((8, 8, 128), F32),
        sent_gain=pltpu.VMEM((2, 1, 448), F32),
        got_gain=pltpu.VMEM((16, 1, 448), F32),
        flat=pltpu.VMEM((2, 1024, 896), BF16),
        rings=[],
    )
    for n, (_, w) in enumerate(BACK_BATCHES):
        scratch["rings"].append(
            [
                pltpu.VMEM((2, 4, 4, 16, w), BF16),
                pltpu.VMEM((2, 4, 8, 16, w), BF16),
                pltpu.VMEM((2, 4, 4, 16, w), BF16),
                pltpu.VMEM((4, 8, 16, w), BF16),
                pltpu.VMEM((3, 8, 16, w), BF16),
            ]
        )
    return scratch


def params(number, limit=56):
    return pltpu.CompilerParams(
        collective_id=number, has_side_effects=True, vmem_limit_bytes=limit * 2**20
    )


def sems(n):
    return [pltpu.SemaphoreType.DMA((n,)), pltpu.SemaphoreType.DMA((n,))]


def shape(dims, kind):
    return jax.ShapeDtypeStruct(dims, kind)


def middle_scratch():
    scratch = dict(
        head=pltpu.VMEM((1024, 7168), BF16),
        rows=pltpu.VMEM((4, 4, 4, 32, 1792), BF16),
        terms=pltpu.VMEM((4, 4, 4, 32, 1792), BF16),
        raw=pltpu.VMEM((512, 1024), F32),
        grad=pltpu.VMEM((512, 1024), BF16),
        grad_t=pltpu.VMEM((1024, 512), BF16),
        scale_wide=pltpu.VMEM((512, 128), F32),
        log_wide=pltpu.VMEM((512, 128), F32),
        cols=pltpu.VMEM((2, 4, 2, 2, 4, 16, 896), BF16),
        raw_in=pltpu.VMEM((2, 16, 7168), BF16),
        normed=pltpu.VMEM((8, 16, SHARED), BF16),
        direct=pltpu.VMEM((8, 2, 2, 4, 16, 896 - SHARED), BF16),
        weights=pltpu.VMEM((2, 448, 896), BF16),
        loss=pltpu.VMEM((2, 8, 128), F32),
        tgt_wide=pltpu.VMEM((512, 128), F32),
        mask_wide=pltpu.VMEM((512, 128), F32),
        away=pltpu.VMEM((4, 128, 448), F32),
        sib=pltpu.VMEM((4, 128, 448), F32),
        summed=pltpu.VMEM((4, 128, 448), F32),
        summed_out=pltpu.VMEM((4, 128, 448), BF16),
        three=pltpu.VMEM((3, 128, 448), BF16),
        projected=pltpu.VMEM((128, 448), F32),
        square=pltpu.VMEM((8, 128), F32),
        squares=pltpu.VMEM((16, 8, 128), F32),
        scales=pltpu.VMEM((4, 8, 128), F32),
        piece=pltpu.VMEM((4, 32, 448), BF16),
        pieces=pltpu.VMEM((4, 32, 448), BF16),
        back=pltpu.VMEM((4, 32, 448), F32),
        backs=pltpu.VMEM((4, 32, 448), F32),
        whole=pltpu.VMEM((32, 1792), F32),
        gain_mine=pltpu.VMEM((8, 448), F32),
        gain_all=pltpu.VMEM((8, 8, 448), F32),
        tile=pltpu.VMEM((8, 128), F32),
        sums=pltpu.VMEM((8, 128), F32),
        dot_tile=pltpu.VMEM((8, 128), F32),
        sums2=pltpu.VMEM((8, 128), F32),
        group=pltpu.VMEM((16, 8, 128), F32),
        group2=pltpu.VMEM((16, 8, 128), F32),
        line=pltpu.VMEM((4, 8, 128), F32),
        line2=pltpu.VMEM((4, 8, 128), F32),
        ones=[],
        threes=[],
        twos=[],
        helds=[],
        outs=[],
    )
    for _, w, _ in PARTS:
        scratch["ones"].append(pltpu.VMEM((2, 4, 4, 16, w), BF16))
        scratch["helds"].append(pltpu.VMEM((2, 4, 4, 16, w), BF16))
        scratch["twos"].append(pltpu.VMEM((2, 4, 4, 32, w), BF16))
        scratch["outs"] += [pltpu.VMEM((4, 4, 32, w), BF16), pltpu.VMEM((4, 32, w), BF16)]
        scratch["threes"] += [pltpu.VMEM((3, 4, 32, w), BF16), pltpu.VMEM((3, 32, w), BF16)]
    return scratch


def contract_last(left, right):
    return lax.dot_general(
        left, right, (((1,), (1,)), ((), ())), preferred_element_type=F32
    )


def local(
    hidden_state, embedded_next, gain_hidden, gain_embed, proj_hidden, proj_embed,
    final_gain, head, targets, loss_mask,
):
    proj_grad, gain_grad, loss, cols, head_half, rows_sib, lgr_sib = pl.pallas_call(
        middle_kernel,
        out_shape=[
            shape((4, 2, 128, 448), BF16), shape((1, 448), F32), shape((1, 1), F32),
            shape((2, 4, 2, 2, 4, 16, 896), BF16),
            shape(head.shape, BF16), shape((4, 4, 4, 32, 1792), BF16), shape((512, 512), BF16),
        ],
        in_specs=[ANY, ANY, VMEM, VMEM, ANY, ANY, VMEM, ANY, VMEM, VMEM],
        out_specs=[VMEM, VMEM, VMEM, ANY, ANY, ANY, ANY],
        scratch_shapes=[middle_scratch()] + sems(360) + [pltpu.SemaphoreType.DMA((16,))],
        compiler_params=params(2, 61),
        name="middle",
    )(
        hidden_state, embedded_next, gain_hidden[None, :], gain_embed[None, :],
        proj_hidden.T, proj_embed.T, final_gain[None, :], head,
        targets.reshape(8, 128), loss_mask.reshape(8, 128),
    )
    grad_h, grad_e, gain_grad_h, gain_grad_e, grad_proj_h, grad_proj_e, grad_head = pl.pallas_call(
        back_kernel,
        out_shape=[
            shape((448, 128), BF16), shape((448, 128), BF16), shape((1, 448), F32), shape((1, 448), F32),
            shape((448, 896), BF16), shape((448, 896), BF16), shape(head.shape, BF16),
        ],
        in_specs=[VMEM, ANY, ANY, ANY, ANY, ANY, VMEM, VMEM, ANY, ANY, ANY],
        out_specs=[VMEM] * 6 + [ANY],
        scratch_shapes=[back_scratch()]
        + sems(46)
        + sems(32)
        + [pltpu.SemaphoreType.DMA((15,)), pltpu.SemaphoreType.DMA((4,))],
        compiler_params=params(5, 58),
        name="back",
    )(
        proj_grad.reshape(1024, 448), proj_hidden.T, proj_embed.T, cols, hidden_state, embedded_next,
        gain_hidden[None, :], gain_embed[None, :], head_half, rows_sib, lgr_sib,
    )
    values = [
        loss, gain_grad_h, gain_grad_e, gain_grad, grad_h, grad_e, grad_proj_h, grad_proj_e, grad_head,
    ]
    specs = [VMEM] * 4 + [ANY] * 5
    loss, gain_grad_h, gain_grad_e, gain_grad, grad_h, grad_e, grad_proj_h, grad_proj_e, grad_head = (
        pl.pallas_call(
            place_kernel,
            out_shape=[shape(value.shape, value.dtype) for value in values],
            in_specs=specs,
            out_specs=specs,
            scratch_shapes=[pltpu.VMEM(value.shape, value.dtype) for value in values[4:]]
            + [pltpu.SemaphoreType.DMA((12,)), pltpu.SemaphoreType.DMA((12,))],
            compiler_params=pltpu.CompilerParams(vmem_limit_bytes=60 * 2**20),
            name="place",
        )(*values)
    )
    return (
        loss[0, 0], grad_h.T, grad_e.T, gain_grad_h[0], gain_grad_e[0],
        grad_proj_h.T, grad_proj_e.T, gain_grad[0], grad_head,
    )


def solution(mesh):
    in_specs = (
        P("ctx", None), P("ctx", None), P(), P(), P("ctx", "vocab"), P("ctx", "vocab"),
        P("vocab"), P(("ctx", "vocab"), None), P(), P(),
    )
    out_specs = (
        P(), P("ctx", "vocab"), P("ctx", "vocab"), P("vocab"), P("vocab"),
        P("ctx", "vocab"), P("ctx", "vocab"), P("vocab"), P(("ctx", "vocab"), None),
    )
    return jax.shard_map(local, mesh=mesh, in_specs=in_specs, out_specs=out_specs, check_vma=False)
```

```python
import jax
import jax.numpy as jnp
from jax import lax
from jax.experimental import pallas as pl
from jax.experimental.pallas import tpu as pltpu
from jax.sharding import PartitionSpec as P

EPSILON = 1e-06
MESH = pl.DeviceIdType.MESH
VMEM = pl.BlockSpec(memory_space=pltpu.VMEM)
ANY = pl.BlockSpec(memory_space=pl.ANY)
F32 = jnp.float32
BF16 = jnp.bfloat16
PARTS = (
    (0, 384, "xyz"),
    (384, 384, "yzx"),
    (768, 256, "zxy"),
    (1024, 256, "xyz"),
    (1280, 256, "yzx"),
    (1536, 256, "zxy"),
)
BATCHES = ((0, 1024), (1024, 768))
SHARED = 640


class Place:
    def __init__(self):
        self.ctx = lax.axis_index("ctx")
        self.v = lax.axis_index("vocab")
        self.c = {"x": self.ctx // 2, "y": self.v // 4, "z": self.v % 4}
        self.core = self.ctx % 2

    def at(self, ctx=None, v=None):
        return {"ctx": self.ctx if ctx is None else ctx, "vocab": self.v if v is None else v}

    def along(self, axis, step):
        i = lax.rem(self.c[axis] + step + 4, 4)
        if axis == "x":
            return self.at(ctx=i * 2 + self.core)
        if axis == "y":
            return self.at(v=i * 4 + self.c["z"])
        return self.at(v=self.c["y"] * 4 + i)

    def sibling(self):
        return self.at(ctx=self.c["x"] * 2 + 1 - self.core)

    def ctx_peer(self, o):
        return self.at(ctx=lax.rem(self.ctx + o, 8))

    def v_peer(self, o):
        return self.at(v=lax.rem(self.v + o, 16))


class Copies:
    def __init__(self, send, recv):
        self.send, self.recv, self.count, self.started = send, recv, 0, []

    def go(self, src, dst, device):
        assert self.count < self.send.shape[0]
        copy = pltpu.make_async_remote_copy(
            src_ref=src,
            dst_ref=dst,
            send_sem=self.send.at[self.count],
            recv_sem=self.recv.at[self.count],
            device_id=device,
            device_id_type=MESH,
        )
        self.count += 1
        copy.start()
        self.started.append(copy)
        return copy

    def finish(self):
        for copy in self.started:
            copy.wait_send()
        self.started = []


def greet(devices):
    barrier = pltpu.get_barrier_semaphore()
    for device in devices:
        pl.semaphore_signal(barrier, inc=1, device_id=device, device_id_type=MESH)


def met(devices):
    pl.semaphore_wait(pltpu.get_barrier_semaphore(), len(devices))


def run(*rings):
    rings = list(rings)
    while rings:
        left = []
        for ring in rings:
            try:
                next(ring)
                left.append(ring)
            except StopIteration:
                pass
        rings = left


def chain(*makers):
    for maker in makers:
        yield from maker()


def gather_ring(copies, here, axis, slab):
    me = here.c[axis]
    right, left = here.along(axis, 1), here.along(axis, -1)
    before, after = lax.rem(me + 3, 4), lax.rem(me + 1, 4)

    def send(i, h, device):
        return copies.go(slab(i, h), slab(i, h), device)

    right_0, left_1 = send(me, 0, right), send(me, 1, left)
    right_1, left_0 = send(me, 1, right), send(me, 0, left)
    yield
    right_0.wait_recv()
    far_a = send(before, 0, right)
    left_1.wait_recv()
    far_b = send(after, 1, left)
    yield
    for copy in (right_1, left_0, far_a, far_b):
        copy.wait_recv()


def gather_near(copies, here, axis, slab):
    me = here.c[axis]
    ins = [copies.go(slab(me, None), slab(me, None), here.along(axis, o)) for o in (1, 2, 3)]
    yield
    for copy in ins:
        copy.wait_recv()


def reduce_ring(copies, here, axis, slab, half, one, two, held, add):
    if isinstance(axis, str):
        me, right, left = here.c[axis], here.along(axis, 1), here.along(axis, -1)
    else:
        me, right, left = axis
    before, after, far = lax.rem(me + 3, 4), lax.rem(me + 1, 4), lax.rem(me + 2, 4)
    a1 = copies.go(slab(far, 0), one.at[0], right)
    b1 = copies.go(slab(far, 1), one.at[1], left)
    a2 = copies.go(slab(after, 1), half(two.at[0], 1), right)
    b2 = copies.go(slab(before, 0), half(two.at[1], 0), left)
    yield
    a1.wait_recv()
    add(held.at[0], (slab(after, 0), one.at[0]))
    a3 = copies.go(held.at[0], half(two.at[0], 0), right)
    b1.wait_recv()
    add(held.at[1], (slab(before, 1), one.at[1]))
    b3 = copies.go(held.at[1], half(two.at[1], 1), left)
    yield
    a2.wait_recv()
    b2.wait_recv()
    a3.wait_recv()
    b3.wait_recv()


def reduce_near(copies, here, axis, slab, recv, finish):
    if isinstance(axis, str):
        me, to = here.c[axis], [here.along(axis, o) for o in (1, 2, 3)]
    else:
        me, to = axis
    ins = [
        copies.go(slab(lax.rem(me + o, 4)), recv.at[o - 1], to[o - 1]) for o in (1, 2, 3)
    ]
    yield
    for copy in ins:
        copy.wait_recv()
    finish(slab(me), [recv.at[o] for o in range(3)])


def add_refs(out, terms):
    lead = out.shape[:-2]
    total = 1
    for n in lead:
        total *= n

    def block(index):
        acc = terms[0][index].astype(F32)
        for term in terms[1:]:
            acc = acc + term[index].astype(F32)
        out[index] = acc.astype(out.dtype)

    if total == 1:
        block(tuple(0 for _ in lead) + (slice(None), slice(None)))
        return

    @pl.loop(0, total)
    def _(i):
        index = []
        for n in reversed(lead):
            index.append(i % n)
            i = i // n
        block(tuple(reversed(index)) + (slice(None), slice(None)))


def all_sum(copies, here, tile, group, line, out):
    group[here.v] = tile[...]
    ins = [copies.go(tile, group.at[here.v], here.v_peer(o)) for o in range(1, 16)]
    yield
    for copy in ins:
        copy.wait_recv()
    x = here.c["x"]
    line[x] = jnp.sum(group[...], axis=0)
    ins = [copies.go(line.at[x], line.at[x], here.along("x", o)) for o in (1, 2, 3)]
    yield
    for copy in ins:
        copy.wait_recv()
    out[...] = jnp.sum(line[...], axis=0)


def spread(row):
    return jnp.broadcast_to(row, (128, 128)).T


def lanes(values):
    total = jnp.sum(values.T, axis=0, keepdims=True)
    return [total[:, i * 128 : (i + 1) * 128] for i in range(4)]


class Bag:
    def __init__(self, refs):
        self.__dict__.update(refs)


def trickle(pieces):
    for start in pieces:
        start()
        yield


def middle_kernel(
    hidden, embed, gain_h, gain_e, proj_h, proj_e, gain, head_own, targets, loss_mask,
    proj_grad, gain_grad, loss, cols_out, half_out, rows_sib, lgr_sib,
    r, send, recv, local_sem,
):
    r = Bag(r)
    here = Place()
    copies = Copies(send, recv)
    friends = [here.ctx_peer(o) for o in range(1, 8)] + [here.v_peer(o) for o in range(1, 16)]
    greet(friends)
    width = 7168
    x, y, z, core = here.c["x"], here.c["y"], here.c["z"], here.core
    head, rows, cols = r.head, r.rows, r.cols
    locals_ = []

    def bring(src, dst):
        copy = pltpu.make_async_copy(src, dst, local_sem.at[len(locals_)])
        copy.start()
        locals_.append(copy)
        return copy

    sliver = pl.ds(pl.multiple_of(lax.rem(here.v, 8) * 16, 16), 16)
    raw_in = [bring(hidden.at[sliver], r.raw_in.at[0]), bring(embed.at[sliver], r.raw_in.at[1])]
    wide_in = [bring(hidden, head.at[pl.ds(0, 128)]), bring(embed, head.at[pl.ds(128, 128)])]
    weights = [bring(proj_h, r.weights.at[0]), bring(proj_e, r.weights.at[1])]
    for copy in raw_in:
        copy.wait()
    first = here.v < 8
    normed = r.normed

    def norm(e, gains):
        wide = r.raw_in[e].astype(F32)
        scale = lax.rsqrt(jnp.mean(wide * wide, axis=-1, keepdims=True) + EPSILON)
        for c in range(8):
            part = slice(c * 896, c * 896 + SHARED)
            normed[c] = (wide[:, part] * scale * gains[:, part]).astype(BF16)

    @pl.when(first)
    def _():
        norm(0, gain_h)

    @pl.when(jnp.logical_not(first))
    def _():
        norm(1, gain_e)

    met(friends)

    def sliver_at(c):
        return cols.at[y // 2, c // 2, c % 2, y % 2, z, :, pl.ds(0, SHARED)]

    arrivals = []
    for o in range(1, 8):
        peer = lax.rem(here.ctx + o, 8)
        arrivals.append(copies.go(normed.at[peer], sliver_at(here.ctx), here.ctx_peer(o)))
    cols[y // 2, x, core, y % 2, z, :, :SHARED] = normed[here.ctx]

    for arrival in arrivals:
        arrival.wait_recv()

    def col_slabs(part):
        lanes_ = pl.ds(*part)

        def span(h):
            return slice(None) if h is None else pl.ds(h * 2, 2)

        return {
            "y_first": lambda i, h: cols.at[i // 2, span(h), :, i % 2, z, :, lanes_],
            "z_last": lambda i, h: cols.at[:, span(h), :, :, i, :, lanes_],
            "z_first": lambda i, h: cols.at[y // 2, span(h), :, y % 2, i, :, lanes_],
            "y_last": lambda i, h: cols.at[i // 2, span(h), :, i % 2, :, :, lanes_],
        }

    def col_ring(part, names):
        slabs = col_slabs(part)
        return chain(
            lambda: gather_near(copies, here, names[0][0], slabs[names[0]]),
            lambda: gather_ring(copies, here, names[1][0], slabs[names[1]]),
        )

    def straight_part():
        direct = r.direct
        for copy in wide_in:
            copy.wait()
        for e, gains in enumerate((gain_h, gain_e)):
            lines = slice(e * 128, (e + 1) * 128)
            squares = jnp.zeros((128, 128), F32)
            for c in range(56):
                part = head[lines, c * 128 : (c + 1) * 128].astype(F32)
                squares = squares + part * part
            scale = lax.rsqrt(jnp.sum(squares, axis=1, keepdims=True) / width + EPSILON)
            for c in range(8):
                part = slice(c * 896 + SHARED, (c + 1) * 896)
                direct[c, e] = (
                    (head[lines, part].astype(F32) * scale * gains[:, part])
                    .astype(BF16)
                    .reshape(2, 4, 16, 896 - SHARED)
                )

        straight = []
        for o in range(1, 8):
            peer = lax.rem(here.ctx + o, 8)
            straight.append(
                copies.go(
                    direct.at[peer],
                    cols.at[:, x, core, :, :, :, pl.ds(SHARED, 896 - SHARED)],
                    here.ctx_peer(o),
                )
            )
        cols[:, x, core, :, :, :, SHARED:] = direct[here.ctx]
        yield
        yield
        for copy in straight:
            copy.wait_recv()

    head_pieces = []

    def head_piece(i):
        piece_rows = pl.ds(i * 128, 128)
        head_pieces.append(
            copies.go(
                head_own.at[piece_rows], head.at[pl.ds(512 + i * 128, 128)], here.sibling()
            )
        )

    for i in range(4):
        head_piece(i)
    mark, kept = copies.count, copies.started
    copies.started = []

    @pl.when(core == 0)
    def _():
        run(*[col_ring(part, ("y_first", "z_last")) for part in ((0, 384), (384, 256))], straight_part())
        copies.finish()

    copies.count = mark

    @pl.when(core == 1)
    def _():
        run(*[col_ring(part, ("z_first", "y_last")) for part in ((0, 384), (384, 256))], straight_part())
        copies.finish()

    copies.started = kept
    loads = [bring(head_own.at[pl.ds(i * 128, 128)], head.at[pl.ds(i * 128, 128)]) for i in range(4)]
    for copy in weights:
        copy.wait()

    def project(k):
        return contract_last(cols[0, :, k].reshape(512, 896), r.weights[0]) + contract_last(
            cols[1, :, k].reshape(512, 896), r.weights[1]
        )

    r.away[...] = project(1 - core).reshape(4, 128, 448)
    swap = copies.go(r.away, r.sib, here.sibling())
    summed = r.summed
    summed[...] = project(core).reshape(4, 128, 448)
    bring(cols, cols_out)
    tgt_wide, mask_wide = r.tgt_wide, r.mask_wide
    mask_rows = []
    for i in range(4):
        at = pl.ds(i * 2 + core, 1)
        tgt_wide[i * 128 : (i + 1) * 128] = spread(targets[at].astype(F32))
        mask_row = loss_mask[at].astype(F32)
        mask_rows.append(mask_row)
        mask_wide[i * 128 : (i + 1) * 128] = spread(mask_row)
    swap.wait_recv()
    for i in range(4):
        summed[i] += r.sib[i]
        r.summed_out[i] = summed[i].astype(BF16)

    def add_x(own, others):
        del own
        total = summed[x]
        for other in others:
            total = total + other[...].astype(F32)
        r.projected[...] = total

    run(reduce_near(copies, here, "x", lambda i: r.summed_out.at[i], r.three, add_x))
    total = r.projected[...]
    piece, pieces = r.piece, r.pieces
    piece[...] = (total * gain[...]).astype(BF16).reshape(piece.shape)
    exchange = []
    for o in range(1, 4):
        to = lax.rem(z + o, 4)
        exchange.append(copies.go(piece.at[to], pieces.at[z], here.along("z", o)))
    pieces[z] = piece[z]
    r.square[...] = lax.dot_general(
        jnp.ones((8, total.shape[1]), F32), total * total, (((1,), (1,)), ((), ())),
        precision=lax.Precision.HIGHEST, preferred_element_type=F32,
    )
    squares, scales = r.squares, r.scales
    squares[here.v] = r.square[...]
    for copy in exchange:
        copy.wait_recv()
    for i in range(4):
        rows[y, x, z, :, i * 448 : (i + 1) * 448] = pieces[i]

    def stage(part, k):
        off, w, order = part

        def slab(i, h):
            index = []
            for a in "yxz":
                at = order.index(a)
                index.append(i if at == k else slice(None) if at < k else here.c[a])
            lines = slice(None) if h is None else pl.ds(h * 16, 16)
            return rows.at[(*index, lines, pl.ds(off, w))]

        ring = gather_near if k < 2 else gather_ring
        return lambda: ring(copies, here, order[k], slab)

    def scale():
        ins = [copies.go(r.square, squares.at[here.v], here.v_peer(o)) for o in range(1, 16)]
        yield
        yield
        for copy in ins:
            copy.wait_recv()
        scales[x] = lax.rsqrt(jnp.sum(squares[...], axis=0) / width + EPSILON)
        ins = [copies.go(scales.at[x], scales.at[x], here.along("x", o)) for o in range(1, 4)]
        yield
        yield
        for copy in ins:
            copy.wait_recv()

    raw = r.raw

    def logits_of(batch):
        off, w = BATCHES[batch]

        @pl.loop(0, 4)
        def _(j):
            term = lax.dot_general(
                rows[j, :, :, :, off : off + w].reshape(512, w),
                head[:, pl.ds(pl.multiple_of(j * 1792 + off, 128), w)],
                (((1,), (1,)), ((), ())), preferred_element_type=F32,
            )
            if batch:
                raw[...] += term
            else:

                @pl.when(j == 0)
                def _():
                    raw[...] = term

                @pl.when(j > 0)
                def _():
                    raw[...] += term

    gathers = [chain(*[stage(part, k) for k in range(3)]) for part in PARTS]
    leading, trailing, scaling = gathers[:3], gathers[3:], scale()

    def advance(group):
        alive = False
        for ring in group:
            try:
                next(ring)
                alive = True
            except StopIteration:
                pass
        return alive

    advance(leading)
    advance([scaling])
    alive = True
    while alive:
        alive = advance(leading)
        advance(trailing)
        advance([scaling])
    while advance([scaling]):
        pass
    for copy in loads:
        copy.wait()
    for copy in head_pieces:
        copy.wait_recv()
    logits_of(0)
    advance(trailing)
    logits_of(1)

    scale_wide, log_wide = r.scale_wide, r.log_wide
    for i in range(4):
        scale_wide[i * 128 : (i + 1) * 128] = spread(scales[i, :1])
    column = lax.broadcasted_iota(jnp.int32, (512, 128), 1)
    starts = [(here.ctx * 16 + here.v) * 512, ((here.ctx + 1 - 2 * core) * 16 + here.v) * 512]

    def is_hit(j):
        return tgt_wide[...] == (column + (starts[j // 4] + j % 4 * 128)).astype(F32)

    exps = jnp.zeros((512, 128), F32)
    hits = jnp.zeros((512, 128), F32)
    for j in range(8):
        logit = raw[:, j * 128 : (j + 1) * 128] * scale_wide[...]
        exps = exps + jnp.exp(logit)
        hits = hits + jnp.where(is_hit(j), logit, 0.0)
    tile, sums = r.tile, r.sums
    for i, row in enumerate(lanes(exps) + lanes(hits)):
        tile[i : i + 1] = row
    run(all_sum(copies, here, tile, r.group, r.line, sums))
    logs = jnp.log(sums[:4])
    for i in range(4):
        log_wide[i * 128 : (i + 1) * 128] = spread(logs[i : i + 1])
    grad, grad_t = r.grad, r.grad_t

    def wide_of(j):
        term = raw[:, j * 128 : (j + 1) * 128]
        prob = jnp.exp(term * scale_wide[...] - log_wide[...])
        return mask_wide[...] * (prob - is_hit(j).astype(F32)), term

    for j in range(8):
        grad[:, j * 128 : (j + 1) * 128] = wide_of(j)[0].astype(BF16)
    late = []

    def beside():
        each = logs - sums[4:]
        lost = sum(
            jnp.sum(mask_rows[i] * each[i : i + 1], axis=1, keepdims=True) for i in range(4)
        )
        loss_part = r.loss
        loss_part[core] = jnp.broadcast_to(lost, (8, 128))
        late.append(copies.go(loss_part.at[core], loss_part.at[core], here.sibling()))
        dots = jnp.zeros((512, 128), F32)
        for j in range(8):
            wide, term = wide_of(j)
            dots = dots + wide.astype(BF16).astype(F32) * term
            grad_t[j * 128 : (j + 1) * 128] = (wide * scale_wide[...]).T.astype(BF16)
        dot_tile = r.dot_tile
        for i, row in enumerate(lanes(dots)):
            dot_tile[i : i + 1] = row
            dot_tile[i + 4 : i + 5] = row
        late.append(copies.go(grad_t.at[pl.ds(512, 512)], lgr_sib, here.sibling()))

    terms, whole = r.terms, r.whole

    def half_lines(ref, h):
        index = (slice(None),) * (len(ref.shape) - 2) + (pl.ds(h * 16, 16),)
        return ref.at[index]

    def part_rings(n, part):
        off, w, order = part
        order = order[::-1]
        axes = "yxz"
        cols = pl.ds(off, w)
        one, two, held = r.ones[n], r.twos[n], r.helds[n]
        out = r.outs[n * 2]

        def slab(i, h):
            index = tuple(i if a == order[0] else slice(None) for a in "yxz")
            lines = slice(None) if h is None else pl.ds(h * 16, 16)
            return terms.at[(*index, lines, cols)]

        yield from reduce_ring(copies, here, order[0], slab, half_lines, one, two, held, add_refs)
        add_refs(out, (slab(here.c[order[0]], None), two.at[0], two.at[1]))
        axes = axes.replace(order[0], "")
        last = r.outs[n * 2 + 1]

        def second(i):
            return out.at[tuple(i if a == order[1] else slice(None) for a in axes)]

        yield from reduce_near(
            copies, here, order[1], second, r.threes[n * 2],
            lambda own, others: add_refs(last, (own, *others)),
        )

        def third(own, others):
            total = own[...].astype(F32)
            for other in others:
                total = total + other[...].astype(F32)
            whole[:, off : off + w] = total

        yield from reduce_near(
            copies, here, order[2], lambda i: last.at[i], r.threes[n * 2 + 1], third
        )

    def product(off, w):

        @pl.loop(0, 4)
        def _(j):
            terms[j, :, :, :, off : off + w] = (
                jnp.dot(
                    grad[...], head[:, pl.ds(pl.multiple_of(j * 1792 + off, 128), w)],
                    preferred_element_type=F32,
                )
                .astype(BF16)
                .reshape(4, 4, 32, w)
            )

    swap_rows = []

    def row_piece(j):
        swap_rows.append(copies.go(rows.at[j], rows_sib.at[j], here.sibling()))

    rings = [part_rings(n, part) for n, part in enumerate(PARTS)]
    for n in range(3):
        product(*PARTS[n][:2])
        advance(rings[n : n + 1])
    product(*BATCHES[1])
    advance(rings[3:])
    beside()
    row_dots = all_sum(copies, here, r.dot_tile, r.group2, r.line2, r.sums2)

    def half_head(j):
        lanes_ = pl.ds(j * 1792, 1792)
        head[:512, lanes_] = jnp.dot(
            grad_t[:512], rows[j].reshape(512, 1792), preferred_element_type=F32
        ).astype(BF16)
        bring(head.at[pl.ds(0, 512), lanes_], half_out.at[:, lanes_])

    run(
        *rings,
        row_dots,
        trickle([lambda j=j: row_piece(j) for j in range(4)]),
        trickle([lambda j=j: half_head(j) for j in range(4)]),
    )

    back, backs = r.back, r.backs
    for i in range(4):
        back[i] = whole[:, i * 448 : (i + 1) * 448]
    exchange = []
    for o in range(1, 4):
        to = lax.rem(z + o, 4)
        exchange.append(copies.go(back.at[to], backs.at[z], here.along("z", o)))
    backs[z] = back[z]
    row_scale = scale_wide[pl.ds(pl.multiple_of(x * 128, 128), 128)][:, :1]
    row_dot = spread(r.sums2[pl.ds(x, 1)])[:, :1]
    wide = r.projected[...]
    for copy in exchange:
        copy.wait_recv()
    normed_grad = backs[...].reshape(128, 448)
    grad_out = row_scale * (normed_grad * gain[...]) - wide * (
        row_scale * row_scale * row_scale
    ) * (row_dot / width)
    proj_grad[x, core] = grad_out.astype(BF16)

    def share():
        def at(i):
            return proj_grad.at[i, core]

        def pass_on(i):
            return copies.go(at(i), at(i), here.sibling())

        ins = [copies.go(at(x), at(x), here.along("x", o)) for o in (1, 2, 3)]
        passed = [pass_on(x)]
        yield
        for o in (1, 3, 2):
            ins[o - 1].wait_recv()
            passed.append(pass_on(lax.rem(x + 4 - o, 4)))
        for copy in passed:
            copy.wait_recv()

    def gain_sum():
        mine, every = r.gain_mine, r.gain_all
        mine[...] = jnp.broadcast_to(
            jnp.sum(normed_grad * wide * row_scale, axis=0, keepdims=True), (8, 448)
        )
        every[here.ctx] = mine[...]
        ins = [copies.go(mine, every.at[here.ctx], here.ctx_peer(o)) for o in range(1, 8)]
        yield
        yield
        for copy in ins:
            copy.wait_recv()
        gain_grad[...] = jnp.sum(every[...], axis=0)[:1]

    run(share(), gain_sum())
    for copy in (*swap_rows, *late):
        copy.wait_recv()
    loss[...] = (r.loss[0, :1, :1] + r.loss[1, :1, :1]) / 1024.0
    for copy in [copy for copy in locals_[6:] if not any(copy is one for one in loads)]:
        copy.wait()
    copies.finish()


BACK_BATCHES = ((0, 384), (384, 512))


def back_kernel(
    proj_grad, proj_h, proj_e, cols, hidden, embed, gain_h, gain_e, head_half, rows_sib, lgr_sib,
    grad_h, grad_e, gain_grad_h, gain_grad_e, grad_proj_h, grad_proj_e, grad_head,
    r, send, recv, send_far, recv_far, local_sem, out_sem,
):
    r = Bag(r)
    here = Place()
    copies = Copies(send, recv)
    y, z, v, ctx, core = here.c["y"], here.c["z"], here.v, here.ctx, here.core
    width = 7168
    friends = (
        [here.v_peer(o) for o in range(1, 16)]
        + [here.ctx_peer(o) for o in range(1, 8)]
        + [here.at(ctx=v // 2, v=source) for source in range(16)]
    )
    greet(friends)
    locals_ = []

    def bring(src, dst):
        copy = pltpu.make_async_copy(src, dst, local_sem.at[len(locals_)])
        copy.start()
        locals_.append(copy)
        return copy

    weights = [bring(proj_h, r.weights.at[0]), bring(proj_e, r.weights.at[1])]
    cols_in = bring(cols, r.cols)
    inputs = [bring(hidden, r.inputs.at[0]), bring(embed, r.inputs.at[1])]
    lgr_in = bring(lgr_sib, r.lgr)
    rows_in = []
    for j in range(4):
        rows_in.append(
            [
                bring(head_half.at[:, pl.ds(j * 1792, 1792)], r.halves.at[j]),
                bring(rows_sib.at[j], r.rows.at[j]),
            ]
        )
    for copy in weights:
        copy.wait()

    first_at, second_at = jnp.where(core == 0, y, z), jnp.where(core == 0, z, y)

    def near(second, step):
        along_y, along_z = here.along("y", step)["vocab"], here.along("z", step)["vocab"]
        pick = (core == 0) if not second else (core == 1)
        return here.at(v=jnp.where(pick, along_y, along_z))

    ring_first = (first_at, near(False, 1), near(False, -1))
    ring_second = (second_at, [near(True, o) for o in (1, 2, 3)])
    terms, summed, flat = r.terms, r.summed, r.flat

    def fill(batch):
        off, w = BACK_BATCHES[batch]
        for e in range(2):
            back = jnp.dot(
                proj_grad[...], r.weights[e, :, off : off + w], preferred_element_type=F32
            ).astype(BF16)
            flat[e, :, off : off + w] = back
            back = back.reshape(8, 8, 16, w)
            for j in range(8):
                at_y, at_z = e * 2 + j // 4, j % 4
                p = jnp.where(core == 0, at_y, at_z)
                q = jnp.where(core == 0, at_z, at_y)
                terms[p, q, :, :, off : off + w] = back[:, j]

    def back_ring(batch):
        off, w = BACK_BATCHES[batch]
        lanes_ = pl.ds(off, w)

        def span(h):
            return slice(None) if h is None else pl.ds(h * 4, 4)

        one, two, held, out, three = r.rings[batch]

        def big(i, h):
            return terms.at[i, :, span(h), :, lanes_]

        yield from reduce_ring(
            copies, here, ring_first, big, lambda ref, h: ref.at[:, span(h)], one, two, held, add_refs
        )
        add_refs(out, (big(first_at, None), two.at[0], two.at[1]))

        def end(own, others):
            for c in range(8):
                total = own[c].astype(F32)
                for other in others:
                    total = total + other[c].astype(F32)
                summed[c, :, off : off + w] = total

        yield from reduce_near(copies, here, ring_second, lambda i: out.at[i], three, end)

    outs = []

    def head_part(j):
        for copy in rows_in[j]:
            copy.wait()
        slot = j % 2
        if j >= 2:
            outs[j - 2].wait()
        r.stage[slot] = (
            jnp.dot(r.lgr[...], r.rows[j].reshape(512, 1792), preferred_element_type=F32)
            + r.halves[j].astype(F32)
        ).astype(BF16)
        copy = pltpu.make_async_copy(
            r.stage.at[slot], grad_head.at[:, pl.ds(j * 1792, 1792)], out_sem.at[j]
        )
        copy.start()
        outs.append(copy)

    def proj_part(e):
        out = (grad_proj_h, grad_proj_e)[e]
        out[...] = jnp.dot(
            r.turned[...], r.cols[e].reshape(1024, 896), preferred_element_type=F32
        ).astype(BF16)

    mine_dot, dots, dot_rows, dot_in = r.mine_dot, r.dots, r.dot_rows, r.dot_in

    def inner():
        for e in range(2):
            acc = jnp.zeros((1024, 128), F32)
            for c in range(7):
                part = slice(c * 128, (c + 1) * 128)
                cols_part = r.cols[e, :, :, :, :, :, part].reshape(1024, 128).astype(F32)
                acc = acc + flat[e, :, part].astype(F32) * cols_part
            for c in range(8):
                row = jnp.sum(acc[c * 128 : (c + 1) * 128].T, axis=0, keepdims=True)
                mine_dot[e, c : c + 1] = row
        ins = [copies.go(mine_dot, dots.at[v], here.v_peer(o)) for o in range(1, 16)]
        dots[v] = mine_dot[...]
        yield
        for copy in ins:
            copy.wait_recv()
        total = jnp.sum(dots[...], axis=0)
        for c in range(8):
            for e in range(2):
                dot_rows[c, e : e + 1] = total[e, c : c + 1]
        ins = [
            copies.go(dot_rows.at[lax.rem(ctx + o, 8)], dot_in.at[ctx], here.ctx_peer(o))
            for o in range(1, 8)
        ]
        dot_in[ctx] = dot_rows[ctx]
        yield
        for copy in ins:
            copy.wait_recv()

    rings = [back_ring(0), back_ring(1)]
    dotting = inner()
    fill(0)
    met(friends)
    next(rings[0])
    fill(1)
    next(rings[1])
    dot_rows[...] = jnp.zeros_like(dot_rows)
    cols_in.wait()
    next(dotting)
    next(rings[0])
    r.turned[...] = proj_grad[...].astype(F32).T.astype(BF16)
    proj_part(0)
    next(rings[1])
    lgr_in.wait()
    head_part(0)
    head_part(1)
    next(rings[0])
    next(dotting)
    next(rings[1])
    proj_part(1)
    next(rings[0], None)
    next(rings[1], None)
    next(dotting, None)

    sent_gain, got_gain = r.sent_gain, r.got_gain
    gain_acc = jnp.zeros((1, 896), F32)
    for c in range(8):
        gain_acc = gain_acc + jnp.sum(
            summed[c] * r.cols[y // 2, c // 2, c % 2, y % 2, z].astype(F32), axis=0, keepdims=True
        )
    sent_gain[0] = gain_acc[:, :448]
    sent_gain[1] = gain_acc[:, 448:]

    @pl.loop(0, 8)
    def _(c):
        r.sent[0, c] = summed[c][:, :448].astype(BF16)
        r.sent[1, c] = summed[c][:, 448:].astype(BF16)

    sent, got = r.sent, r.got

    def far_copy(o, s):
        to = lax.rem(ctx + o, 8)
        return pltpu.make_async_remote_copy(
            src_ref=sent.at[s, to],
            dst_ref=got.at[v // 8, pl.ds(pl.multiple_of(lax.rem(v, 8) * 16, 16), 16)],
            send_sem=send_far.at[o * 2 + s],
            recv_sem=recv_far.at[v],
            device_id=here.at(ctx=to, v=ctx * 2 + s),
            device_id_type=MESH,
        )

    def far_gain(o, s):
        return pltpu.make_async_remote_copy(
            src_ref=sent_gain.at[s],
            dst_ref=got_gain.at[v],
            send_sem=send_far.at[16 + o * 2 + s],
            recv_sem=recv_far.at[16 + v],
            device_id=here.at(ctx=lax.rem(ctx + o, 8), v=ctx * 2 + s),
            device_id_type=MESH,
        )

    for o in range(8):
        for s in range(2):
            if o:
                far_copy(o, s).start()
                far_gain(o, s).start()
            else:

                @pl.when(v != ctx * 2 + s)
                def _(s=s):
                    far_copy(0, s).start()
                    far_gain(0, s).start()

                @pl.when(v == ctx * 2 + s)
                def _(s=s):
                    got_gain[v] = sent_gain[s]
                    got[v // 8, pl.ds(pl.multiple_of(lax.rem(v, 8) * 16, 16), 16)] = sent[s, ctx]

    for copy in inputs:
        copy.wait()
    odd = lax.rem(v, 2)
    window = pl.ds(pl.multiple_of(v // 2 * 896 + odd * 384, 128), 512)
    mine, gains, scales = r.mine, r.gains, r.scales
    for e, gain in enumerate((gain_h, gain_e)):
        squares = jnp.zeros((128, 128), F32)
        for c in range(56):
            part = r.inputs[e, :, c * 128 : (c + 1) * 128].astype(F32)
            squares = squares + part * part
        scales[e] = jnp.broadcast_to(
            lax.rsqrt(jnp.sum(squares, axis=1, keepdims=True) / width + EPSILON), (128, 128)
        )

        @pl.when(odd == 0)
        def _(e=e, gain=gain):
            mine[e] = r.inputs[e, :, window][:, :448].astype(F32)
            gains[e] = gain[:, window][:, :448]

        @pl.when(odd == 1)
        def _(e=e, gain=gain):
            mine[e] = r.inputs[e, :, window].astype(F32)[:, 64:]
            gains[e] = gain[:, window][:, 64:]

    head_part(2)
    head_part(3)
    for source in range(16):

        @pl.when(jnp.logical_or(ctx != v // 2, v != source))
        def _(source=source):
            pltpu.make_async_remote_copy(
                src_ref=sent.at[0, 0],
                dst_ref=got.at[source // 8, pl.ds(source % 8 * 16, 16)],
                send_sem=send_far.at[0],
                recv_sem=recv_far.at[source],
                device_id=here.at(ctx=lax.rem(ctx + 1, 8)),
                device_id_type=MESH,
            ).wait_recv()
            pltpu.make_async_remote_copy(
                src_ref=sent_gain.at[0],
                dst_ref=got_gain.at[source],
                send_sem=send_far.at[0],
                recv_sem=recv_far.at[16 + source],
                device_id=here.at(ctx=lax.rem(ctx + 1, 8)),
                device_id_type=MESH,
            ).wait_recv()

    dot_sum = jnp.sum(dot_in[...], axis=0).T
    for e, (out, gain_out) in enumerate(((grad_h, gain_grad_h), (grad_e, gain_grad_e))):
        back = got[e].astype(F32)
        scale = scales[e][:, :1]
        dot = dot_sum[:, e : e + 1]
        grad = scale * (back * gains[e]) - mine[e] * (scale * scale) * (dot / width)
        out[...] = grad.T.astype(BF16)
        gain_out[...] = jnp.sum(got_gain[e * 8 : e * 8 + 8], axis=0) / gains[e]
    for o in range(8):
        for s in range(2):
            if o:
                far_copy(o, s).wait_send()
                far_gain(o, s).wait_send()
            else:

                @pl.when(v != ctx * 2 + s)
                def _(s=s):
                    far_copy(0, s).wait_send()
                    far_gain(0, s).wait_send()

    for copy in outs[2:]:
        copy.wait()
    copies.finish()


def place_kernel(*refs):
    ins, outs, buffers, sem_in, sem_out = refs[:9], refs[9:18], refs[18:23], refs[23], refs[24]
    moves = [(ins[4 + i], buffers[i], outs[4 + i]) for i in range(4)]
    for i in range(16):
        lines = pl.ds(i * 32, 32)
        moves.append((ins[8].at[lines], buffers[4].at[lines], outs[8].at[lines]))
    loads = [pltpu.make_async_copy(a, b, sem_in.at[n]) for n, (a, b, _) in enumerate(moves)]
    stores = [pltpu.make_async_copy(b, c, sem_out.at[n]) for n, (_, b, c) in enumerate(moves)]
    for load in loads:
        load.start()
    for value, out in zip(ins[:4], outs[:4]):
        out[...] = value[...]
    for load, store in zip(loads, stores):
        load.wait()
        store.start()
    for store in stores:
        store.wait()


def back_scratch():
    scratch = dict(
        weights=pltpu.VMEM((2, 448, 896), BF16),
        cols=pltpu.VMEM((2, 4, 2, 2, 4, 16, 896), BF16),
        inputs=pltpu.VMEM((2, 128, 7168), BF16),
        lgr=pltpu.VMEM((512, 512), BF16),
        rows=pltpu.VMEM((4, 4, 4, 32, 1792), BF16),
        halves=pltpu.VMEM((4, 512, 1792), BF16),
        terms=pltpu.VMEM((4, 4, 8, 16, 896), BF16),
        summed=pltpu.VMEM((8, 16, 896), F32),
        stage=pltpu.VMEM((2, 512, 1792), BF16),
        turned=pltpu.VMEM((448, 1024), BF16),
        sent=pltpu.VMEM((2, 8, 16, 448), BF16),
        got=pltpu.VMEM((2, 128, 448), BF16),
        mine=pltpu.VMEM((2, 128, 448), F32),
        gains=pltpu.VMEM((2, 1, 448), F32),
        scales=pltpu.VMEM((2, 128, 128), F32),
        mine_dot=pltpu.VMEM((2, 8, 128), F32),
        dots=pltpu.VMEM((16, 2, 8, 128), F32),
        dot_rows=pltpu.VMEM((8, 8, 128), F32),
        dot_in=pltpu.VMEM((8, 8, 128), F32),
        sent_gain=pltpu.VMEM((2, 1, 448), F32),
        got_gain=pltpu.VMEM((16, 1, 448), F32),
        flat=pltpu.VMEM((2, 1024, 896), BF16),
        rings=[],
    )
    for n, (_, w) in enumerate(BACK_BATCHES):
        scratch["rings"].append(
            [
                pltpu.VMEM((2, 4, 4, 16, w), BF16),
                pltpu.VMEM((2, 4, 8, 16, w), BF16),
                pltpu.VMEM((2, 4, 4, 16, w), BF16),
                pltpu.VMEM((4, 8, 16, w), BF16),
                pltpu.VMEM((3, 8, 16, w), BF16),
            ]
        )
    return scratch


def params(number, limit=56):
    return pltpu.CompilerParams(
        collective_id=number, has_side_effects=True, vmem_limit_bytes=limit * 2**20
    )


def sems(n):
    return [pltpu.SemaphoreType.DMA((n,)), pltpu.SemaphoreType.DMA((n,))]


def shape(dims, kind):
    return jax.ShapeDtypeStruct(dims, kind)


def middle_scratch():
    scratch = dict(
        head=pltpu.VMEM((1024, 7168), BF16),
        rows=pltpu.VMEM((4, 4, 4, 32, 1792), BF16),
        terms=pltpu.VMEM((4, 4, 4, 32, 1792), BF16),
        raw=pltpu.VMEM((512, 1024), F32),
        grad=pltpu.VMEM((512, 1024), BF16),
        grad_t=pltpu.VMEM((1024, 512), BF16),
        scale_wide=pltpu.VMEM((512, 128), F32),
        log_wide=pltpu.VMEM((512, 128), F32),
        cols=pltpu.VMEM((2, 4, 2, 2, 4, 16, 896), BF16),
        raw_in=pltpu.VMEM((2, 16, 7168), BF16),
        normed=pltpu.VMEM((8, 16, SHARED), BF16),
        direct=pltpu.VMEM((8, 2, 2, 4, 16, 896 - SHARED), BF16),
        weights=pltpu.VMEM((2, 448, 896), BF16),
        loss=pltpu.VMEM((2, 8, 128), F32),
        tgt_wide=pltpu.VMEM((512, 128), F32),
        mask_wide=pltpu.VMEM((512, 128), F32),
        away=pltpu.VMEM((4, 128, 448), F32),
        sib=pltpu.VMEM((4, 128, 448), F32),
        summed=pltpu.VMEM((4, 128, 448), F32),
        summed_out=pltpu.VMEM((4, 128, 448), BF16),
        three=pltpu.VMEM((3, 128, 448), BF16),
        projected=pltpu.VMEM((128, 448), F32),
        square=pltpu.VMEM((8, 128), F32),
        squares=pltpu.VMEM((16, 8, 128), F32),
        scales=pltpu.VMEM((4, 8, 128), F32),
        piece=pltpu.VMEM((4, 32, 448), BF16),
        pieces=pltpu.VMEM((4, 32, 448), BF16),
        back=pltpu.VMEM((4, 32, 448), F32),
        backs=pltpu.VMEM((4, 32, 448), F32),
        whole=pltpu.VMEM((32, 1792), F32),
        gain_mine=pltpu.VMEM((8, 448), F32),
        gain_all=pltpu.VMEM((8, 8, 448), F32),
        tile=pltpu.VMEM((8, 128), F32),
        sums=pltpu.VMEM((8, 128), F32),
        dot_tile=pltpu.VMEM((8, 128), F32),
        sums2=pltpu.VMEM((8, 128), F32),
        group=pltpu.VMEM((16, 8, 128), F32),
        group2=pltpu.VMEM((16, 8, 128), F32),
        line=pltpu.VMEM((4, 8, 128), F32),
        line2=pltpu.VMEM((4, 8, 128), F32),
        ones=[],
        threes=[],
        twos=[],
        helds=[],
        outs=[],
    )
    for _, w, _ in PARTS:
        scratch["ones"].append(pltpu.VMEM((2, 4, 4, 16, w), BF16))
        scratch["helds"].append(pltpu.VMEM((2, 4, 4, 16, w), BF16))
        scratch["twos"].append(pltpu.VMEM((2, 4, 4, 32, w), BF16))
        scratch["outs"] += [pltpu.VMEM((4, 4, 32, w), BF16), pltpu.VMEM((4, 32, w), BF16)]
        scratch["threes"] += [pltpu.VMEM((3, 4, 32, w), BF16), pltpu.VMEM((3, 32, w), BF16)]
    return scratch


def contract_last(left, right):
    return lax.dot_general(
        left, right, (((1,), (1,)), ((), ())), preferred_element_type=F32
    )


def local(
    hidden_state, embedded_next, gain_hidden, gain_embed, proj_hidden, proj_embed,
    final_gain, head, targets, loss_mask,
):
    proj_grad, gain_grad, loss, cols, head_half, rows_sib, lgr_sib = pl.pallas_call(
        middle_kernel,
        out_shape=[
            shape((4, 2, 128, 448), BF16), shape((1, 448), F32), shape((1, 1), F32),
            shape((2, 4, 2, 2, 4, 16, 896), BF16),
            shape(head.shape, BF16), shape((4, 4, 4, 32, 1792), BF16), shape((512, 512), BF16),
        ],
        in_specs=[ANY, ANY, VMEM, VMEM, ANY, ANY, VMEM, ANY, VMEM, VMEM],
        out_specs=[VMEM, VMEM, VMEM, ANY, ANY, ANY, ANY],
        scratch_shapes=[middle_scratch()] + sems(360) + [pltpu.SemaphoreType.DMA((16,))],
        compiler_params=params(2, 61),
        name="middle",
    )(
        hidden_state, embedded_next, gain_hidden[None, :], gain_embed[None, :],
        proj_hidden.T, proj_embed.T, final_gain[None, :], head,
        targets.reshape(8, 128), loss_mask.reshape(8, 128),
    )
    grad_h, grad_e, gain_grad_h, gain_grad_e, grad_proj_h, grad_proj_e, grad_head = pl.pallas_call(
        back_kernel,
        out_shape=[
            shape((448, 128), BF16), shape((448, 128), BF16), shape((1, 448), F32), shape((1, 448), F32),
            shape((448, 896), BF16), shape((448, 896), BF16), shape(head.shape, BF16),
        ],
        in_specs=[VMEM, ANY, ANY, ANY, ANY, ANY, VMEM, VMEM, ANY, ANY, ANY],
        out_specs=[VMEM] * 6 + [ANY],
        scratch_shapes=[back_scratch()]
        + sems(46)
        + sems(32)
        + [pltpu.SemaphoreType.DMA((15,)), pltpu.SemaphoreType.DMA((4,))],
        compiler_params=params(5, 58),
        name="back",
    )(
        proj_grad.reshape(1024, 448), proj_hidden.T, proj_embed.T, cols, hidden_state, embedded_next,
        gain_hidden[None, :], gain_embed[None, :], head_half, rows_sib, lgr_sib,
    )
    values = [
        loss, gain_grad_h, gain_grad_e, gain_grad, grad_h, grad_e, grad_proj_h, grad_proj_e, grad_head,
    ]
    specs = [VMEM] * 4 + [ANY] * 5
    loss, gain_grad_h, gain_grad_e, gain_grad, grad_h, grad_e, grad_proj_h, grad_proj_e, grad_head = (
        pl.pallas_call(
            place_kernel,
            out_shape=[shape(value.shape, value.dtype) for value in values],
            in_specs=specs,
            out_specs=specs,
            scratch_shapes=[pltpu.VMEM(value.shape, value.dtype) for value in values[4:]]
            + [pltpu.SemaphoreType.DMA((20,)), pltpu.SemaphoreType.DMA((20,))],
            compiler_params=pltpu.CompilerParams(vmem_limit_bytes=60 * 2**20),
            name="place",
        )(*values)
    )
    return (
        loss[0, 0], grad_h.T, grad_e.T, gain_grad_h[0], gain_grad_e[0],
        grad_proj_h.T, grad_proj_e.T, gain_grad[0], grad_head,
    )


def solution(mesh):
    in_specs = (
        P("ctx", None), P("ctx", None), P(), P(), P("ctx", "vocab"), P("ctx", "vocab"),
        P("vocab"), P(("ctx", "vocab"), None), P(), P(),
    )
    out_specs = (
        P(), P("ctx", "vocab"), P("ctx", "vocab"), P("vocab"), P("vocab"),
        P("ctx", "vocab"), P("ctx", "vocab"), P("vocab"), P(("ctx", "vocab"), None),
    )
    return jax.shard_map(local, mesh=mesh, in_specs=in_specs, out_specs=out_specs, check_vma=False)
```
